256 devices in a mesh: tm: 8 (over y, core), rows: 32 (over x, z).
Axes of the slice: x: 4, y: 4, z: 8, core: 2. Of those that a mesh axis runs over, the one named last changes fastest.
Arguments:
- latent: bfloat16 [8, 96, 128, 384], P('tm', 'rows'), may hold values from -6 to 6
- norm1_gain: float32 [384], replicated, may hold values from 0.1 to 1.9
- conv1_weight: bfloat16 [3, 3, 3, 384, 384], replicated, may hold values from -0.0625 to 0.0625
- conv1_bias: float32 [384], replicated, may hold values from -3 to 3
- attention_gain: float32 [384], replicated, may hold values from 0.1 to 1.9
- qkv_weight: bfloat16 [384, 1152], replicated, may hold values from -1.5 to 1.5
- qkv_bias: float32 [1152], replicated, may hold values from -28 to 28
- proj_weight: bfloat16 [384, 384], replicated, may hold values from -0.3125 to 0.3125
- proj_bias: float32 [384], replicated, may hold values from -3 to 3
- up_weight: bfloat16 [3, 3, 384, 192], replicated, may hold values from -0.109375 to 0.109375
- up_bias: float32 [192], replicated, may hold values from -3 to 3
Outputs:
- upsampled: bfloat16 [8, 192, 256, 192], P('tm', 'rows')
The draws below stay inside these ranges and needn't reach their ends.
All inputs are finite; a program needn't handle non-finite values.
Results may differ from the reference program's by a relative error of at most 0.035.
Values may be sent and summed in bfloat16 or wider, within the bound.
No kernel may reach another device: no remote copies, remote signals or barrier semaphores. Data moves between devices by JAX's collectives and lax.ppermute only.
A program may use at most 128 MiB of HBM per device.

```python
import jax
import jax.numpy as jnp
from jax import lax

CH = 384
OUT_CH = 192
WIDTH = 128
HEIGHT = 96
FRAMES = 8


def draw_qkv_weight(key, part):
    key = jax.random.fold_in(key, 7)
    first, second, third = jax.random.split(key, 3)
    spread = CH ** (-0.5)
    query_w = jax.random.normal(first, (CH, CH), jnp.float32) * spread * 2.0
    key_w = jax.random.normal(second, (CH, CH), jnp.float32) * spread * 2.0
    values_w = jax.random.normal(third, (CH, CH), jnp.float32) * spread
    whole = jnp.concatenate([query_w, key_w, values_w], 1)
    return jnp.clip(whole, -1.5, 1.5).astype(jnp.bfloat16)


def draw_qkv_bias(key, part):
    key = jax.random.fold_in(key, 11)
    first = jax.random.fold_in(key, 0)
    base = jnp.clip(jax.random.normal(first, (3 * CH,), jnp.float32) * 0.5, -3.0, 3.0)
    return base


def shard_levels(key, dims, shards, least, top_value):
    def one(position, blocks):
        heights = jax.random.uniform(jax.random.fold_in(jax.random.fold_in(key, 6), position), (blocks,), jnp.float32, least / len(shards), top_value / len(shards))
        return jnp.repeat(jnp.exp(heights), dims[position] // blocks).reshape((-1,) + (1,) * (len(dims) - position - 1))

    factor_of = one(*shards[0])
    for cut in shards[1:]:
        factor_of = factor_of * one(*cut)
    return factor_of


def normal_values(stream_key, shape, deviation, reach, cuts=(), dtype=jnp.bfloat16):
    values = jax.random.normal(stream_key, shape, jnp.float32) * deviation
    if len(cuts) > 0:
        values = shard_levels(stream_key, shape, cuts, -0.22, 0.18) * values
    return jnp.clip(values, min=-reach, max=reach).astype(dtype)


def setup_inputs(seed: int = 0) -> dict:
    keys = jax.random.split(jax.random.key(seed), 12)
    latent = normal_values(keys[0], (FRAMES, HEIGHT, WIDTH, CH), 1.0, 6.0, ((0, 8), (1, 32)))
    norm1_gain = jnp.clip(1.0 + 0.18 * jax.random.normal(keys[1], (CH,), jnp.float32), 0.1, 1.9)
    conv1_weight = normal_values(keys[2], (3, 3, 3, CH, CH), (27 * CH) ** -0.5, 0.0625)
    conv1_bias = normal_values(keys[3], (CH,), 0.5, 3.0, (), jnp.float32)
    attention_gain = jnp.clip(1.0 + 0.18 * jax.random.normal(keys[4], (CH,), jnp.float32), 0.1, 1.9)
    qkv_weight = draw_qkv_weight(jax.random.fold_in(keys[11], 71), 0)
    qkv_bias = draw_qkv_bias(jax.random.fold_in(keys[11], 71), 0)
    proj_weight = normal_values(keys[7], (CH, CH), CH ** -0.5, 0.3125)
    proj_bias = normal_values(keys[8], (CH,), 0.5, 3.0, (), jnp.float32)
    up_weight = normal_values(keys[9], (3, 3, CH, OUT_CH), (9 * CH) ** -0.5, 0.109375)
    up_bias = normal_values(keys[10], (OUT_CH,), 0.5, 3.0, (), jnp.float32)
    return dict(latent=latent, norm1_gain=norm1_gain, conv1_weight=conv1_weight, conv1_bias=conv1_bias, attention_gain=attention_gain, qkv_weight=qkv_weight, qkv_bias=qkv_bias, proj_weight=proj_weight, proj_bias=proj_bias, up_weight=up_weight, up_bias=up_bias)


def root_norm(values_in, norm_gain):
    return values_in * lax.rsqrt(lax.optimization_barrier(jnp.mean(values_in * values_in, -1, keepdims=True)) + 1e-06) * norm_gain

def conv_taps(padded, weight):
    depth = weight.shape[0]
    frames = padded.shape[0] - depth + 1
    height = padded.shape[1] - 2
    width = padded.shape[2] - 2
    outputs = weight.shape[-1]
    total = jnp.zeros((frames * height * width, outputs), jnp.float32)
    for time_tap in range(depth):
        block = padded[time_tap:time_tap + frames]
        columns = jnp.concatenate([block[:, row_tap:row_tap + height, col_tap:col_tap + width, :] for row_tap in range(3) for col_tap in range(3)], -1)
        matrix = weight[time_tap].reshape(-1, outputs)
        total = total + jnp.dot(columns.reshape(frames * height * width, -1), matrix, preferred_element_type=jnp.float32)
    return total.reshape(frames, height, width, outputs)

def reference(latent, norm1_gain, conv1_weight, conv1_bias, attention_gain, qkv_weight, qkv_bias, proj_weight, proj_bias, up_weight, up_bias):
    latent_f = latent.astype(jnp.float32)
    act1 = jax.nn.silu(root_norm(latent_f, norm1_gain)).astype(jnp.bfloat16)
    padded_in = jnp.pad(act1, ((2, 0), (1, 1), (1, 1), (0, 0)))
    conv1 = (conv_taps(padded_in, conv1_weight) + conv1_bias).astype(jnp.bfloat16)
    block = (latent_f + conv1.astype(jnp.float32)).astype(jnp.bfloat16)
    frames, height, width, channels = block.shape
    normed = root_norm(block.astype(jnp.float32), attention_gain).astype(jnp.bfloat16)
    projected = jnp.dot(normed.reshape(-1, channels), qkv_weight, preferred_element_type=jnp.float32) + qkv_bias
    projected = projected.astype(jnp.bfloat16).reshape(frames, height * width, 3 * channels)
    scale = channels ** (-0.5)

    def one_frame(triple):
        queries = triple[:, :channels]
        keys_all = triple[:, channels:2 * channels]
        values_all = triple[:, 2 * channels:]
        scores = jnp.dot(queries, keys_all.T, preferred_element_type=jnp.float32) * scale
        top = lax.optimization_barrier(jnp.max(scores, -1, keepdims=True))
        expd = jnp.exp(scores - top)
        total = lax.optimization_barrier(jnp.sum(expd, -1, keepdims=True))
        weights = expd.astype(jnp.bfloat16)
        summed = jnp.dot(weights, values_all, preferred_element_type=jnp.float32)
        return (summed / total).astype(jnp.bfloat16)
    mixed = lax.map(one_frame, projected)
    attended = jnp.dot(mixed.reshape(-1, channels), proj_weight, preferred_element_type=jnp.float32) + proj_bias
    attended = (attended + block.reshape(-1, channels).astype(jnp.float32)).astype(jnp.bfloat16)
    attended = attended.reshape(frames, height, width, channels)
    enlarged = jnp.repeat(jnp.repeat(attended, 2, axis=1), 2, axis=2)
    padded = jnp.pad(enlarged, ((0, 0), (1, 1), (1, 1), (0, 0)))
    result = conv_taps(padded, up_weight[None]) + up_bias
    return result.astype(jnp.bfloat16)
```

```python
import functools
import math

import jax
import jax.numpy as jnp
from jax import lax
from jax.experimental import pallas as pl
from jax.experimental.pallas import tpu as pltpu
from jax.sharding import PartitionSpec as P

F32 = jnp.float32
BF16 = jnp.bfloat16
ROWS = 3
W = 128
C = 384
OUT = 192
CELLS = ROWS * W
XN, ZN, TN = 4, 8, 8
QALL = XN * CELLS
HALF = C // 2
STAT = 16
LOG2E = math.log2(math.e)


def dot(a, b, dims):
    return lax.dot_general(a, b, (dims, ((), ())), preferred_element_type=F32)


def params(mib=40):
    return pltpu.CompilerParams(vmem_limit_bytes=mib * 2**20)


def cost(flops, bytes_accessed):
    return pl.CostEstimate(flops=int(flops), bytes_accessed=int(bytes_accessed), transcendentals=0)


def whole(shape):
    zeros = (0,) * len(shape)
    return pl.BlockSpec(shape, lambda *_: zeros)


def col_variants(y, store):
    column = lax.broadcasted_iota(jnp.int32, y.shape, 0)
    before = jnp.where(column == 0, 0.0, pltpu.roll(y, 1, 0))
    after = jnp.where(column == W - 1, 0.0, pltpu.roll(y, W - 1, 0))
    store(0, before.astype(BF16))
    store(1, y.astype(BF16))
    store(2, after.astype(BF16))


def activate(row, gain):
    x = row.astype(F32)
    y = x * lax.rsqrt(jnp.mean(x * x, -1, keepdims=True) + 1e-6) * gain
    y = y / (1.0 + jnp.exp(-y))
    return y.astype(BF16).astype(F32)


def fill_rows(scratch, base, rows, gain):
    for index, row in enumerate(rows):
        y = activate(row, gain)

        def store(variant, value, index=index):
            scratch[base + index, :, variant * C : (variant + 1) * C] = value

        col_variants(y, store)


def conv_first(own, two, low, high, gain, weight, acc, scratch):
    step = pl.program_id(0)
    g = gain[...]

    @pl.when(step == 0)
    def _():
        fill_rows(scratch, 0, [low[0], own[0], own[1], own[2], high[0]], g)
        acc[...] = jnp.zeros_like(acc)

    @pl.when(step == 3)
    def _():
        fill_rows(scratch, 5, [low[1], two[0], two[1], two[2], high[1]], g)

    base = (step // 3) * 5 + step % 3
    left = scratch[pl.ds(base, ROWS)].reshape(CELLS, 3 * C)
    acc[...] += dot(left, weight[0, 0].reshape(3 * C, C), ((1,), (0,)))


def conv_last(one, own, gain, weight, start, bias, gain2, block, normed, scratch, acc):
    step = pl.program_id(0)

    @pl.when(step == 0)
    def _():
        fill_rows(scratch, 0, [one[i] for i in range(5)], gain[...])
        acc[...] = start[...]

    left = scratch[pl.ds(step, ROWS)].reshape(CELLS, 3 * C)
    acc[...] += dot(left, weight[0, 0].reshape(3 * C, C), ((1,), (0,)))

    @pl.when(step == 2)
    def _():
        conv = (acc[...] + bias[...]).astype(BF16).astype(F32)
        x = own[...].reshape(CELLS, C).astype(F32) + conv
        x = x.astype(BF16)
        block[...] = x
        x = x.astype(F32)
        x = x * lax.rsqrt(jnp.mean(x * x, -1, keepdims=True) + 1e-6) * gain2[...]
        normed[...] = x.astype(BF16)


def conv1(own, two, low, high, one, gain, weight, bias, gain2):
    row5 = (5, W, C)
    wblock = (1, 1, 3, C, C)
    acc = pl.pallas_call(
        conv_first,
        grid=(6,),
        in_specs=[
            whole((ROWS, W, C)),
            whole((ROWS, W, C)),
            whole((2, W, C)),
            whole((2, W, C)),
            whole((1, C)),
            pl.BlockSpec(wblock, lambda s: (2 - 2 * (s // 3), s % 3, 0, 0, 0)),
        ],
        out_specs=whole((CELLS, C)),
        out_shape=jax.ShapeDtypeStruct((CELLS, C), F32),
        scratch_shapes=[pltpu.VMEM((10, W, 3 * C), BF16)],
        compiler_params=params(),
        cost_estimate=cost(2 * CELLS * 18 * C * C, 6e6),
        name="conv_first",
    )(own, two, low, high, gain, weight)
    return pl.pallas_call(
        conv_last,
        grid=(3,),
        in_specs=[
            whole(row5),
            whole((ROWS, W, C)),
            whole((1, C)),
            pl.BlockSpec(wblock, lambda s: (1, s, 0, 0, 0)),
            whole((CELLS, C)),
            whole((1, C)),
            whole((1, C)),
        ],
        out_specs=[whole((CELLS, C)), whole((CELLS, C))],
        out_shape=[jax.ShapeDtypeStruct((CELLS, C), BF16)] * 2,
        scratch_shapes=[pltpu.VMEM((5, W, 3 * C), BF16), pltpu.VMEM((CELLS, C), F32)],
        compiler_params=params(),
        cost_estimate=cost(2 * CELLS * 9 * C * C, 4e6),
        name="conv_last",
    )(one, own, gain, weight, acc, bias, gain2)


def query_kernel(normed, wq, wk, bq, bk, out, shift):
    scale = C**-0.5 * LOG2E
    q = (dot(normed[...], wq[...], ((1,), (0,))) + bq[...]).astype(BF16)
    out[...] = (dot(wk[...], q, ((1,), (1,))) * scale).astype(BF16)
    bias = jnp.broadcast_to(bk[...], (8, C))
    shift[...] = dot(bias, q.astype(F32), ((1,), (1,)))[:1] * scale


def queries_of(normed, qkv_weight, qkv_bias):
    return pl.pallas_call(
        query_kernel,
        grid=(1,),
        in_specs=[
            whole((CELLS, C)),
            pl.BlockSpec((C, C), lambda i: (0, 0)),
            pl.BlockSpec((C, C), lambda i: (0, 1)),
            pl.BlockSpec((1, C), lambda i: (0, 0)),
            pl.BlockSpec((1, C), lambda i: (0, 1)),
        ],
        out_specs=[whole((C, CELLS)), whole((1, CELLS))],
        out_shape=[
            jax.ShapeDtypeStruct((C, CELLS), BF16),
            jax.ShapeDtypeStruct((1, CELLS), F32),
        ],
        compiler_params=params(),
        cost_estimate=cost(4 * CELLS * C * C, 1.5e6),
        name="queries",
    )(normed, qkv_weight, qkv_weight, qkv_bias, qkv_bias)


def softmax_step(keys, q, m_old, l_old, acc_old):
    s = [dot(k, q, ((1,), (0,))) for k in keys]
    m = functools.reduce(jnp.maximum, [jnp.max(x, 0, keepdims=True) for x in s])
    if m_old is not None:
        m = jnp.maximum(m, m_old)
    p = [jnp.exp2(x - m) for x in s]
    total = functools.reduce(jnp.add, [jnp.sum(x, 0, keepdims=True) for x in p])
    acc = functools.reduce(
        jnp.add, [dot(k, x.astype(BF16), ((0,), (0,))) for k, x in zip(keys, p)]
    )
    if m_old is not None:
        alpha = jnp.exp2(m_old - m)
        total = total + alpha * l_old
        acc = acc + alpha * acc_old
    return m, total, acc


def attention_kernel(count, first, *refs):
    keys = [r[...] for r in refs[:count]]
    q = refs[count][...]
    state = refs[count + 1 : -3]
    old = (None, None, None) if first else tuple(r[...] for r in state)
    for ref, value in zip(refs[-3:], softmax_step(keys, q, *old)):
        ref[...] = value


def attention_step(keys, queries, state, size, blocks):
    count = len(keys)
    rows = sum(k.shape[0] for k in keys)
    col = lambda i: (0, i)
    state_specs = [
        pl.BlockSpec((1, size), col),
        pl.BlockSpec((1, size), col),
        pl.BlockSpec((C, size), col),
    ]
    first = state is None
    n = size * blocks
    return pl.pallas_call(
        functools.partial(attention_kernel, count, first),
        grid=(blocks,),
        in_specs=[whole(k.shape) for k in keys]
        + [pl.BlockSpec((C, size), col)]
        + ([] if first else state_specs),
        out_specs=state_specs,
        out_shape=[
            jax.ShapeDtypeStruct((1, n), F32),
            jax.ShapeDtypeStruct((1, n), F32),
            jax.ShapeDtypeStruct((C, n), F32),
        ],
        compiler_params=params(),
        cost_estimate=cost(4 * rows * n * C, 6e6),
        name="attention_step",
    )(*keys, queries, *(() if first else state))


def split3(x):
    hi = x.astype(BF16)
    rest = x - hi.astype(F32)
    mid = rest.astype(BF16)
    low = (rest - mid.astype(F32)).astype(BF16)
    return hi, mid, low


def stat_rows(parts):
    n = parts[0].shape[1]
    row = lax.broadcasted_iota(jnp.int32, (STAT, n), 0)
    block = jnp.zeros((STAT, n), F32)
    for i, part in enumerate(parts):
        for j, piece in enumerate(split3(part)):
            block = jnp.where(row == 3 * i + j, piece.astype(F32), block)
    return block.astype(BF16)


def stat_of(block, i):
    b = block.astype(F32)
    return b[3 * i : 3 * i + 1] + b[3 * i + 1 : 3 * i + 2] + b[3 * i + 2 : 3 * i + 3]


def opposite_kernel(count, *refs):
    keys = [r[...] for r in refs[:count]]
    q, m_old, l_old, acc_old = (r[...] for r in refs[count : count + 4])
    top, bottom = refs[-2:]
    m, total, acc = softmax_step(keys, q, m_old, l_old, acc_old)
    out = (acc / total).astype(BF16)
    stats = stat_rows([m + jnp.log2(total)])
    top[:HALF] = out[:HALF]
    top[HALF:] = stats
    bottom[:HALF] = out[HALF:]
    bottom[HALF:] = stats


def opposite(keys, queries, state):
    count = len(keys)
    rows = sum(k.shape[0] for k in keys)
    col = lambda i: (0, XN - 1)
    return pl.pallas_call(
        functools.partial(opposite_kernel, count),
        grid=(1,),
        in_specs=[whole(k.shape) for k in keys]
        + [
            pl.BlockSpec((C, CELLS), col),
            pl.BlockSpec((1, CELLS), col),
            pl.BlockSpec((1, CELLS), col),
            pl.BlockSpec((C, CELLS), col),
        ],
        out_specs=[whole((HALF + STAT, CELLS))] * 2,
        out_shape=[jax.ShapeDtypeStruct((HALF + STAT, CELLS), BF16)] * 2,
        compiler_params=params(),
        cost_estimate=cost(4 * rows * CELLS * C, 2e6),
        name="opposite",
    )(*keys, queries, *state)


def merge(parts):
    top = functools.reduce(jnp.maximum, [s for s, _ in parts])
    w = [jnp.exp2(s - top) for s, _ in parts]
    total = functools.reduce(jnp.add, w)
    inverse = 1.0 / total
    out = functools.reduce(jnp.add, [(a * inverse) * o for a, (_, o) in zip(w, parts)])
    return top + jnp.log2(total), out


def relay_kernel(from_low, from_high, m, total, acc, to_low, to_high):
    for side, got, out in ((0, from_high, to_low), (1, from_low, to_high)):
        cols = slice(side * CELLS, (side + 1) * CELLS)
        stat = m[:, cols] + jnp.log2(total[:, cols])
        mine = acc[:, cols] / total[:, cols]
        theirs = (stat_of(got[HALF:], 0), got[:HALF].astype(F32))
        if side == 0:
            stat_t, half_t = stat, mine[:HALF]
            stat_b, half_b = merge([(stat, mine[HALF:]), theirs])
        else:
            stat_t, half_t = merge([(stat, mine[:HALF]), theirs])
            stat_b, half_b = stat, mine[HALF:]
        out[:HALF] = half_t.astype(BF16)
        out[HALF:C] = half_b.astype(BF16)
        out[C:] = stat_rows([stat_t, stat_b])


def relay(from_low, from_high, state):
    half = (HALF + STAT, CELLS)
    return pl.pallas_call(
        relay_kernel,
        grid=(1,),
        in_specs=[
            whole(half),
            whole(half),
            whole((1, 2 * CELLS)),
            whole((1, 2 * CELLS)),
            whole((C, 2 * CELLS)),
        ],
        out_specs=[whole((C + STAT, CELLS))] * 2,
        out_shape=[jax.ShapeDtypeStruct((C + STAT, CELLS), BF16)] * 2,
        compiler_params=params(),
        cost_estimate=cost(1e6, 4e6),
        name="relay",
    )(from_low, from_high, *state)


def finish_kernel(from_low, from_high, m, total, acc, shift, wv, bv, wp, bp, block, out):
    c = shift[...]
    stat = m[...] + jnp.log2(total[...]) + c
    mine = acc[...] / total[...]
    halves = []
    for i in range(2):
        rows = slice(i * HALF, (i + 1) * HALF)
        parts = [(stat, mine[rows])] + [
            (stat_of(got[C:], i) + c, got[rows].astype(F32)) for got in (from_low, from_high)
        ]
        halves.append(merge(parts)[1])
    mixed_in = jnp.concatenate(halves, 0).astype(BF16)
    mixed = (dot(mixed_in, wv[...], ((0,), (0,))) + bv[...]).astype(BF16)
    attended = dot(mixed, wp[...], ((1,), (0,))) + bp[...] + block[...].astype(F32)
    out[...] = attended.astype(BF16)


def finish(from_low, from_high, state, shift, qkv_weight, qkv_bias, proj_weight, proj_bias, block):
    pay = (C + STAT, CELLS)
    return pl.pallas_call(
        finish_kernel,
        grid=(1,),
        in_specs=[
            whole(pay),
            whole(pay),
            whole((1, CELLS)),
            whole((1, CELLS)),
            whole((C, CELLS)),
            whole((1, CELLS)),
            pl.BlockSpec((C, C), lambda i: (0, 2)),
            pl.BlockSpec((1, C), lambda i: (0, 2)),
            whole((C, C)),
            whole((1, C)),
            whole((CELLS, C)),
        ],
        out_specs=whole((CELLS, C)),
        out_shape=jax.ShapeDtypeStruct((CELLS, C), BF16),
        compiler_params=params(),
        cost_estimate=cost(4 * CELLS * C * C, 3e6),
        name="finish",
    )(from_low, from_high, *state, shift, qkv_weight, qkv_bias, proj_weight, proj_bias, block)


def up_phases(weight):
    w = weight.astype(F32)

    def pairs(v, axis):
        a, b, c = (lax.index_in_dim(v, i, axis, keepdims=False) for i in range(3))
        return jnp.stack([jnp.stack([a, b + c]), jnp.stack([a + b, c])])

    v = pairs(w, 0)
    v = pairs(v, 2)
    v = v.transpose(2, 0, 3, 1, 4, 5).reshape(2, 2, 2, 2 * C, OUT)
    return jnp.pad(v.astype(BF16), ((0, 0),) * 4 + ((0, 256 - OUT),))


def up_kernel(body, low, high, weight, bias, out, scratch, wide):
    for index, ref in enumerate((low, None, None, None, high)):
        row = body[index - 1] if ref is None else ref[0]

        def store(variant, value, index=index):
            scratch[index, :, variant * C : (variant + 1) * C] = value

        col_variants(row.astype(F32), store)
    for di in range(2):
        for dj in range(2):
            total = jnp.broadcast_to(bias[...], (CELLS, 256))
            for rt in range(2):
                left = scratch[di + rt : di + rt + ROWS, :, dj * C : (dj + 2) * C]
                total += dot(left.reshape(CELLS, 2 * C), weight[di, dj, rt], ((1,), (0,)))
            for i in range(ROWS):
                for part in range(2):
                    wide[part, 2 * i + di, pl.ds(dj, W, stride=2), :] = total[
                        i * W : (i + 1) * W, part * 128 : (part + 1) * 128
                    ]
    for row in range(2 * ROWS):
        out[row, :, :128] = wide[0, row].astype(BF16)
        out[row, :, 128:] = wide[1, row, :, : OUT - 128].astype(BF16)


def up_conv(body, low, high, weight, bias):
    return pl.pallas_call(
        up_kernel,
        grid=(1,),
        in_specs=[
            whole((ROWS, W, C)),
            whole((1, W, C)),
            whole((1, W, C)),
            whole((2, 2, 2, 2 * C, 256)),
            whole((1, 256)),
        ],
        out_specs=whole((2 * ROWS, 2 * W, OUT)),
        out_shape=jax.ShapeDtypeStruct((2 * ROWS, 2 * W, OUT), BF16),
        scratch_shapes=[
            pltpu.VMEM((5, W, 3 * C), BF16),
            pltpu.VMEM((2, 2 * ROWS, 2 * W, 128), F32),
        ],
        compiler_params=params(),
        cost_estimate=cost(2 * CELLS * 16 * C * OUT, 4e6),
        name="up_conv",
    )(body, low, high, weight, bias)


def permute_z(value, by):
    pairs = [(x * ZN + z, x * ZN + (z + by) % ZN) for x in range(XN) for z in range(ZN)]
    return lax.ppermute(value, "rows", pairs)


def permute_x(value, by):
    pairs = [(x * ZN + z, (x + by) % XN * ZN + z) for x in range(XN) for z in range(ZN)]
    return lax.ppermute(value, "rows", pairs)


def to_bands(value, by):
    n = XN * ZN
    return lax.ppermute(value, "rows", [(i, i + by) for i in range(n) if 0 <= i + by < n])


def on_device(
    latent,
    norm1_gain,
    conv1_weight,
    conv1_bias,
    attention_gain,
    qkv_weight,
    qkv_bias,
    proj_weight,
    proj_bias,
    up_weight,
    up_bias,
):
    own = latent[0]
    two = lax.ppermute(own, "tm", [(t, t + 2) for t in range(TN - 2)])
    low = to_bands(jnp.concatenate([own[2:], two[2:]], 0), 1)
    high = to_bands(jnp.concatenate([own[:1], two[:1]], 0), -1)
    even = lax.axis_index("tm") % 2 == 0
    mid = jnp.where(even, own, two)
    edge_low = jnp.where(even, low[:1], low[1:])
    edge_high = jnp.where(even, high[:1], high[1:])
    one = lax.ppermute(
        jnp.concatenate([edge_low, mid, edge_high], 0), "tm", [(t, t ^ 1) for t in range(TN)]
    )
    gain = norm1_gain[None]
    block, normed = conv1(
        own, two, low, high, one, gain, conv1_weight, conv1_bias[None], attention_gain[None]
    )

    up, down = permute_z(normed, 1), permute_z(normed, -1)
    qkv_b = qkv_bias[None]
    query, shift = queries_of(normed, qkv_weight, qkv_b)
    q_low, q_high = permute_x(query, 1), permute_x(query, -1)
    q_far = jnp.concatenate([permute_x(q_low[:HALF], 1), permute_x(q_high[HALF:], -1)], 0)
    queries = jnp.concatenate([q_low, q_high, query, q_far], 1)
    up2, down2 = permute_z(up, 1), permute_z(down, -1)
    state = attention_step([normed, up, down], queries, None, 512, 3)
    up3, down3 = permute_z(up2, 1), permute_z(down2, -1)
    state = attention_step([up2, down2], queries, state, 512, 3)
    up4, down4 = permute_z(up3[: CELLS // 2], 1), permute_z(down3[CELLS // 2 :], -1)
    state = attention_step([up3, down3], queries, state, 512, 3)
    last = [up4, down4]
    pay_t, pay_b = opposite(last, queries, state)
    half_low, half_high = permute_x(pay_t, 1), permute_x(pay_b, -1)
    state = attention_step(last, queries, state, CELLS, 3)
    to_low, to_high = relay(half_low, half_high, state)
    from_low, from_high = permute_x(to_high, 1), permute_x(to_low, -1)
    state = [v[:, 2 * CELLS :] for v in state]
    attended = finish(
        from_low,
        from_high,
        state,
        shift,
        qkv_weight,
        qkv_b,
        proj_weight,
        proj_bias[None],
        block,
    ).reshape(ROWS, W, C)
    edge_low, edge_high = to_bands(attended[2:], 1), to_bands(attended[:1], -1)
    bias = jnp.pad(up_bias, (0, 256 - OUT))[None]
    result = up_conv(attended, edge_low, edge_high, up_phases(up_weight), bias)
    return result[None]


def solution(mesh):
    return jax.shard_map(
        on_device,
        mesh=mesh,
        in_specs=(P("tm", "rows", None, None), P(), P(), P(), P(), P(), P(), P(), P(), P(), P()),
        out_specs=P("tm", "rows", None, None),
        check_vma=False,
    )
```

```python
import functools
import math

import jax
import jax.numpy as jnp
from jax import lax
from jax.experimental import pallas as pl
from jax.experimental.pallas import tpu as pltpu
from jax.sharding import PartitionSpec as P

F32 = jnp.float32
BF16 = jnp.bfloat16
ROWS = 3
W = 128
C = 384
OUT = 192
CELLS = ROWS * W
XN, ZN, TN = 4, 8, 8
QALL = XN * CELLS
HALF = C // 2
STAT = 16
LOG2E = math.log2(math.e)


def dot(a, b, dims):
    return lax.dot_general(a, b, (dims, ((), ())), preferred_element_type=F32)


def params(mib=32):
    return pltpu.CompilerParams(vmem_limit_bytes=mib * 2**20)


def cost(flops, bytes_accessed):
    return pl.CostEstimate(flops=int(flops), bytes_accessed=int(bytes_accessed), transcendentals=0)


VM = pl.BlockSpec(memory_space=pltpu.VMEM)
ANY = pl.BlockSpec(memory_space=pl.ANY)


def call(body, outs, *args, name, flops=1e6, nbytes=1e6, aliases=None, scratch=(), mib=32, unread=()):
    shapes = [jax.ShapeDtypeStruct(shape, dtype) for shape, dtype in outs]
    result = pl.pallas_call(
        body,
        in_specs=[ANY if i in unread else VM for i in range(len(args))],
        out_specs=[VM] * len(shapes),
        out_shape=shapes,
        input_output_aliases=aliases or {},
        scratch_shapes=list(scratch),
        compiler_params=params(mib),
        cost_estimate=cost(flops, nbytes),
        name=name,
    )(*args)
    return result[0] if len(shapes) == 1 else result


def col_variants(y, store):
    column = lax.broadcasted_iota(jnp.int32, y.shape, 0)
    before = jnp.where(column == 0, 0.0, pltpu.roll(y, 1, 0))
    after = jnp.where(column == W - 1, 0.0, pltpu.roll(y, W - 1, 0))
    store(0, before.astype(BF16))
    store(1, y.astype(BF16))
    store(2, after.astype(BF16))


def activate(row, gain):
    x = row.astype(F32)
    y = x * lax.rsqrt(jnp.mean(x * x, -1, keepdims=True) + 1e-6) * gain
    y = y / (1.0 + jnp.exp(-y))
    return y.astype(BF16).astype(F32)


def fill_rows(scratch, rows, gain):
    for index, row in enumerate(rows):
        y = activate(row, gain)

        def store(variant, value, index=index):
            scratch[index, :, variant * C : (variant + 1) * C] = value

        col_variants(y, store)


def interior(scratch, weight, time_tap):
    whole_band = scratch[...].reshape(CELLS, 3 * C)

    def tap(b):
        return weight[time_tap, b].reshape(3 * C, C)

    total = dot(whole_band, tap(1), ((1,), (0,)))
    shift_down = dot(whole_band[: 2 * W], tap(0), ((1,), (0,)))
    shift_up = dot(whole_band[W:], tap(2), ((1,), (0,)))
    top = total[:W] + shift_up[:W]
    middle = total[W : 2 * W] + shift_down[:W] + shift_up[W:]
    bottom = total[2 * W :] + shift_down[W:]
    return top, middle, bottom


def conv_own_kernel(own, gain, weight, acc, scratch):
    fill_rows(scratch, [own[i] for i in range(ROWS)], gain[...])
    for i, part in enumerate(interior(scratch, weight, 2)):
        acc[i * W : (i + 1) * W] = part


def conv_two_kernel(two, gain, weight, start, acc, scratch):
    fill_rows(scratch, [two[i] for i in range(ROWS)], gain[...])
    for i, part in enumerate(interior(scratch, weight, 0)):
        acc[i * W : (i + 1) * W] = start[i * W : (i + 1) * W] + part


def conv_edges_kernel(low, high, gain, weight, start, acc, scratch):
    fill_rows(scratch, [low[0], low[1], high[0], high[1]], gain[...])
    top = start[:W]
    bottom = start[2 * W :]
    for i, time_tap in ((0, 2), (1, 0)):
        top += dot(scratch[i], weight[time_tap, 0].reshape(3 * C, C), ((1,), (0,)))
        bottom += dot(scratch[2 + i], weight[time_tap, 2].reshape(3 * C, C), ((1,), (0,)))
    acc[:W] = top
    acc[W : 2 * W] = start[W : 2 * W]
    acc[2 * W :] = bottom


def conv_last_kernel(one, own, gain, weight, start, bias, gain2, block, normed, scratch):
    fill_rows(scratch, [one[i] for i in range(5)], gain[...])
    total = start[...] + bias[...]
    for b in range(3):
        left = scratch[b : b + ROWS].reshape(CELLS, 3 * C)
        total += dot(left, weight[1, b].reshape(3 * C, C), ((1,), (0,)))
    conv = total.astype(BF16).astype(F32)
    x = (own[...].reshape(CELLS, C).astype(F32) + conv).astype(BF16)
    block[...] = x
    x = x.astype(F32)
    x = x * lax.rsqrt(jnp.mean(x * x, -1, keepdims=True) + 1e-6) * gain2[...]
    normed[...] = x.astype(BF16)


def edge_payload_kernel(own, two, _acc, _phases, to_next, to_previous):
    to_next[0] = own[ROWS - 1]
    to_next[1] = two[ROWS - 1]
    to_previous[0] = own[0]
    to_previous[1] = two[0]


def pair_payload_kernel(odd, own, two, low, high, _acc, out):
    def write(frame, index):
        out[0] = low[index]
        out[1 : 1 + ROWS] = frame[...]
        out[1 + ROWS] = high[index]

    @pl.when(odd[0] == 0)
    def _():
        write(own, 0)

    @pl.when(odd[0] == 1)
    def _():
        write(two, 1)


def pair_payload(odd, *args):
    return pl.pallas_call(
        pair_payload_kernel,
        in_specs=[pl.BlockSpec(memory_space=pltpu.SMEM)] + [VM] * 4 + [ANY],
        out_specs=VM,
        out_shape=jax.ShapeDtypeStruct((5, W, C), BF16),
        compiler_params=params(),
        cost_estimate=cost(1e6, 1e6),
        name="pair_payload",
    )(odd, *args)


def query_kernel(normed, weight, bias, out, shift):
    scale = C**-0.5 * LOG2E
    wq, wk = weight[:, :C], weight[:, C : 2 * C]
    q = (dot(normed[...], wq, ((1,), (0,))) + bias[:, :C]).astype(BF16)
    out[...] = (dot(wk, q, ((1,), (1,))) * scale).astype(BF16)
    bk = jnp.broadcast_to(bias[:, C : 2 * C], (8, C))
    shift[...] = dot(bk, q.astype(F32), ((1,), (1,)))[:1] * scale


def softmax_step(keys, q, m_old, l_old, acc_old):
    s = dot(keys, q, ((1,), (0,)))
    m = jnp.max(s, 0, keepdims=True)
    if m_old is not None:
        m = jnp.maximum(m, m_old)
    p = jnp.exp2(s - m)
    total = jnp.sum(p, 0, keepdims=True)
    acc = dot(keys, p.astype(BF16), ((0,), (0,)))
    if m_old is not None:
        alpha = jnp.exp2(m_old - m)
        total = total + alpha * l_old
        acc = acc + alpha * acc_old
    return m, total, acc


def joined(refs):
    return refs[0][...] if len(refs) == 1 else jnp.concatenate([r[...] for r in refs], 0)


def attention_kernel(count, first, start, size, *refs):
    keys = joined(refs[:count])
    q = refs[count]
    state = refs[count + 1 : -3]
    for at in range(0, refs[-1].shape[1], size):
        here, there = slice(start + at, start + at + size), slice(at, at + size)
        old = (None, None, None) if first else tuple(r[:, here] for r in state)
        for ref, value in zip(refs[-3:], softmax_step(keys, q[:, here], *old)):
            ref[:, there] = value


def attention_step(keys, queries, state, size=512, start=0, n=QALL):
    count = len(keys)
    rows = sum(k.shape[0] for k in keys)
    first = state is None
    in_place = not first and n == QALL
    return call(
        functools.partial(attention_kernel, count, first, start, size),
        [((1, n), F32), ((1, n), F32), ((C, n), F32)],
        *keys,
        queries,
        *(() if first else state),
        name="attention_step",
        flops=4 * rows * n * C,
        nbytes=6e6,
        aliases={count + 1 + i: i for i in range(3)} if in_place else None,
    )


def split3(x):
    hi = x.astype(BF16)
    rest = x - hi.astype(F32)
    mid = rest.astype(BF16)
    low = (rest - mid.astype(F32)).astype(BF16)
    return hi, mid, low


def stat_rows(parts):
    n = parts[0].shape[1]
    row = lax.broadcasted_iota(jnp.int32, (STAT, n), 0)
    block = jnp.zeros((STAT, n), F32)
    for i, part in enumerate(parts):
        for j, piece in enumerate(split3(part)):
            block = jnp.where(row == 3 * i + j, piece.astype(F32), block)
    return block.astype(BF16)


def stat_of(block, i):
    b = block.astype(F32)
    return b[3 * i : 3 * i + 1] + b[3 * i + 1 : 3 * i + 2] + b[3 * i + 2 : 3 * i + 3]


def opposite_kernel(count, *refs):
    keys = joined(refs[:count])
    cols = slice(3 * CELLS, 4 * CELLS)
    q, m_old, l_old, acc_old = (r[:, cols] for r in refs[count : count + 4])
    top, bottom = refs[-2:]
    m, total, acc = softmax_step(keys, q, m_old, l_old, acc_old)
    out = (acc / total).astype(BF16)
    stats = stat_rows([m + jnp.log2(total)])
    top[:HALF] = out[:HALF]
    top[HALF:] = stats
    bottom[:HALF] = out[HALF:]
    bottom[HALF:] = stats


def opposite(keys, queries, state):
    rows = sum(k.shape[0] for k in keys)
    return call(
        functools.partial(opposite_kernel, len(keys)),
        [((HALF + STAT, CELLS), BF16)] * 2,
        *keys,
        queries,
        *state,
        name="opposite",
        flops=4 * rows * CELLS * C,
        nbytes=2e6,
    )


def merge(parts):
    top = functools.reduce(jnp.maximum, [s for s, _ in parts])
    w = [jnp.exp2(s - top) for s, _ in parts]
    total = functools.reduce(jnp.add, w)
    inverse = 1.0 / total
    out = functools.reduce(jnp.add, [(a * inverse) * o for a, (_, o) in zip(w, parts)])
    return top + jnp.log2(total), out


def relay_kernel(from_low, from_high, m, total, acc, to_low, to_high):
    for side, got, out in ((0, from_high, to_low), (1, from_low, to_high)):
        cols = slice(side * CELLS, (side + 1) * CELLS)
        stat = m[:, cols] + jnp.log2(total[:, cols])
        mine = acc[:, cols] / total[:, cols]
        theirs = (stat_of(got[HALF:], 0), got[:HALF].astype(F32))
        if side == 0:
            stat_t, half_t = stat, mine[:HALF]
            stat_b, half_b = merge([(stat, mine[HALF:]), theirs])
        else:
            stat_t, half_t = merge([(stat, mine[:HALF]), theirs])
            stat_b, half_b = stat, mine[HALF:]
        out[:HALF] = half_t.astype(BF16)
        out[HALF:C] = half_b.astype(BF16)
        out[C:] = stat_rows([stat_t, stat_b])


def finish_kernel(from_low, from_high, m, total, acc, shift, weight, bias, wp, bp, block, out):
    c = shift[...]
    stat = m[...] + jnp.log2(total[...]) + c
    mine = acc[...] / total[...]
    halves = []
    for i in range(2):
        rows = slice(i * HALF, (i + 1) * HALF)
        parts = [(stat, mine[rows])] + [
            (stat_of(got[C:], i) + c, got[rows].astype(F32)) for got in (from_low, from_high)
        ]
        halves.append(merge(parts)[1])
    mixed_in = jnp.concatenate(halves, 0).astype(BF16)
    mixed = (dot(mixed_in, weight[:, 2 * C :], ((0,), (0,))) + bias[:, 2 * C :]).astype(BF16)
    attended = dot(mixed, wp[...], ((1,), (0,))) + bp[...] + block[...].astype(F32)
    out[...] = attended.astype(BF16)


def up_phases_kernel(weight, out):
    w = [[weight[b, c].astype(F32) for c in range(3)] for b in range(3)]

    def pairs(a, b, c):
        return ((a, b + c), (a + b, c))

    by_row = [pairs(*(w[b][c] for b in range(3))) for c in range(3)]
    for di in range(2):
        for rt in range(2):
            by_column = pairs(*(by_row[c][di][rt] for c in range(3)))
            for dj in range(2):
                for ct in range(2):
                    value = jnp.concatenate(
                        [by_column[dj][ct], jnp.zeros((256 - OUT, C), F32)], 0
                    )
                    out[di, dj, rt, ct * C : (ct + 1) * C] = value.T.astype(BF16)


def up_kernel(body, low, high, weight, bias, out, scratch, wide):
    for index, ref in enumerate((low, None, None, None, high)):
        row = body[index - 1] if ref is None else ref[0]

        def store(variant, value, index=index):
            scratch[index, :, variant * C : (variant + 1) * C] = value

        col_variants(row.astype(F32), store)
    b = jnp.concatenate([bias[...], jnp.zeros((1, 256 - OUT), F32)], 1)
    for di in range(2):
        for dj in range(2):
            total = jnp.broadcast_to(b, (CELLS, 256))
            for rt in range(2):
                left = scratch[di + rt : di + rt + ROWS, :, dj * C : (dj + 2) * C]
                part = dot(left.reshape(CELLS, 2 * C), weight[di, dj, rt], ((1,), (0,)))
                total += part
            for i in range(ROWS):
                for part in range(2):
                    wide[part, 2 * i + di, pl.ds(dj, W, stride=2), :] = total[
                        i * W : (i + 1) * W, part * 128 : (part + 1) * 128
                    ]
    for row in range(2 * ROWS):
        out[row, :128] = wide[0, row].T.astype(BF16)
        out[row, 128:] = wide[1, row].T[: OUT - 128].astype(BF16)


def up_conv(body, low, high, weight, bias):
    return call(
        up_kernel,
        [((2 * ROWS, OUT, 2 * W), BF16)],
        body,
        low,
        high,
        weight,
        bias,
        name="up_conv",
        flops=2 * CELLS * 16 * C * OUT,
        nbytes=4e6,
        scratch=[
            pltpu.VMEM((5, W, 3 * C), BF16),
            pltpu.VMEM((2, 2 * ROWS, 2 * W, 128), F32),
        ],
    )


def permute_z(value, by):
    pairs = [(x * ZN + z, x * ZN + (z + by) % ZN) for x in range(XN) for z in range(ZN)]
    return lax.ppermute(value, "rows", pairs)


def permute_x(value, by):
    pairs = [(x * ZN + z, (x + by) % XN * ZN + z) for x in range(XN) for z in range(ZN)]
    return lax.ppermute(value, "rows", pairs)


def to_bands(value, by):
    n = XN * ZN
    return lax.ppermute(value, "rows", [(i, i + by) for i in range(n) if 0 <= i + by < n])


def on_device(
    latent,
    norm1_gain,
    conv1_weight,
    conv1_bias,
    attention_gain,
    qkv_weight,
    qkv_bias,
    proj_weight,
    proj_bias,
    up_weight,
    up_bias,
):
    own = latent[0]
    gain = norm1_gain[None]
    qkv_b = qkv_bias[None]
    two = lax.ppermute(own, "tm", [(t, t + 2) for t in range(TN - 2)])
    phases = call(
        up_phases_kernel,
        [((2, 2, 2, 2 * C, 256), BF16)],
        up_weight.transpose(0, 1, 3, 2),
        name="up_phases",
        flops=1e7,
        nbytes=4e6,
    )
    band = pltpu.VMEM((ROWS, W, 3 * C), BF16)
    flops = 2 * CELLS * 9 * C * C
    acc = call(
        conv_own_kernel,
        [((CELLS, C), F32)],
        own,
        gain,
        conv1_weight,
        name="conv_own",
        flops=flops,
        scratch=[band],
    )
    to_next, to_previous = call(
        edge_payload_kernel,
        [((2, W, C), BF16)] * 2,
        own,
        two,
        acc,
        phases,
        name="edge_payload",
        unread=(2, 3),
    )
    low, high = to_bands(to_next, 1), to_bands(to_previous, -1)
    acc = call(
        conv_two_kernel,
        [((CELLS, C), F32)],
        two,
        gain,
        conv1_weight,
        acc,
        name="conv_two",
        flops=flops,
        scratch=[band],
    )
    odd = (lax.axis_index("tm") % 2).astype(jnp.int32).reshape(1)
    one = lax.ppermute(
        pair_payload(odd, own, two, low, high, acc), "tm", [(t, t ^ 1) for t in range(TN)]
    )
    acc = call(
        conv_edges_kernel,
        [((CELLS, C), F32)],
        low,
        high,
        gain,
        conv1_weight,
        acc,
        name="conv_edges",
        flops=flops / 4,
        scratch=[pltpu.VMEM((4, W, 3 * C), BF16)],
    )
    block, normed = call(
        conv_last_kernel,
        [((CELLS, C), BF16)] * 2,
        one,
        own,
        gain,
        conv1_weight,
        acc,
        conv1_bias[None],
        attention_gain[None],
        name="conv_last",
        flops=flops,
        scratch=[pltpu.VMEM((5, W, 3 * C), BF16)],
    )

    up, down = permute_z(normed, 1), permute_z(normed, -1)
    query, shift = call(
        query_kernel,
        [((C, CELLS), BF16), ((1, CELLS), F32)],
        normed,
        qkv_weight,
        qkv_b,
        name="queries",
        flops=4 * CELLS * C * C,
    )
    q_low, q_high = permute_x(query, 1), permute_x(query, -1)
    q_far = jnp.concatenate([permute_x(q_low[:HALF], 1), permute_x(q_high[HALF:], -1)], 0)
    queries = jnp.concatenate([q_low, q_high, query, q_far], 1)
    up2, down2 = permute_z(up, 1), permute_z(down, -1)
    state = attention_step([normed, up, down], queries, None)
    up3, down3 = permute_z(up2, 1), permute_z(down2, -1)
    state = attention_step([up2, down2], queries, state)
    up4, down4 = permute_z(up3[: CELLS // 2], 1), permute_z(down3[CELLS // 2 :], -1)
    state = attention_step([up3, down3], queries, state)
    last = [up4, down4]
    pay_t, pay_b = opposite(last, queries, state)
    half_low, half_high = permute_x(pay_t, 1), permute_x(pay_b, -1)
    sides = attention_step(last, queries, state, CELLS, 0, 2 * CELLS)
    to_low, to_high = call(
        relay_kernel,
        [((C + STAT, CELLS), BF16)] * 2,
        half_low,
        half_high,
        *sides,
        name="relay",
    )
    from_low, from_high = permute_x(to_high, 1), permute_x(to_low, -1)
    mine = attention_step(last, queries, state, CELLS, 2 * CELLS, CELLS)
    attended = call(
        finish_kernel,
        [((CELLS, C), BF16)],
        from_low,
        from_high,
        *mine,
        shift,
        qkv_weight,
        qkv_b,
        proj_weight,
        proj_bias[None],
        block,
        name="finish",
        flops=4 * CELLS * C * C,
    ).reshape(ROWS, W, C)
    edge_low, edge_high = to_bands(attended[2:], 1), to_bands(attended[:1], -1)
    result = up_conv(attended, edge_low, edge_high, phases, up_bias[None])
    return result.transpose(0, 2, 1)[None]


def solution(mesh):
    return jax.shard_map(
        on_device,
        mesh=mesh,
        in_specs=(P("tm", "rows", None, None), P(), P(), P(), P(), P(), P(), P(), P(), P(), P()),
        out_specs=P("tm", "rows", None, None),
        check_vma=False,
    )
```

```python
import functools
import math

import jax
import jax.numpy as jnp
from jax import lax
from jax.experimental import pallas as pl
from jax.experimental.pallas import tpu as pltpu
from jax.sharding import PartitionSpec as P

F32 = jnp.float32
BF16 = jnp.bfloat16
ROWS = 3
W = 128
C = 384
OUT = 192
CELLS = ROWS * W
XN, ZN, TN = 4, 8, 8
QALL = XN * CELLS
HALF = C // 2
STAT = 16
LOG2E = math.log2(math.e)


def dot(a, b, dims):
    return lax.dot_general(a, b, (dims, ((), ())), preferred_element_type=F32)


def params(mib=32):
    return pltpu.CompilerParams(vmem_limit_bytes=mib * 2**20)


def cost(flops, bytes_accessed):
    return pl.CostEstimate(flops=int(flops), bytes_accessed=int(bytes_accessed), transcendentals=0)


VM = pl.BlockSpec(memory_space=pltpu.VMEM)
ANY = pl.BlockSpec(memory_space=pl.ANY)


def call(body, outs, *args, name, flops=1e6, nbytes=1e6, aliases=None, scratch=(), mib=32, specs=None, out_spec=VM):
    shapes = [jax.ShapeDtypeStruct(shape, dtype) for shape, dtype in outs]
    result = pl.pallas_call(
        body,
        in_specs=specs or [VM] * len(args),
        out_specs=[out_spec] * len(shapes),
        out_shape=shapes,
        input_output_aliases=aliases or {},
        scratch_shapes=list(scratch),
        compiler_params=params(mib),
        cost_estimate=cost(flops, nbytes),
        name=name,
    )(*args)
    return result[0] if len(shapes) == 1 else result


def col_variants(y, store):
    column = lax.broadcasted_iota(jnp.int32, y.shape, 0)
    before = jnp.where(column == 0, 0.0, pltpu.roll(y, 1, 0))
    after = jnp.where(column == W - 1, 0.0, pltpu.roll(y, W - 1, 0))
    store(0, before.astype(BF16))
    store(1, y.astype(BF16))
    store(2, after.astype(BF16))


def activate(row, gain):
    x = row.astype(F32)
    y = x * lax.rsqrt(jnp.mean(x * x, -1, keepdims=True) + 1e-6) * gain
    y = y / (1.0 + jnp.exp(-y))
    return y.astype(BF16).astype(F32)


def fill_rows(scratch, rows, gain):
    for index, row in enumerate(rows):
        y = activate(row, gain)

        def store(variant, value, index=index):
            scratch[index, :, variant * C : (variant + 1) * C] = value

        col_variants(y, store)


def interior(scratch, weight):
    whole_band = scratch[...].reshape(CELLS, 3 * C)

    def tap(b):
        return weight[0, b].reshape(3 * C, C)

    total = dot(whole_band, tap(1), ((1,), (0,)))
    shift_down = dot(whole_band[: 2 * W], tap(0), ((1,), (0,)))
    shift_up = dot(whole_band[W:], tap(2), ((1,), (0,)))
    top = total[:W] + shift_up[:W]
    middle = total[W : 2 * W] + shift_down[:W] + shift_up[W:]
    bottom = total[2 * W :] + shift_down[W:]
    return top, middle, bottom


def conv_band_kernel(first, frame, small, weight, *refs):
    start = None if first else refs[0]
    acc, scratch = refs[-2:]
    fill_rows(scratch, [frame[i] for i in range(ROWS)], small[0:1, :C])
    for i, part in enumerate(interior(scratch, weight)):
        rows = slice(i * W, (i + 1) * W)
        acc[rows] = part if first else start[rows] + part


def conv_band(frame, small, weight, start=None):
    first = start is None
    return call(
        functools.partial(conv_band_kernel, first),
        [((CELLS, C), F32)],
        frame,
        small,
        weight,
        *(() if first else (start,)),
        name="conv_band",
        flops=2 * CELLS * 9 * C * C,
        scratch=[pltpu.VMEM((ROWS, W, 3 * C), BF16)],
        aliases=None if first else {3: 0},
    )


def edge_taps(scratch, low, high, weight):
    left = dot(scratch[low], weight[0, 0].reshape(3 * C, C), ((1,), (0,)))
    right = dot(scratch[high], weight[0, 2].reshape(3 * C, C), ((1,), (0,)))
    return left, right


def conv_edges_kernel(low, high, small, w_own, w_two, start, acc, scratch):
    fill_rows(scratch, [low[0], low[1], high[0], high[1]], small[0:1, :C])
    own = edge_taps(scratch, 0, 2, w_own)
    two = edge_taps(scratch, 1, 3, w_two)
    acc[...] = start[...]
    acc[:W] += own[0] + two[0]
    acc[2 * W :] += own[1] + two[1]


def conv_last_kernel(edges, own, small, weight, start, block, normed, scratch):
    fill_rows(scratch, [edges[0], edges[1]], small[0:1, :C])
    sides = edge_taps(scratch, 0, 1, weight)
    bias, gain2 = small[1:2, :C], small[2:3, :C]
    for i in range(ROWS):
        rows = slice(i * W, (i + 1) * W)
        total = start[rows] + bias
        if i != 1:
            total += sides[i // 2]
        x = (own[i].astype(F32) + total.astype(BF16).astype(F32)).astype(BF16)
        block[rows] = x
        x = x.astype(F32)
        x = x * lax.rsqrt(jnp.mean(x * x, -1, keepdims=True) + 1e-6) * gain2
        normed[rows] = x.astype(BF16)


SMEM = pl.BlockSpec(memory_space=pltpu.SMEM)


def edge_payload_kernel(odd, own, two, _acc, _phases, to_next, to_previous, pair):
    to_next[0] = own[ROWS - 1]
    to_next[1] = two[ROWS - 1]
    to_previous[0] = own[0]
    to_previous[1] = two[0]

    @pl.when(odd[0] == 0)
    def _():
        pair[...] = own[...]

    @pl.when(odd[0] == 1)
    def _():
        pair[...] = two[...]


def pair_edges_kernel(odd, low, high, _acc, out):
    index = odd[0]
    out[0] = low[index]
    out[1] = high[index]


def query_kernel(normed, weight, small, out, shift):
    scale = C**-0.5 * LOG2E
    wq, wk = weight[:, :C], weight[:, C : 2 * C]
    q = (dot(normed[...], wq, ((1,), (0,))) + small[4:5, :C]).astype(BF16)
    out[...] = (dot(wk, q, ((1,), (1,))) * scale).astype(BF16)
    bk = jnp.broadcast_to(small[4:5, C : 2 * C], (8, C))
    shift[...] = dot(bk, q.astype(F32), ((1,), (1,)))[:1] * scale


def spans(refs, low, high):
    at = 0
    for ref in refs:
        n = ref.shape[1]
        first, last = max(low, at), min(high, at + n)
        if first < last:
            yield ref, first - at, last - at, first - low, last - low
        at += n


def read(refs, low, high):
    pieces = [ref[:, a:b] for ref, a, b, _, _ in spans(refs, low, high)]
    return pieces[0] if len(pieces) == 1 else jnp.concatenate(pieces, 1)


def write(refs, low, high, value):
    for ref, a, b, first, last in spans(refs, low, high):
        ref[:, a:b] = value[:, first:last]


def joined(refs):
    return refs[0][...] if len(refs) == 1 else jnp.concatenate([r[...] for r in refs], 0)


def softmax_tiles(keys, tiles, q_of, old_of, give):
    keys_t = keys.T

    def scores(tile):
        return dot(keys, q_of(*tile), ((1,), (0,)))

    following = scores(tiles[0])
    for i, tile in enumerate(tiles):
        s = following
        if i + 1 < len(tiles):
            following = scores(tiles[i + 1])
        old = old_of(*tile)
        m = jnp.max(s, 0, keepdims=True)
        if old is not None:
            m = jnp.maximum(m, old[0])
        p = jnp.exp2(s - m)
        total = jnp.sum(p, 0, keepdims=True)
        acc = dot(keys_t, p.astype(BF16), ((1,), (0,)))
        if old is not None:
            alpha = jnp.exp2(old[0] - m)
            total = total + alpha * old[1]
            acc = acc + alpha * old[2]
        give(*tile, (m, total, acc))


def tiles_of(low, high, size=512):
    return [(at, min(at + size, high)) for at in range(low, high, size)]


def attention_kernel(n_keys, n_q, n_state, n_out, low, high, *refs):
    keys = joined(refs[:n_keys])
    queries = refs[n_keys : n_keys + n_q]
    state = refs[n_keys + n_q : n_keys + n_q + 3 * n_state]
    outs = refs[n_keys + n_q + 3 * n_state :]

    def old_of(a, b):
        return [read(state[i::3], a, b) for i in range(3)] if n_state else None

    def give(a, b, values):
        for i, value in enumerate(values):
            write(outs[i::3], a - low, b - low, value)

    softmax_tiles(keys, tiles_of(low, high), lambda a, b: read(queries, a, b), old_of, give)


def attention_step(keys, queries, state=(), low=0, high=None):
    widths = [q.shape[1] for q in queries]
    high = sum(widths) if high is None else high
    rows = sum(k.shape[0] for k in keys)
    whole_state = bool(state) and high - low == sum(s[0].shape[1] for s in state)
    outs = [s[0].shape[1] for s in state] if whole_state else [high - low]
    flat = [v for s in state for v in s]
    before = len(keys) + len(queries)
    result = call(
        functools.partial(
            attention_kernel, len(keys), len(queries), len(state), len(outs), low, high
        ),
        [shape for n in outs for shape in (((1, n), F32), ((1, n), F32), ((C, n), F32))],
        *keys,
        *queries,
        *flat,
        name="attention_step",
        flops=4 * rows * (high - low) * C,
        nbytes=6e6,
        aliases={before + i: i for i in range(len(flat))} if whole_state else None,
    )
    return [tuple(result[i : i + 3]) for i in range(0, len(result), 3)]


def gate_kernel(*refs):
    pass


def after(values, done):
    count = len(values)
    return call(
        gate_kernel,
        [(v.shape, v.dtype) for v in values],
        *values,
        done,
        name="gate",
        flops=1,
        nbytes=1,
        specs=[ANY] * (count + 1),
        out_spec=ANY,
        aliases={i: i for i in range(count)},
    )


def split3(x):
    hi = x.astype(BF16)
    rest = x - hi.astype(F32)
    mid = rest.astype(BF16)
    low = (rest - mid.astype(F32)).astype(BF16)
    return hi, mid, low


def stat_rows(parts):
    n = parts[0].shape[1]
    row = lax.broadcasted_iota(jnp.int32, (STAT, n), 0)
    block = jnp.zeros((STAT, n), F32)
    for i, part in enumerate(parts):
        for j, piece in enumerate(split3(part)):
            block = jnp.where(row == 3 * i + j, piece.astype(F32), block)
    return block.astype(BF16)


def stat_of(block, i):
    b = block.astype(F32)
    return b[3 * i : 3 * i + 1] + b[3 * i + 1 : 3 * i + 2] + b[3 * i + 2 : 3 * i + 3]


def opposite_kernel(n_keys, *refs):
    q, m_old, l_old, acc_old, top, bottom = refs[n_keys:]

    def give(_a, _b, values):
        m, total, acc = values
        out = (acc / total).astype(BF16)
        stats = stat_rows([m + jnp.log2(total)])
        top[:HALF] = out[:HALF]
        top[HALF:] = stats
        bottom[:HALF] = out[HALF:]
        bottom[HALF:] = stats

    old = lambda a, b: (m_old[...], l_old[...], acc_old[...])
    softmax_tiles(joined(refs[:n_keys]), [(0, CELLS)], lambda a, b: q[...], old, give)


def opposite(keys, q_far, state):
    rows = sum(k.shape[0] for k in keys)
    return call(
        functools.partial(opposite_kernel, len(keys)),
        [((HALF + STAT, CELLS), BF16)] * 2,
        *keys,
        q_far,
        *state,
        name="opposite",
        flops=4 * rows * CELLS * C,
        nbytes=2e6,
    )


def merge(parts):
    top = functools.reduce(jnp.maximum, [s for s, _ in parts])
    w = [jnp.exp2(s - top) for s, _ in parts]
    total = functools.reduce(jnp.add, w)
    inverse = 1.0 / total
    out = functools.reduce(jnp.add, [(a * inverse) * o for a, (_, o) in zip(w, parts)])
    return top + jnp.log2(total), out


def relay_kernel(from_low, from_high, m, total, acc, to_low, to_high):
    for side, got, out in ((0, from_high, to_low), (1, from_low, to_high)):
        cols = slice(side * CELLS, (side + 1) * CELLS)
        stat = m[:, cols] + jnp.log2(total[:, cols])
        mine = acc[:, cols] / total[:, cols]
        theirs = (stat_of(got[HALF:], 0), got[:HALF].astype(F32))
        if side == 0:
            stat_t, half_t = stat, mine[:HALF]
            stat_b, half_b = merge([(stat, mine[HALF:]), theirs])
        else:
            stat_t, half_t = merge([(stat, mine[:HALF]), theirs])
            stat_b, half_b = stat, mine[HALF:]
        out[:HALF] = half_t.astype(BF16)
        out[HALF:C] = half_b.astype(BF16)
        out[C:] = stat_rows([stat_t, stat_b])


def finish_kernel(from_low, from_high, m, total, acc, shift, weight, wp, small, block, out):
    c = shift[...]
    stat = m[...] + jnp.log2(total[...]) + c
    mine = acc[...] / total[...]
    halves = []
    for i in range(2):
        rows = slice(i * HALF, (i + 1) * HALF)
        parts = [(stat, mine[rows])] + [
            (stat_of(got[C:], i) + c, got[rows].astype(F32)) for got in (from_low, from_high)
        ]
        halves.append(merge(parts)[1])
    mixed_in = jnp.concatenate(halves, 0).astype(BF16)
    mixed = (dot(mixed_in, weight[:, 2 * C :], ((0,), (0,))) + small[4:5, 2 * C :]).astype(BF16)
    attended = dot(mixed, wp[...], ((1,), (0,))) + small[3:4, :C] + block[...].astype(F32)
    out[...] = attended.astype(BF16)


def prepare_kernel(weight, gain1, bias1, gain2, bias_p, bias_qkv, bias_up, out, small):
    w = [[weight[b, c].astype(F32) for c in range(3)] for b in range(3)]

    def pairs(a, b, c):
        return ((a, b + c), (a + b, c))

    by_row = [pairs(*(w[b][c] for b in range(3))) for c in range(3)]
    for di in range(2):
        for rt in range(2):
            by_column = pairs(*(by_row[c][di][rt] for c in range(3)))
            for dj in range(2):
                for ct in range(2):
                    value = jnp.concatenate(
                        [by_column[dj][ct], jnp.zeros((256 - OUT, C), F32)], 0
                    )
                    out[di, dj, rt, ct * C : (ct + 1) * C] = value.T.astype(BF16)
    small[...] = jnp.zeros_like(small)
    for i, ref in enumerate((gain1, bias1, gain2, bias_p, bias_qkv, bias_up)):
        small[i : i + 1, : ref.shape[1]] = ref[...]


def fill_plain(scratch, index, row):
    def store(variant, value):
        scratch[index, :, variant * C : (variant + 1) * C] = value

    col_variants(row.astype(F32), store)


def store_phase(wide, row, dj, value):
    for part in range(2):
        wide[part, row, pl.ds(dj, W, stride=2), :] = value[:, part * 128 : (part + 1) * 128]


def read_row(wide, row):
    return jnp.concatenate([wide[0, row].T, wide[1, row].T[: OUT - 128]], 0)


def up_inner_kernel(body, weight, small, out, edge, scratch, wide):
    for i in range(ROWS):
        fill_plain(scratch, i, body[i])
    b = small[5:6, :256]
    for di in range(2):
        for dj in range(2):
            full = scratch[:, :, dj * C : (dj + 2) * C].reshape(CELLS, 2 * C)
            if di == 0:
                here = dot(full, weight[0, dj, 1], ((1,), (0,))) + b
                beside = dot(full[: 2 * W], weight[0, dj, 0], ((1,), (0,)))
                parts = [here[:W], here[W : 2 * W] + beside[:W], here[2 * W :] + beside[W:]]
            else:
                here = dot(full, weight[1, dj, 0], ((1,), (0,))) + b
                beside = dot(full[W:], weight[1, dj, 1], ((1,), (0,)))
                parts = [here[:W] + beside[:W], here[W : 2 * W] + beside[W:], here[2 * W :]]
            for i, part in enumerate(parts):
                store_phase(wide, 2 * i + di, dj, part)
    for row in range(1, 2 * ROWS - 1):
        out[row] = read_row(wide, row).astype(BF16)
    edge[0] = read_row(wide, 0)
    edge[1] = read_row(wide, 2 * ROWS - 1)


def up_edges_kernel(low, high, weight, edge, start, out, scratch, wide):
    for row in range(1, 2 * ROWS - 1):
        out[row] = start[row]
    fill_plain(scratch, 0, low[0])
    fill_plain(scratch, 1, high[0])
    for side in range(2):
        for dj in range(2):
            left = scratch[side, :, dj * C : (dj + 2) * C]
            store_phase(wide, side, dj, dot(left, weight[side, dj, side], ((1,), (0,))))
        out[side * (2 * ROWS - 1)] = (edge[side] + read_row(wide, side)).astype(BF16)


def permute_z(value, by):
    pairs = [(x * ZN + z, x * ZN + (z + by) % ZN) for x in range(XN) for z in range(ZN)]
    return lax.ppermute(value, "rows", pairs)


def permute_x(value, by):
    pairs = [(x * ZN + z, (x + by) % XN * ZN + z) for x in range(XN) for z in range(ZN)]
    return lax.ppermute(value, "rows", pairs)


def to_bands(value, by):
    n = XN * ZN
    return lax.ppermute(value, "rows", [(i, i + by) for i in range(n) if 0 <= i + by < n])


def on_device(
    latent,
    norm1_gain,
    conv1_weight,
    conv1_bias,
    attention_gain,
    qkv_weight,
    qkv_bias,
    proj_weight,
    proj_bias,
    up_weight,
    up_bias,
):
    own = latent[0]
    two = lax.ppermute(own, "tm", [(t, t + 2) for t in range(TN - 2)])
    phases, small = call(
        prepare_kernel,
        [((2, 2, 2, 2 * C, 256), BF16), ((8, 3 * C), F32)],
        up_weight.transpose(0, 1, 3, 2),
        norm1_gain[None],
        conv1_bias[None],
        attention_gain[None],
        proj_bias[None],
        qkv_bias[None],
        up_bias[None],
        name="prepare",
        flops=1e7,
        nbytes=4e6,
    )
    w_two, w_one, w_own = (conv1_weight[i : i + 1] for i in range(3))
    acc = conv_band(own, small, w_own)
    odd = (lax.axis_index("tm") % 2).astype(jnp.int32).reshape(1)
    pairs = [(t, t ^ 1) for t in range(TN)]
    to_next, to_previous, pair = call(
        edge_payload_kernel,
        [((2, W, C), BF16)] * 2 + [((ROWS, W, C), BF16)],
        odd,
        own,
        two,
        acc,
        phases,
        name="edge_payload",
        specs=[SMEM, VM, VM, ANY, ANY],
    )
    low, high = to_bands(to_next, 1), to_bands(to_previous, -1)
    one = lax.ppermute(pair, "tm", pairs)
    acc = conv_band(two, small, w_two, acc)
    acc = conv_band(one, small, w_one, acc)
    pair_edges = call(
        pair_edges_kernel,
        [((2, W, C), BF16)],
        odd,
        low,
        high,
        acc,
        name="pair_edges",
        specs=[SMEM, VM, VM, ANY],
    )
    one_edges = lax.ppermute(pair_edges, "tm", pairs)
    acc = call(
        conv_edges_kernel,
        [((CELLS, C), F32)],
        low,
        high,
        small,
        w_own,
        w_two,
        acc,
        name="conv_edges",
        flops=2 * CELLS * 2 * C * C,
        scratch=[pltpu.VMEM((4, W, 3 * C), BF16)],
        aliases={5: 0},
    )
    block, normed = call(
        conv_last_kernel,
        [((CELLS, C), BF16)] * 2,
        one_edges,
        own,
        small,
        w_one,
        acc,
        name="conv_last",
        flops=2 * CELLS * C * C,
        scratch=[pltpu.VMEM((2, W, 3 * C), BF16)],
    )

    up, down = permute_z(normed, 1), permute_z(normed, -1)
    query, shift = call(
        query_kernel,
        [((C, CELLS), BF16), ((1, CELLS), F32)],
        normed,
        qkv_weight,
        small,
        name="queries",
        flops=4 * CELLS * C * C,
    )
    q_low, q_high = permute_x(query, 1), permute_x(query, -1)
    q_top, q_bottom = permute_x(q_low[:HALF], 1), permute_x(q_high[HALF:], -1)
    up2, down2 = permute_z(up, 1), permute_z(down, -1)
    early = [normed, up, down]
    near = [q_low, q_high, query]
    (state,) = attention_step(early, near)
    up2, down2 = after((up2, down2), state[0])
    up3, down3 = permute_z(up2, 1), permute_z(down2, -1)
    q_far = jnp.concatenate([q_top, q_bottom], 0)
    (far,) = attention_step(early, [q_far])
    queries = near + [q_far]
    state, far = attention_step([up2, down2], queries, (state, far))
    up4, down4 = permute_z(up3[: CELLS // 2], 1), permute_z(down3[CELLS // 2 :], -1)
    state, far = attention_step([up3, down3], queries, (state, far))
    last = [up4, down4]
    pay_t, pay_b = opposite(last, q_far, far)
    half_low, half_high = permute_x(pay_t, 1), permute_x(pay_b, -1)
    (sides,) = attention_step(last, near, (state,), 0, 2 * CELLS)
    to_low, to_high = call(
        relay_kernel,
        [((C + STAT, CELLS), BF16)] * 2,
        half_low,
        half_high,
        *sides,
        name="relay",
    )
    from_low, from_high = permute_x(to_high, 1), permute_x(to_low, -1)
    (mine,) = attention_step(last, near, (state,), 2 * CELLS, 3 * CELLS)
    attended = call(
        finish_kernel,
        [((CELLS, C), BF16)],
        from_low,
        from_high,
        *mine,
        shift,
        qkv_weight,
        proj_weight,
        small,
        block,
        name="finish",
        flops=4 * CELLS * C * C,
    ).reshape(ROWS, W, C)
    edge_low, edge_high = to_bands(attended[2:], 1), to_bands(attended[:1], -1)
    inner, edge = call(
        up_inner_kernel,
        [((2 * ROWS, OUT, 2 * W), BF16), ((2, OUT, 2 * W), F32)],
        attended,
        phases,
        small,
        name="up_inner",
        flops=2 * CELLS * 14 * C * OUT,
        scratch=[
            pltpu.VMEM((ROWS, W, 3 * C), BF16),
            pltpu.VMEM((2, 2 * ROWS, 2 * W, 128), F32),
        ],
    )
    result = call(
        up_edges_kernel,
        [((2 * ROWS, OUT, 2 * W), BF16)],
        edge_low,
        edge_high,
        phases,
        edge,
        inner,
        name="up_edges",
        flops=2 * CELLS * 2 * C * OUT,
        scratch=[
            pltpu.VMEM((2, W, 3 * C), BF16),
            pltpu.VMEM((2, 2, 2 * W, 128), F32),
        ],
        aliases={4: 0},
    )
    return result.transpose(0, 2, 1)[None]


def solution(mesh):
    return jax.shard_map(
        on_device,
        mesh=mesh,
        in_specs=(P("tm", "rows", None, None), P(), P(), P(), P(), P(), P(), P(), P(), P(), P()),
        out_specs=P("tm", "rows", None, None),
        check_vma=False,
    )
```

```python
import functools
import math

import jax
import jax.numpy as jnp
from jax import lax
from jax.experimental import pallas as pl
from jax.experimental.pallas import tpu as pltpu
from jax.sharding import PartitionSpec as P

F32 = jnp.float32
BF16 = jnp.bfloat16
ROWS = 3
W = 128
C = 384
OUT = 192
CELLS = ROWS * W
XN, ZN, TN = 4, 8, 8
QALL = XN * CELLS
HALF = C // 2
STAT = 16
LOG2E = math.log2(math.e)


def dot(a, b, dims):
    return lax.dot_general(a, b, (dims, ((), ())), preferred_element_type=F32)


def params(mib=32):
    return pltpu.CompilerParams(vmem_limit_bytes=mib * 2**20)


def cost(flops, bytes_accessed):
    return pl.CostEstimate(flops=int(flops), bytes_accessed=int(bytes_accessed), transcendentals=0)


VM = pl.BlockSpec(memory_space=pltpu.VMEM)
ANY = pl.BlockSpec(memory_space=pl.ANY)
HBM = pl.BlockSpec(memory_space=pltpu.HBM)


def call(body, outs, *args, name, flops=1e6, nbytes=1e6, aliases=None, scratch=(), mib=32, specs=None, out_spec=VM):
    shapes = [jax.ShapeDtypeStruct(shape, dtype) for shape, dtype in outs]
    result = pl.pallas_call(
        body,
        in_specs=specs or [VM] * len(args),
        out_specs=[out_spec] * len(shapes),
        out_shape=shapes,
        input_output_aliases=aliases or {},
        scratch_shapes=list(scratch),
        compiler_params=params(mib),
        cost_estimate=cost(flops, nbytes),
        name=name,
    )(*args)
    return result[0] if len(shapes) == 1 else result


def col_variants(y, store):
    column = lax.broadcasted_iota(jnp.int32, y.shape, 0)
    before = jnp.where(column == 0, 0.0, pltpu.roll(y, 1, 0))
    after = jnp.where(column == W - 1, 0.0, pltpu.roll(y, W - 1, 0))
    store(0, before.astype(BF16))
    store(1, y.astype(BF16))
    store(2, after.astype(BF16))


def activate(row, gain):
    x = row.astype(F32)
    y = x * lax.rsqrt(jnp.mean(x * x, -1, keepdims=True) + 1e-6) * gain
    y = y / (1.0 + jnp.exp(-y))
    return y.astype(BF16).astype(F32)


def fill_rows(scratch, rows, gain):
    for index, row in enumerate(rows):
        y = activate(row, gain)

        def store(variant, value, index=index):
            scratch[index, :, variant * C : (variant + 1) * C] = value

        col_variants(y, store)


def conv_band_kernel(first, time_tap, frame, small, weight, *refs):
    start = None if first else refs[0]
    acc, beside, scratch, middle, sem = refs[-5:]
    copies = [
        pltpu.make_async_copy(weight.at[time_tap, b], target, sem.at[b])
        for b, target in enumerate((beside.at[0], middle, beside.at[1]))
    ]
    for b in (1, 0, 2):
        copies[b].start()
    fill_rows(scratch, [frame[i] for i in range(ROWS)], small[0:1, :C])
    band = scratch[...].reshape(CELLS, 3 * C)
    copies[1].wait()
    total = dot(band, middle[...].reshape(3 * C, C), ((1,), (0,)))
    if not first:
        total += start[...]
    copies[0].wait()
    down = dot(band[: 2 * W], beside[0].reshape(3 * C, C), ((1,), (0,)))
    copies[2].wait()
    up = dot(band[W:], beside[1].reshape(3 * C, C), ((1,), (0,)))
    acc[:W] = total[:W] + up[:W]
    acc[W : 2 * W] = total[W : 2 * W] + down[:W] + up[W:]
    acc[2 * W :] = total[2 * W :] + down[W:]


def conv_band(frame, small, weight, time_tap, start=None):
    first = start is None
    return call(
        functools.partial(conv_band_kernel, first, time_tap),
        [((CELLS, C), F32), ((2, 3, C, C), BF16)],
        frame,
        small,
        weight,
        *(() if first else (start,)),
        name="conv_band",
        flops=2 * CELLS * 9 * C * C,
        scratch=[
            pltpu.VMEM((ROWS, W, 3 * C), BF16),
            pltpu.VMEM((3, C, C), BF16),
            pltpu.SemaphoreType.DMA((3,)),
        ],
        specs=[VM, VM, HBM] + ([] if first else [VM]),
        aliases=None if first else {3: 0},
        mib=49,
    )


def edge_taps(scratch, low, high, weight):
    left = dot(scratch[low], weight[0].reshape(3 * C, C), ((1,), (0,)))
    right = dot(scratch[high], weight[1].reshape(3 * C, C), ((1,), (0,)))
    return left, right


def conv_edges_kernel(low, high, small, w_own, w_two, start, acc, scratch):
    fill_rows(scratch, [low[0], low[1], high[0], high[1]], small[0:1, :C])
    own = edge_taps(scratch, 0, 2, w_own)
    two = edge_taps(scratch, 1, 3, w_two)
    acc[...] = start[...]
    acc[:W] += own[0] + two[0]
    acc[2 * W :] += own[1] + two[1]


def conv_last_kernel(edges, own, small, weight, start, block, normed, scratch):
    fill_rows(scratch, [edges[0], edges[1]], small[0:1, :C])
    sides = edge_taps(scratch, 0, 1, weight)
    bias, gain2 = small[1:2, :C], small[2:3, :C]
    for i in range(ROWS):
        rows = slice(i * W, (i + 1) * W)
        total = start[rows] + bias
        if i != 1:
            total += sides[i // 2]
        x = (own[i].astype(F32) + total.astype(BF16).astype(F32)).astype(BF16)
        block[rows] = x
        x = x.astype(F32)
        x = x * lax.rsqrt(jnp.mean(x * x, -1, keepdims=True) + 1e-6) * gain2
        normed[rows] = x.astype(BF16)


SMEM = pl.BlockSpec(memory_space=pltpu.SMEM)


def edge_payload_kernel(odd, own, two, _acc, _phases, to_next, to_previous, pair):
    to_next[0] = own[ROWS - 1]
    to_next[1] = two[ROWS - 1]
    to_previous[0] = own[0]
    to_previous[1] = two[0]

    @pl.when(odd[0] == 0)
    def _():
        pair[...] = own[...]

    @pl.when(odd[0] == 1)
    def _():
        pair[...] = two[...]


def pair_edges_kernel(odd, low, high, _acc, out):
    index = odd[0]
    out[0] = low[index]
    out[1] = high[index]


def query_kernel(normed, weight, small, out, shift):
    scale = C**-0.5 * LOG2E
    wq, wk = weight[:, :C], weight[:, C : 2 * C]
    q = (dot(normed[...], wq, ((1,), (0,))) + small[4:5, :C]).astype(BF16)
    out[...] = (dot(wk, q, ((1,), (1,))) * scale).astype(BF16)
    bk = jnp.broadcast_to(small[4:5, C : 2 * C], (8, C))
    shift[...] = dot(bk, q.astype(F32), ((1,), (1,)))[:1] * scale


def spans(refs, low, high):
    at = 0
    for ref in refs:
        n = ref.shape[1]
        first, last = max(low, at), min(high, at + n)
        if first < last:
            yield ref, first - at, last - at, first - low, last - low
        at += n


def read(refs, low, high):
    pieces = [ref[:, a:b] for ref, a, b, _, _ in spans(refs, low, high)]
    return pieces[0] if len(pieces) == 1 else jnp.concatenate(pieces, 1)


def write(refs, low, high, value):
    for ref, a, b, first, last in spans(refs, low, high):
        ref[:, a:b] = value[:, first:last]


def joined(refs):
    return refs[0][...] if len(refs) == 1 else jnp.concatenate([r[...] for r in refs], 0)


def softmax_tiles(keys, tiles, q_of, old_of, give):
    keys_t = keys.T

    def scores(tile):
        return dot(keys, q_of(*tile), ((1,), (0,)))

    following = scores(tiles[0])
    for i, tile in enumerate(tiles):
        s = following
        if i + 1 < len(tiles):
            following = scores(tiles[i + 1])
        old = old_of(*tile)
        m = jnp.max(s, 0, keepdims=True)
        if old is not None:
            m = jnp.maximum(m, old[0])
        p = jnp.exp2(s - m)
        total = jnp.sum(p, 0, keepdims=True)
        acc = dot(keys_t, p.astype(BF16), ((1,), (0,)))
        if old is not None:
            alpha = jnp.exp2(old[0] - m)
            total = total + alpha * old[1]
            acc = acc + alpha * old[2]
        give(*tile, (m, total, acc))


def tiles_of(low, high, size=512):
    return [(at, min(at + size, high)) for at in range(low, high, size)]


def attention_kernel(n_keys, n_q, n_state, n_out, low, high, *refs):
    keys = joined(refs[:n_keys])
    queries = refs[n_keys : n_keys + n_q]
    state = refs[n_keys + n_q : n_keys + n_q + 3 * n_state]
    outs = refs[n_keys + n_q + 3 * n_state :]

    def old_of(a, b):
        return [read(state[i::3], a, b) for i in range(3)] if n_state else None

    def give(a, b, values):
        for i, value in enumerate(values):
            write(outs[i::3], a - low, b - low, value)

    softmax_tiles(keys, tiles_of(low, high), lambda a, b: read(queries, a, b), old_of, give)


def attention_step(keys, queries, state=(), low=0, high=None):
    widths = [q.shape[1] for q in queries]
    high = sum(widths) if high is None else high
    rows = sum(k.shape[0] for k in keys)
    whole_state = bool(state) and high - low == sum(s[0].shape[1] for s in state)
    outs = [s[0].shape[1] for s in state] if whole_state else [high - low]
    flat = [v for s in state for v in s]
    before = len(keys) + len(queries)
    result = call(
        functools.partial(
            attention_kernel, len(keys), len(queries), len(state), len(outs), low, high
        ),
        [shape for n in outs for shape in (((1, n), F32), ((1, n), F32), ((C, n), F32))],
        *keys,
        *queries,
        *flat,
        name="attention_step",
        flops=4 * rows * (high - low) * C,
        nbytes=6e6,
        aliases={before + i: i for i in range(len(flat))} if whole_state else None,
    )
    return [tuple(result[i : i + 3]) for i in range(0, len(result), 3)]


def gate_kernel(*refs):
    pass


def after(values, done):
    count = len(values)
    return call(
        gate_kernel,
        [(v.shape, v.dtype) for v in values],
        *values,
        done,
        name="gate",
        flops=1,
        nbytes=1,
        specs=[ANY] * (count + 1),
        out_spec=ANY,
        aliases={i: i for i in range(count)},
    )


def split3(x):
    hi = x.astype(BF16)
    rest = x - hi.astype(F32)
    mid = rest.astype(BF16)
    low = (rest - mid.astype(F32)).astype(BF16)
    return hi, mid, low


def stat_rows(parts):
    n = parts[0].shape[1]
    row = lax.broadcasted_iota(jnp.int32, (STAT, n), 0)
    block = jnp.zeros((STAT, n), F32)
    for i, part in enumerate(parts):
        for j, piece in enumerate(split3(part)):
            block = jnp.where(row == 3 * i + j, piece.astype(F32), block)
    return block.astype(BF16)


def stat_of(block, i):
    b = block.astype(F32)
    return b[3 * i : 3 * i + 1] + b[3 * i + 1 : 3 * i + 2] + b[3 * i + 2 : 3 * i + 3]


def opposite_kernel(n_keys, *refs):
    q, m_old, l_old, acc_old, top, bottom = refs[n_keys:]

    def give(_a, _b, values):
        m, total, acc = values
        out = (acc / total).astype(BF16)
        stats = stat_rows([m + jnp.log2(total)])
        top[:HALF] = out[:HALF]
        top[HALF:] = stats
        bottom[:HALF] = out[HALF:]
        bottom[HALF:] = stats

    old = lambda a, b: (m_old[...], l_old[...], acc_old[...])
    softmax_tiles(joined(refs[:n_keys]), [(0, CELLS)], lambda a, b: q[...], old, give)


def opposite(keys, q_far, state):
    rows = sum(k.shape[0] for k in keys)
    return call(
        functools.partial(opposite_kernel, len(keys)),
        [((HALF + STAT, CELLS), BF16)] * 2,
        *keys,
        q_far,
        *state,
        name="opposite",
        flops=4 * rows * CELLS * C,
        nbytes=2e6,
    )


def merge(parts):
    top = functools.reduce(jnp.maximum, [s for s, _ in parts])
    w = [jnp.exp2(s - top) for s, _ in parts]
    total = functools.reduce(jnp.add, w)
    inverse = 1.0 / total
    out = functools.reduce(jnp.add, [(a * inverse) * o for a, (_, o) in zip(w, parts)])
    return top + jnp.log2(total), out


def relay_kernel(from_low, from_high, m, total, acc, to_low, to_high):
    for side, got, out in ((0, from_high, to_low), (1, from_low, to_high)):
        cols = slice(side * CELLS, (side + 1) * CELLS)
        stat = m[:, cols] + jnp.log2(total[:, cols])
        mine = acc[:, cols] / total[:, cols]
        theirs = (stat_of(got[HALF:], 0), got[:HALF].astype(F32))
        if side == 0:
            stat_t, half_t = stat, mine[:HALF]
            stat_b, half_b = merge([(stat, mine[HALF:]), theirs])
        else:
            stat_t, half_t = merge([(stat, mine[:HALF]), theirs])
            stat_b, half_b = stat, mine[HALF:]
        out[:HALF] = half_t.astype(BF16)
        out[HALF:C] = half_b.astype(BF16)
        out[C:] = stat_rows([stat_t, stat_b])


def finish_kernel(from_low, from_high, m, total, acc, shift, weight, wp, small, block, out):
    c = shift[...]
    stat = m[...] + jnp.log2(total[...]) + c
    mine = acc[...] / total[...]
    halves = []
    for i in range(2):
        rows = slice(i * HALF, (i + 1) * HALF)
        parts = [(stat, mine[rows])] + [
            (stat_of(got[C:], i) + c, got[rows].astype(F32)) for got in (from_low, from_high)
        ]
        halves.append(merge(parts)[1])
    mixed_in = jnp.concatenate(halves, 0).astype(BF16)
    mixed = (dot(mixed_in, weight[:, 2 * C :], ((0,), (0,))) + small[4:5, 2 * C :]).astype(BF16)
    attended = dot(mixed, wp[...], ((1,), (0,))) + small[3:4, :C] + block[...].astype(F32)
    out[...] = attended.astype(BF16)


def prepare_kernel(weight, gain1, bias1, gain2, bias_p, bias_qkv, bias_up, out, small):
    w = [[weight[b, c].astype(F32) for c in range(3)] for b in range(3)]

    def pairs(a, b, c):
        return ((a, b + c), (a + b, c))

    by_row = [pairs(*(w[b][c] for b in range(3))) for c in range(3)]
    for di in range(2):
        for rt in range(2):
            by_column = pairs(*(by_row[c][di][rt] for c in range(3)))
            for dj in range(2):
                for ct in range(2):
                    value = jnp.concatenate(
                        [by_column[dj][ct], jnp.zeros((256 - OUT, C), F32)], 0
                    )
                    out[di, dj, rt, ct * C : (ct + 1) * C] = value.T.astype(BF16)
    small[...] = jnp.zeros_like(small)
    for i, ref in enumerate((gain1, bias1, gain2, bias_p, bias_qkv, bias_up)):
        small[i : i + 1, : ref.shape[1]] = ref[...]


def fill_plain(scratch, index, row):
    def store(variant, value):
        scratch[index, :, variant * C : (variant + 1) * C] = value

    col_variants(row.astype(F32), store)


def store_phase(wide, row, dj, value):
    for part in range(2):
        wide[part, row, pl.ds(dj, W, stride=2), :] = value[:, part * 128 : (part + 1) * 128]


def read_row(wide, row):
    return jnp.concatenate([wide[0, row].T, wide[1, row].T[: OUT - 128]], 0)


def up_inner_kernel(body, weight, small, out, edge, scratch, wide):
    for i in range(ROWS):
        fill_plain(scratch, i, body[i])
    b = small[5:6, :256]
    for di in range(2):
        for dj in range(2):
            full = scratch[:, :, dj * C : (dj + 2) * C].reshape(CELLS, 2 * C)
            if di == 0:
                here = dot(full, weight[0, dj, 1], ((1,), (0,))) + b
                beside = dot(full[: 2 * W], weight[0, dj, 0], ((1,), (0,)))
                parts = [here[:W], here[W : 2 * W] + beside[:W], here[2 * W :] + beside[W:]]
            else:
                here = dot(full, weight[1, dj, 0], ((1,), (0,))) + b
                beside = dot(full[W:], weight[1, dj, 1], ((1,), (0,)))
                parts = [here[:W] + beside[:W], here[W : 2 * W] + beside[W:], here[2 * W :]]
            for i, part in enumerate(parts):
                store_phase(wide, 2 * i + di, dj, part)
    for row in range(1, 2 * ROWS - 1):
        out[row] = read_row(wide, row).astype(BF16)
    edge[0] = read_row(wide, 0)
    edge[1] = read_row(wide, 2 * ROWS - 1)


def up_edges_kernel(low, high, weight, edge, _start, out, scratch, wide, rows, sem):
    fill_plain(scratch, 0, low[0])
    fill_plain(scratch, 1, high[0])
    copies = []
    for side in range(2):
        for dj in range(2):
            left = scratch[side, :, dj * C : (dj + 2) * C]
            store_phase(wide, side, dj, dot(left, weight[side, dj, side], ((1,), (0,))))
        rows[side] = (edge[side] + read_row(wide, side)).astype(BF16)
        row = out.at[side * (2 * ROWS - 1)]
        copies.append(pltpu.make_async_copy(rows.at[side], row, sem.at[side]))
        copies[side].start()
    for copy in copies:
        copy.wait()


def permute_z(value, by):
    pairs = [(x * ZN + z, x * ZN + (z + by) % ZN) for x in range(XN) for z in range(ZN)]
    return lax.ppermute(value, "rows", pairs)


def permute_x(value, by):
    pairs = [(x * ZN + z, (x + by) % XN * ZN + z) for x in range(XN) for z in range(ZN)]
    return lax.ppermute(value, "rows", pairs)


def to_bands(value, by):
    n = XN * ZN
    return lax.ppermute(value, "rows", [(i, i + by) for i in range(n) if 0 <= i + by < n])


def on_device(
    latent,
    norm1_gain,
    conv1_weight,
    conv1_bias,
    attention_gain,
    qkv_weight,
    qkv_bias,
    proj_weight,
    proj_bias,
    up_weight,
    up_bias,
):
    own = latent[0]
    two = lax.ppermute(own, "tm", [(t, t + 2) for t in range(TN - 2)])
    phases, small = call(
        prepare_kernel,
        [((2, 2, 2, 2 * C, 256), BF16), ((8, 3 * C), F32)],
        up_weight.transpose(0, 1, 3, 2),
        norm1_gain[None],
        conv1_bias[None],
        attention_gain[None],
        proj_bias[None],
        qkv_bias[None],
        up_bias[None],
        name="prepare",
        flops=1e7,
        nbytes=4e6,
    )
    acc, w_own = conv_band(own, small, conv1_weight, 2)
    odd = (lax.axis_index("tm") % 2).astype(jnp.int32).reshape(1)
    pairs = [(t, t ^ 1) for t in range(TN)]
    to_next, to_previous, pair = call(
        edge_payload_kernel,
        [((2, W, C), BF16)] * 2 + [((ROWS, W, C), BF16)],
        odd,
        own,
        two,
        acc,
        phases,
        name="edge_payload",
        specs=[SMEM, VM, VM, ANY, ANY],
    )
    low, high = to_bands(to_next, 1), to_bands(to_previous, -1)
    one = lax.ppermute(pair, "tm", pairs)
    acc, w_two = conv_band(two, small, conv1_weight, 0, acc)
    acc, w_one = conv_band(one, small, conv1_weight, 1, acc)
    pair_edges = call(
        pair_edges_kernel,
        [((2, W, C), BF16)],
        odd,
        low,
        high,
        acc,
        name="pair_edges",
        specs=[SMEM, VM, VM, ANY],
    )
    one_edges = lax.ppermute(pair_edges, "tm", pairs)
    acc = call(
        conv_edges_kernel,
        [((CELLS, C), F32)],
        low,
        high,
        small,
        w_own,
        w_two,
        acc,
        name="conv_edges",
        flops=2 * CELLS * 2 * C * C,
        scratch=[pltpu.VMEM((4, W, 3 * C), BF16)],
        aliases={5: 0},
    )
    block, normed = call(
        conv_last_kernel,
        [((CELLS, C), BF16)] * 2,
        one_edges,
        own,
        small,
        w_one,
        acc,
        name="conv_last",
        flops=2 * CELLS * C * C,
        scratch=[pltpu.VMEM((2, W, 3 * C), BF16)],
    )

    up, down = permute_z(normed, 1), permute_z(normed, -1)
    query, shift = call(
        query_kernel,
        [((C, CELLS), BF16), ((1, CELLS), F32)],
        normed,
        qkv_weight,
        small,
        name="queries",
        flops=4 * CELLS * C * C,
    )
    q_low, q_high = permute_x(query, 1), permute_x(query, -1)
    q_far = permute_x(query, 2)
    up2, down2 = permute_z(up, 1), permute_z(down, -1)
    early = [normed, up, down]
    near = [q_low, q_high, query]
    (state,) = attention_step(early, near)
    up2, down2 = after((up2, down2), state[0])
    up3, down3 = permute_z(up2, 1), permute_z(down2, -1)
    (far,) = attention_step(early, [q_far])
    queries = near + [q_far]
    state, far = attention_step([up2, down2], queries, (state, far))
    up4, down4 = permute_z(up3[: CELLS // 2], 1), permute_z(down3[CELLS // 2 :], -1)
    state, far = attention_step([up3, down3], queries, (state, far))
    last = [up4, down4]
    pay_t, pay_b = opposite(last, q_far, far)
    half_low, half_high = permute_x(pay_t, 1), permute_x(pay_b, -1)
    (sides,) = attention_step(last, near, (state,), 0, 2 * CELLS)
    to_low, to_high = call(
        relay_kernel,
        [((C + STAT, CELLS), BF16)] * 2,
        half_low,
        half_high,
        *sides,
        name="relay",
    )
    from_low, from_high = permute_x(to_high, 1), permute_x(to_low, -1)
    (mine,) = attention_step(last, near, (state,), 2 * CELLS, 3 * CELLS)
    attended = call(
        finish_kernel,
        [((CELLS, C), BF16)],
        from_low,
        from_high,
        *mine,
        shift,
        qkv_weight,
        proj_weight,
        small,
        block,
        name="finish",
        flops=4 * CELLS * C * C,
    ).reshape(ROWS, W, C)
    edge_low, edge_high = to_bands(attended[2:], 1), to_bands(attended[:1], -1)
    inner, edge = call(
        up_inner_kernel,
        [((2 * ROWS, OUT, 2 * W), BF16), ((2, OUT, 2 * W), F32)],
        attended,
        phases,
        small,
        name="up_inner",
        flops=2 * CELLS * 14 * C * OUT,
        scratch=[
            pltpu.VMEM((ROWS, W, 3 * C), BF16),
            pltpu.VMEM((2, 2 * ROWS, 2 * W, 128), F32),
        ],
    )
    result = call(
        up_edges_kernel,
        [((2 * ROWS, OUT, 2 * W), BF16)],
        edge_low,
        edge_high,
        phases,
        edge,
        inner,
        name="up_edges",
        flops=2 * CELLS * 2 * C * OUT,
        scratch=[
            pltpu.VMEM((2, W, 3 * C), BF16),
            pltpu.VMEM((2, 2, 2 * W, 128), F32),
            pltpu.VMEM((2, OUT, 2 * W), BF16),
            pltpu.SemaphoreType.DMA((2,)),
        ],
        specs=[VM, VM, VM, VM, ANY],
        out_spec=ANY,
        aliases={4: 0},
    )
    return result.transpose(0, 2, 1)[None]


def solution(mesh):
    return jax.shard_map(
        on_device,
        mesh=mesh,
        in_specs=(P("tm", "rows", None, None), P(), P(), P(), P(), P(), P(), P(), P(), P(), P()),
        out_specs=P("tm", "rows", None, None),
        check_vma=False,
    )
```

```python
import functools
import math

import jax
import jax.numpy as jnp
from jax import lax
from jax.experimental import pallas as pl
from jax.experimental.pallas import tpu as pltpu
from jax.sharding import PartitionSpec as P

F32 = jnp.float32
BF16 = jnp.bfloat16
ROWS = 3
W = 128
C = 384
OUT = 192
CELLS = ROWS * W
XN, ZN, TN = 4, 8, 8
QALL = XN * CELLS
HALF = C // 2
STAT = 16
LOG2E = math.log2(math.e)


def dot(a, b, dims):
    return lax.dot_general(a, b, (dims, ((), ())), preferred_element_type=F32)


def params(mib=32):
    return pltpu.CompilerParams(vmem_limit_bytes=mib * 2**20)


def cost(flops, bytes_accessed):
    return pl.CostEstimate(flops=int(flops), bytes_accessed=int(bytes_accessed), transcendentals=0)


VM = pl.BlockSpec(memory_space=pltpu.VMEM)
ANY = pl.BlockSpec(memory_space=pl.ANY)
HBM = pl.BlockSpec(memory_space=pltpu.HBM)


def call(body, outs, *args, name, flops=1e6, nbytes=1e6, aliases=None, scratch=(), mib=32, specs=None, out_spec=VM):
    shapes = [jax.ShapeDtypeStruct(shape, dtype) for shape, dtype in outs]
    result = pl.pallas_call(
        body,
        in_specs=specs or [VM] * len(args),
        out_specs=[out_spec] * len(shapes),
        out_shape=shapes,
        input_output_aliases=aliases or {},
        scratch_shapes=list(scratch),
        compiler_params=params(mib),
        cost_estimate=cost(flops, nbytes),
        name=name,
    )(*args)
    return result[0] if len(shapes) == 1 else result


def col_variants(y, store):
    column = lax.broadcasted_iota(jnp.int32, y.shape, 0)
    before = jnp.where(column == 0, 0.0, pltpu.roll(y, 1, 0))
    after = jnp.where(column == W - 1, 0.0, pltpu.roll(y, W - 1, 0))
    store(0, before.astype(BF16))
    store(1, y.astype(BF16))
    store(2, after.astype(BF16))


def activate(row, gain):
    x = row.astype(F32)
    y = x * lax.rsqrt(jnp.mean(x * x, -1, keepdims=True) + 1e-6) * gain
    y = y / (1.0 + jnp.exp(-y))
    return y.astype(BF16).astype(F32)


def fill_rows(scratch, rows, gain):
    for index, row in enumerate(rows):
        y = activate(row, gain)

        def store(variant, value, index=index):
            scratch[index, :, variant * C : (variant + 1) * C] = value

        col_variants(y, store)


def conv_band_kernel(first, time_tap, frame, small, weight, *refs):
    start = None if first else refs[0]
    acc, beside, scratch, middle, sem = refs[-5:]
    copies = [
        pltpu.make_async_copy(weight.at[time_tap, b], target, sem.at[b])
        for b, target in enumerate((beside.at[0], middle, beside.at[1]))
    ]
    for b in (1, 0, 2):
        copies[b].start()
    fill_rows(scratch, [frame[i] for i in range(ROWS)], small[0:1, :C])
    band = scratch[...].reshape(CELLS, 3 * C)
    copies[1].wait()
    total = dot(band, middle[...].reshape(3 * C, C), ((1,), (0,)))
    if not first:
        total += start[...]
    copies[0].wait()
    down = dot(band[: 2 * W], beside[0].reshape(3 * C, C), ((1,), (0,)))
    copies[2].wait()
    up = dot(band[W:], beside[1].reshape(3 * C, C), ((1,), (0,)))
    acc[:W] = total[:W] + up[:W]
    acc[W : 2 * W] = total[W : 2 * W] + down[:W] + up[W:]
    acc[2 * W :] = total[2 * W :] + down[W:]


def conv_band(frame, small, weight, time_tap, start=None):
    first = start is None
    return call(
        functools.partial(conv_band_kernel, first, time_tap),
        [((CELLS, C), F32), ((2, 3, C, C), BF16)],
        frame,
        small,
        weight,
        *(() if first else (start,)),
        name="conv_band",
        flops=2 * CELLS * 9 * C * C,
        scratch=[
            pltpu.VMEM((ROWS, W, 3 * C), BF16),
            pltpu.VMEM((3, C, C), BF16),
            pltpu.SemaphoreType.DMA((3,)),
        ],
        specs=[VM, VM, HBM] + ([] if first else [VM]),
        aliases=None if first else {3: 0},
        mib=49,
    )


def edge_taps(scratch, low, high, weight):
    left = dot(scratch[low], weight[0].reshape(3 * C, C), ((1,), (0,)))
    right = dot(scratch[high], weight[1].reshape(3 * C, C), ((1,), (0,)))
    return left, right


def conv_edges_kernel(low, high, small, w_own, w_two, start, acc, scratch):
    fill_rows(scratch, [low[0], low[1], high[0], high[1]], small[0:1, :C])
    own = edge_taps(scratch, 0, 2, w_own)
    two = edge_taps(scratch, 1, 3, w_two)
    acc[...] = start[...]
    acc[:W] += own[0] + two[0]
    acc[2 * W :] += own[1] + two[1]


def conv_last_kernel(edges, own, small, weight, start, block, normed, scratch):
    fill_rows(scratch, [edges[0], edges[1]], small[0:1, :C])
    sides = edge_taps(scratch, 0, 1, weight)
    bias, gain2 = small[1:2, :C], small[2:3, :C]
    for i in range(ROWS):
        rows = slice(i * W, (i + 1) * W)
        total = start[rows] + bias
        if i != 1:
            total += sides[i // 2]
        x = (own[i].astype(F32) + total.astype(BF16).astype(F32)).astype(BF16)
        block[rows] = x
        x = x.astype(F32)
        x = x * lax.rsqrt(jnp.mean(x * x, -1, keepdims=True) + 1e-6) * gain2
        normed[rows] = x.astype(BF16)


SMEM = pl.BlockSpec(memory_space=pltpu.SMEM)


def edge_payload_kernel(odd, own, two, _acc, to_next, to_previous, pair):
    to_next[0] = own[ROWS - 1]
    to_next[1] = two[ROWS - 1]
    to_previous[0] = own[0]
    to_previous[1] = two[0]

    @pl.when(odd[0] == 0)
    def _():
        pair[...] = own[...]

    @pl.when(odd[0] == 1)
    def _():
        pair[...] = two[...]


def pair_edges_kernel(odd, low, high, _acc, out):
    index = odd[0]
    out[0] = low[index]
    out[1] = high[index]


def query_kernel(normed, weight, small, out, shift):
    scale = C**-0.5 * LOG2E
    wq, wk = weight[:, :C], weight[:, C : 2 * C]
    q = (dot(normed[...], wq, ((1,), (0,))) + small[4:5, :C]).astype(BF16)
    out[...] = (dot(wk, q, ((1,), (1,))) * scale).astype(BF16)
    bk = jnp.broadcast_to(small[4:5, C : 2 * C], (8, C))
    shift[...] = dot(bk, q.astype(F32), ((1,), (1,)))[:1] * scale


def spans(refs, low, high):
    at = 0
    for ref in refs:
        n = ref.shape[1]
        first, last = max(low, at), min(high, at + n)
        if first < last:
            yield ref, first - at, last - at, first - low, last - low
        at += n


def read(refs, low, high):
    pieces = [ref[:, a:b] for ref, a, b, _, _ in spans(refs, low, high)]
    return pieces[0] if len(pieces) == 1 else jnp.concatenate(pieces, 1)


def write(refs, low, high, value):
    for ref, a, b, first, last in spans(refs, low, high):
        ref[:, a:b] = value[:, first:last]


def joined(refs):
    return refs[0][...] if len(refs) == 1 else jnp.concatenate([r[...] for r in refs], 0)


def softmax_tiles(keys, tiles, q_of, old_of, give):
    keys_t = keys.T

    def scores(tile):
        return dot(keys, q_of(*tile), ((1,), (0,)))

    following = scores(tiles[0])
    for i, tile in enumerate(tiles):
        s = following
        if i + 1 < len(tiles):
            following = scores(tiles[i + 1])
        old = old_of(*tile)
        m = jnp.max(s, 0, keepdims=True)
        if old is not None:
            m = jnp.maximum(m, old[0])
        p = jnp.exp2(s - m)
        total = jnp.sum(p, 0, keepdims=True)
        acc = dot(keys_t, p.astype(BF16), ((1,), (0,)))
        if old is not None:
            alpha = jnp.exp2(old[0] - m)
            total = total + alpha * old[1]
            acc = acc + alpha * old[2]
        give(*tile, (m, total, acc))


def tiles_of(low, high, size=512):
    return [(at, min(at + size, high)) for at in range(low, high, size)]


def attention_kernel(n_keys, n_q, n_state, n_out, low, high, *refs):
    keys = joined(refs[:n_keys])
    queries = refs[n_keys : n_keys + n_q]
    state = refs[n_keys + n_q : n_keys + n_q + 3 * n_state]
    outs = refs[n_keys + n_q + 3 * n_state :]

    def old_of(a, b):
        return [read(state[i::3], a, b) for i in range(3)] if n_state else None

    def give(a, b, values):
        for i, value in enumerate(values):
            write(outs[i::3], a - low, b - low, value)

    softmax_tiles(keys, tiles_of(low, high), lambda a, b: read(queries, a, b), old_of, give)


def attention_step(keys, queries, state=(), low=0, high=None):
    widths = [q.shape[1] for q in queries]
    high = sum(widths) if high is None else high
    rows = sum(k.shape[0] for k in keys)
    whole_state = bool(state) and high - low == sum(s[0].shape[1] for s in state)
    outs = [s[0].shape[1] for s in state] if whole_state else [high - low]
    flat = [v for s in state for v in s]
    before = len(keys) + len(queries)
    result = call(
        functools.partial(
            attention_kernel, len(keys), len(queries), len(state), len(outs), low, high
        ),
        [shape for n in outs for shape in (((1, n), F32), ((1, n), F32), ((C, n), F32))],
        *keys,
        *queries,
        *flat,
        name="attention_step",
        flops=4 * rows * (high - low) * C,
        nbytes=6e6,
        aliases={before + i: i for i in range(len(flat))} if whole_state else None,
    )
    return [tuple(result[i : i + 3]) for i in range(0, len(result), 3)]


def gate_kernel(*refs):
    pass


def after(values, *done):
    count = len(values)
    return call(
        gate_kernel,
        [(v.shape, v.dtype) for v in values],
        *values,
        *done,
        name="gate",
        flops=1,
        nbytes=1,
        specs=[ANY] * (count + len(done)),
        out_spec=ANY,
        aliases={i: i for i in range(count)},
    )


def split3(x):
    hi = x.astype(BF16)
    rest = x - hi.astype(F32)
    mid = rest.astype(BF16)
    low = (rest - mid.astype(F32)).astype(BF16)
    return hi, mid, low


def stat_rows(parts):
    n = parts[0].shape[1]
    row = lax.broadcasted_iota(jnp.int32, (STAT, n), 0)
    block = jnp.zeros((STAT, n), F32)
    for i, part in enumerate(parts):
        for j, piece in enumerate(split3(part)):
            block = jnp.where(row == 3 * i + j, piece.astype(F32), block)
    return block.astype(BF16)


def stat_of(block, i):
    b = block.astype(F32)
    return b[3 * i : 3 * i + 1] + b[3 * i + 1 : 3 * i + 2] + b[3 * i + 2 : 3 * i + 3]


def opposite_kernel(n_keys, *refs):
    q, m_old, l_old, acc_old, top, bottom = refs[n_keys:]

    def give(_a, _b, values):
        m, total, acc = values
        out = (acc / total).astype(BF16)
        stats = stat_rows([m + jnp.log2(total)])
        top[:HALF] = out[:HALF]
        top[HALF:] = stats
        bottom[:HALF] = out[HALF:]
        bottom[HALF:] = stats

    old = lambda a, b: (m_old[...], l_old[...], acc_old[...])
    softmax_tiles(joined(refs[:n_keys]), [(0, CELLS)], lambda a, b: q[...], old, give)


def opposite(keys, q_far, state):
    rows = sum(k.shape[0] for k in keys)
    return call(
        functools.partial(opposite_kernel, len(keys)),
        [((HALF + STAT, CELLS), BF16)] * 2,
        *keys,
        q_far,
        *state,
        name="opposite",
        flops=4 * rows * CELLS * C,
        nbytes=2e6,
    )


def merge(parts):
    top = functools.reduce(jnp.maximum, [s for s, _ in parts])
    w = [jnp.exp2(s - top) for s, _ in parts]
    total = functools.reduce(jnp.add, w)
    inverse = 1.0 / total
    out = functools.reduce(jnp.add, [(a * inverse) * o for a, (_, o) in zip(w, parts)])
    return top + jnp.log2(total), out


def relay_kernel(from_low, from_high, m, total, acc, to_low, to_high):
    for side, got, out in ((0, from_high, to_low), (1, from_low, to_high)):
        cols = slice(side * CELLS, (side + 1) * CELLS)
        stat = m[:, cols] + jnp.log2(total[:, cols])
        mine = acc[:, cols] / total[:, cols]
        theirs = (stat_of(got[HALF:], 0), got[:HALF].astype(F32))
        if side == 0:
            stat_t, half_t = stat, mine[:HALF]
            stat_b, half_b = merge([(stat, mine[HALF:]), theirs])
        else:
            stat_t, half_t = merge([(stat, mine[:HALF]), theirs])
            stat_b, half_b = stat, mine[HALF:]
        out[:HALF] = half_t.astype(BF16)
        out[HALF:C] = half_b.astype(BF16)
        out[C:] = stat_rows([stat_t, stat_b])


def finish_kernel(from_low, from_high, m, total, acc, shift, weight, wp, small, block, out):
    c = shift[...]
    stat = m[...] + jnp.log2(total[...]) + c
    mine = acc[...] / total[...]
    halves = []
    for i in range(2):
        rows = slice(i * HALF, (i + 1) * HALF)
        parts = [(stat, mine[rows])] + [
            (stat_of(got[C:], i) + c, got[rows].astype(F32)) for got in (from_low, from_high)
        ]
        halves.append(merge(parts)[1])
    mixed_in = jnp.concatenate(halves, 0).astype(BF16)
    mixed = (dot(mixed_in, weight[:, 2 * C :], ((0,), (0,))) + small[4:5, 2 * C :]).astype(BF16)
    attended = dot(mixed, wp[...], ((1,), (0,))) + small[3:4, :C] + block[...].astype(F32)
    out[...] = attended.astype(BF16)


def pack_kernel(flat, small):
    small[...] = jnp.zeros_like(small)
    at = 0
    for i, n in enumerate((C, C, C, C, 3 * C, OUT)):
        small[i, :n] = flat[at : at + n]
        at += n


def up_phases_kernel(weight, out):
    w = [[weight[b, c].astype(F32) for c in range(3)] for b in range(3)]

    def pairs(a, b, c):
        return ((a, b + c), (a + b, c))

    by_row = [pairs(*(w[b][c] for b in range(3))) for c in range(3)]
    for di in range(2):
        for rt in range(2):
            by_column = pairs(*(by_row[c][di][rt] for c in range(3)))
            for dj in range(2):
                for ct in range(2):
                    value = jnp.concatenate(
                        [by_column[dj][ct], jnp.zeros((256 - OUT, C), F32)], 0
                    )
                    out[di, dj, rt, ct * C : (ct + 1) * C] = value.T.astype(BF16)


def fill_plain(scratch, index, row):
    def store(variant, value):
        scratch[index, :, variant * C : (variant + 1) * C] = value

    col_variants(row.astype(F32), store)


def store_phase(wide, row, dj, value):
    for part in range(2):
        wide[part, row, pl.ds(dj, W, stride=2), :] = value[:, part * 128 : (part + 1) * 128]


def read_row(wide, row):
    return jnp.concatenate([wide[0, row].T, wide[1, row].T[: OUT - 128]], 0)


def up_inner_kernel(body, weight, small, out, edge, scratch, wide):
    for i in range(ROWS):
        fill_plain(scratch, i, body[i])
    b = small[5:6, :256]
    for di in range(2):
        for dj in range(2):
            full = scratch[:, :, dj * C : (dj + 2) * C].reshape(CELLS, 2 * C)
            if di == 0:
                here = dot(full, weight[0, dj, 1], ((1,), (0,))) + b
                beside = dot(full[: 2 * W], weight[0, dj, 0], ((1,), (0,)))
                parts = [here[:W], here[W : 2 * W] + beside[:W], here[2 * W :] + beside[W:]]
            else:
                here = dot(full, weight[1, dj, 0], ((1,), (0,))) + b
                beside = dot(full[W:], weight[1, dj, 1], ((1,), (0,)))
                parts = [here[:W] + beside[:W], here[W : 2 * W] + beside[W:], here[2 * W :]]
            for i, part in enumerate(parts):
                store_phase(wide, 2 * i + di, dj, part)
    for row in range(1, 2 * ROWS - 1):
        out[row] = read_row(wide, row).astype(BF16)
    edge[0] = read_row(wide, 0)
    edge[1] = read_row(wide, 2 * ROWS - 1)


def up_edges_kernel(low, high, weight, edge, _start, out, scratch, wide, rows, sem):
    fill_plain(scratch, 0, low[0])
    fill_plain(scratch, 1, high[0])
    copies = []
    for side in range(2):
        for dj in range(2):
            left = scratch[side, :, dj * C : (dj + 2) * C]
            store_phase(wide, side, dj, dot(left, weight[side, dj, side], ((1,), (0,))))
        rows[side] = (edge[side] + read_row(wide, side)).astype(BF16)
        row = out.at[side * (2 * ROWS - 1)]
        copies.append(pltpu.make_async_copy(rows.at[side], row, sem.at[side]))
        copies[side].start()
    for copy in copies:
        copy.wait()


def permute_z(value, by):
    pairs = [(x * ZN + z, x * ZN + (z + by) % ZN) for x in range(XN) for z in range(ZN)]
    return lax.ppermute(value, "rows", pairs)


def permute_x(value, by):
    pairs = [(x * ZN + z, (x + by) % XN * ZN + z) for x in range(XN) for z in range(ZN)]
    return lax.ppermute(value, "rows", pairs)


def to_bands(value, by):
    n = XN * ZN
    return lax.ppermute(value, "rows", [(i, i + by) for i in range(n) if 0 <= i + by < n])


def on_device(
    latent,
    norm1_gain,
    conv1_weight,
    conv1_bias,
    attention_gain,
    qkv_weight,
    qkv_bias,
    proj_weight,
    proj_bias,
    up_weight,
    up_bias,
):
    own = latent[0]
    two = lax.ppermute(own, "tm", [(t, t + 2) for t in range(TN - 2)])
    flat = (norm1_gain, conv1_bias, attention_gain, proj_bias, qkv_bias, up_bias)
    small = call(pack_kernel, [((8, 3 * C), F32)], jnp.concatenate(flat), name="pack")
    acc, w_own = conv_band(own, small, conv1_weight, 2)
    odd = (lax.axis_index("tm") % 2).astype(jnp.int32).reshape(1)
    pairs = [(t, t ^ 1) for t in range(TN)]
    to_next, to_previous, pair = call(
        edge_payload_kernel,
        [((2, W, C), BF16)] * 2 + [((ROWS, W, C), BF16)],
        odd,
        own,
        two,
        acc,
        name="edge_payload",
        specs=[SMEM, VM, VM, ANY],
    )
    low, high = to_bands(to_next, 1), to_bands(to_previous, -1)
    one = lax.ppermute(pair, "tm", pairs)
    acc, w_two = conv_band(two, small, conv1_weight, 0, acc)
    acc, w_one = conv_band(one, small, conv1_weight, 1, acc)
    pair_edges = call(
        pair_edges_kernel,
        [((2, W, C), BF16)],
        odd,
        low,
        high,
        acc,
        name="pair_edges",
        specs=[SMEM, VM, VM, ANY],
    )
    one_edges = lax.ppermute(pair_edges, "tm", pairs)
    acc = call(
        conv_edges_kernel,
        [((CELLS, C), F32)],
        low,
        high,
        small,
        w_own,
        w_two,
        acc,
        name="conv_edges",
        flops=2 * CELLS * 2 * C * C,
        scratch=[pltpu.VMEM((4, W, 3 * C), BF16)],
        aliases={5: 0},
    )
    block, normed = call(
        conv_last_kernel,
        [((CELLS, C), BF16)] * 2,
        one_edges,
        own,
        small,
        w_one,
        acc,
        name="conv_last",
        flops=2 * CELLS * C * C,
        scratch=[pltpu.VMEM((2, W, 3 * C), BF16)],
    )

    up, down = permute_z(normed, 1), permute_z(normed, -1)
    query, shift = call(
        query_kernel,
        [((C, CELLS), BF16), ((1, CELLS), F32)],
        normed,
        qkv_weight,
        small,
        name="queries",
        flops=4 * CELLS * C * C,
    )
    q_low, q_high = permute_x(query, 1), permute_x(query, -1)
    q_far = permute_x(query, 2)
    up2, down2 = permute_z(up, 1), permute_z(down, -1)
    early = [normed, up, down]
    near = [q_low, q_high, query]
    (state,) = attention_step(early, near)
    phases = call(
        up_phases_kernel,
        [((2, 2, 2, 2 * C, 256), BF16)],
        up_weight.transpose(0, 1, 3, 2),
        name="up_phases",
        flops=1e7,
        nbytes=4e6,
    )
    up2, down2 = after((up2, down2), state[0], phases)
    up3, down3 = permute_z(up2, 1), permute_z(down2, -1)
    (far,) = attention_step(early, [q_far])
    queries = near + [q_far]
    state, far = attention_step([up2, down2], queries, (state, far))
    up4, down4 = permute_z(up3[: CELLS // 2], 1), permute_z(down3[CELLS // 2 :], -1)
    state, far = attention_step([up3, down3], queries, (state, far))
    last = [up4, down4]
    pay_t, pay_b = opposite(last, q_far, far)
    half_low, half_high = permute_x(pay_t, 1), permute_x(pay_b, -1)
    (sides,) = attention_step(last, near, (state,), 0, 2 * CELLS)
    to_low, to_high = call(
        relay_kernel,
        [((C + STAT, CELLS), BF16)] * 2,
        half_low,
        half_high,
        *sides,
        name="relay",
    )
    from_low, from_high = permute_x(to_high, 1), permute_x(to_low, -1)
    (mine,) = attention_step(last, near, (state,), 2 * CELLS, 3 * CELLS)
    attended = call(
        finish_kernel,
        [((CELLS, C), BF16)],
        from_low,
        from_high,
        *mine,
        shift,
        qkv_weight,
        proj_weight,
        small,
        block,
        name="finish",
        flops=4 * CELLS * C * C,
    ).reshape(ROWS, W, C)
    edge_low, edge_high = to_bands(attended[2:], 1), to_bands(attended[:1], -1)
    inner, edge = call(
        up_inner_kernel,
        [((2 * ROWS, OUT, 2 * W), BF16), ((2, OUT, 2 * W), F32)],
        attended,
        phases,
        small,
        name="up_inner",
        flops=2 * CELLS * 14 * C * OUT,
        scratch=[
            pltpu.VMEM((ROWS, W, 3 * C), BF16),
            pltpu.VMEM((2, 2 * ROWS, 2 * W, 128), F32),
        ],
    )
    result = call(
        up_edges_kernel,
        [((2 * ROWS, OUT, 2 * W), BF16)],
        edge_low,
        edge_high,
        phases,
        edge,
        inner,
        name="up_edges",
        flops=2 * CELLS * 2 * C * OUT,
        scratch=[
            pltpu.VMEM((2, W, 3 * C), BF16),
            pltpu.VMEM((2, 2, 2 * W, 128), F32),
            pltpu.VMEM((2, OUT, 2 * W), BF16),
            pltpu.SemaphoreType.DMA((2,)),
        ],
        specs=[VM, VM, VM, VM, ANY],
        out_spec=ANY,
        aliases={4: 0},
    )
    return result.transpose(0, 2, 1)[None]


def solution(mesh):
    return jax.shard_map(
        on_device,
        mesh=mesh,
        in_specs=(P("tm", "rows", None, None), P(), P(), P(), P(), P(), P(), P(), P(), P(), P()),
        out_specs=P("tm", "rows", None, None),
        check_vma=False,
    )
```

```python
import functools
import math

import jax
import jax.numpy as jnp
from jax import lax
from jax.experimental import pallas as pl
from jax.experimental.pallas import tpu as pltpu
from jax.sharding import PartitionSpec as P

F32 = jnp.float32
BF16 = jnp.bfloat16
ROWS = 3
W = 128
C = 384
OUT = 192
CELLS = ROWS * W
XN, ZN, TN = 4, 8, 8
QALL = XN * CELLS
HALF = C // 2
STAT = 16
LOG2E = math.log2(math.e)


def dot(a, b, dims):
    return lax.dot_general(a, b, (dims, ((), ())), preferred_element_type=F32)


def params(mib=32):
    return pltpu.CompilerParams(vmem_limit_bytes=mib * 2**20)


def cost(flops, bytes_accessed):
    return pl.CostEstimate(flops=int(flops), bytes_accessed=int(bytes_accessed), transcendentals=0)


VM = pl.BlockSpec(memory_space=pltpu.VMEM)
SMEM = pl.BlockSpec(memory_space=pltpu.SMEM)
ANY = pl.BlockSpec(memory_space=pl.ANY)
HBM = pl.BlockSpec(memory_space=pltpu.HBM)


def call(body, outs, *args, name, flops=1e6, nbytes=1e6, aliases=None, scratch=(), mib=32, specs=None, out_spec=VM):
    shapes = [jax.ShapeDtypeStruct(shape, dtype) for shape, dtype in outs]
    result = pl.pallas_call(
        body,
        in_specs=specs or [VM] * len(args),
        out_specs=[out_spec] * len(shapes),
        out_shape=shapes,
        input_output_aliases=aliases or {},
        scratch_shapes=list(scratch),
        compiler_params=params(mib),
        cost_estimate=cost(flops, nbytes),
        name=name,
    )(*args)
    return result[0] if len(shapes) == 1 else result


def col_variants(y, store):
    column = lax.broadcasted_iota(jnp.int32, y.shape, 0)
    before = jnp.where(column == 0, 0.0, pltpu.roll(y, 1, 0))
    after = jnp.where(column == W - 1, 0.0, pltpu.roll(y, W - 1, 0))
    store(0, before.astype(BF16))
    store(1, y.astype(BF16))
    store(2, after.astype(BF16))


def activate(row, gain):
    x = row.astype(F32)
    y = x * lax.rsqrt(jnp.mean(x * x, -1, keepdims=True) + 1e-6) * gain
    y = y / (1.0 + jnp.exp(-y))
    return y.astype(BF16).astype(F32)


def inside(place):
    frame, band = place[0], place[1]
    return frame >= 2, frame >= 1, band >= 1, band < XN * ZN - 1


def fill_rows(scratch, rows, gain, present=None):
    for index, row in enumerate(rows):
        y = activate(row, gain)
        if present is not None:
            y = jnp.where(present[index], y, 0.0)

        def store(variant, value, index=index):
            scratch[index, :, variant * C : (variant + 1) * C] = value

        col_variants(y, store)


def conv_band_kernel(first, time_tap, place, frame, small, weight, *refs):
    start = None if first else refs[0]
    acc, beside, scratch, middle, sem = refs[-5:]
    copies = [
        pltpu.make_async_copy(weight.at[time_tap, b], target, sem.at[b])
        for b, target in enumerate((beside.at[0], middle, beside.at[1]))
    ]
    for b in (1, 0, 2):
        copies[b].start()
    present = None if first else [inside(place)[time_tap]] * ROWS
    fill_rows(scratch, [frame[i] for i in range(ROWS)], small[0:1, :C], present)
    band = scratch[...].reshape(CELLS, 3 * C)
    copies[1].wait()
    total = dot(band, middle[...].reshape(3 * C, C), ((1,), (0,)))
    if not first:
        total += start[...]
    copies[0].wait()
    down = dot(band[: 2 * W], beside[0].reshape(3 * C, C), ((1,), (0,)))
    copies[2].wait()
    up = dot(band[W:], beside[1].reshape(3 * C, C), ((1,), (0,)))
    acc[:W] = total[:W] + up[:W]
    acc[W : 2 * W] = total[W : 2 * W] + down[:W] + up[W:]
    acc[2 * W :] = total[2 * W :] + down[W:]


def conv_band(place, frame, small, weight, time_tap, start=None):
    first = start is None
    return call(
        functools.partial(conv_band_kernel, first, time_tap),
        [((CELLS, C), F32), ((2, 3, C, C), BF16)],
        place,
        frame,
        small,
        weight,
        *(() if first else (start,)),
        name="conv_band",
        flops=2 * CELLS * 9 * C * C,
        scratch=[
            pltpu.VMEM((ROWS, W, 3 * C), BF16),
            pltpu.VMEM((3, C, C), BF16),
            pltpu.SemaphoreType.DMA((3,)),
        ],
        specs=[SMEM, VM, VM, HBM] + ([] if first else [VM]),
        aliases=None if first else {4: 0},
        mib=49,
    )


def edge_taps(scratch, low, high, weight):
    left = dot(scratch[low], weight[0].reshape(3 * C, C), ((1,), (0,)))
    right = dot(scratch[high], weight[1].reshape(3 * C, C), ((1,), (0,)))
    return left, right


def conv_edges_kernel(place, low, high, small, w_own, w_two, start, acc, scratch):
    two, _, above, below = inside(place)
    present = [above, above & two, below, below & two]
    fill_rows(scratch, [low[0], low[1], high[0], high[1]], small[0:1, :C], present)
    own = edge_taps(scratch, 0, 2, w_own)
    two = edge_taps(scratch, 1, 3, w_two)
    acc[...] = start[...]
    acc[:W] += own[0] + two[0]
    acc[2 * W :] += own[1] + two[1]


def conv_last_kernel(place, edges, own, small, weight, start, block, normed, scratch):
    _, one, above, below = inside(place)
    fill_rows(scratch, [edges[0], edges[1]], small[0:1, :C], [above & one, below & one])
    sides = edge_taps(scratch, 0, 1, weight)
    bias, gain2 = small[1:2, :C], small[2:3, :C]
    for i in range(ROWS):
        rows = slice(i * W, (i + 1) * W)
        total = start[rows] + bias
        if i != 1:
            total += sides[i // 2]
        x = (own[i].astype(F32) + total.astype(BF16).astype(F32)).astype(BF16)
        block[rows] = x
        x = x.astype(F32)
        x = x * lax.rsqrt(jnp.mean(x * x, -1, keepdims=True) + 1e-6) * gain2
        normed[rows] = x.astype(BF16)


def edge_payload_kernel(place, own, two, _acc, to_next, to_previous, pair):
    to_next[0] = own[ROWS - 1]
    to_next[1] = two[ROWS - 1]
    to_previous[0] = own[0]
    to_previous[1] = two[0]

    odd = lax.rem(place[0], 2)

    @pl.when(odd == 0)
    def _():
        pair[...] = own[...]

    @pl.when(odd == 1)
    def _():
        pair[...] = two[...]


def pair_edges_kernel(place, low, high, _acc, out):
    index = lax.rem(place[0], 2)
    out[0] = low[index]
    out[1] = high[index]


def query_kernel(normed, weight, small, out, shift):
    scale = C**-0.5 * LOG2E
    wq, wk = weight[:, :C], weight[:, C : 2 * C]
    q = (dot(normed[...], wq, ((1,), (0,))) + small[4:5, :C]).astype(BF16)
    out[...] = (dot(wk, q, ((1,), (1,))) * scale).astype(BF16)
    bk = jnp.broadcast_to(small[4:5, C : 2 * C], (8, C))
    shift[...] = dot(bk, q.astype(F32), ((1,), (1,)))[:1] * scale


def spans(refs, low, high):
    at = 0
    for ref in refs:
        n = ref.shape[1]
        first, last = max(low, at), min(high, at + n)
        if first < last:
            yield ref, first - at, last - at, first - low, last - low
        at += n


def read(refs, low, high):
    pieces = [ref[:, a:b] for ref, a, b, _, _ in spans(refs, low, high)]
    return pieces[0] if len(pieces) == 1 else jnp.concatenate(pieces, 1)


def write(refs, low, high, value):
    for ref, a, b, first, last in spans(refs, low, high):
        ref[:, a:b] = value[:, first:last]


def joined(refs):
    return refs[0][...] if len(refs) == 1 else jnp.concatenate([r[...] for r in refs], 0)


def softmax_tiles(keys, tiles, q_of, old_of, give):
    keys_t = keys.T

    def scores(tile):
        return dot(keys, q_of(*tile), ((1,), (0,)))

    following = scores(tiles[0])
    for i, tile in enumerate(tiles):
        s = following
        if i + 1 < len(tiles):
            following = scores(tiles[i + 1])
        old = old_of(*tile)
        m = jnp.max(s, 0, keepdims=True)
        if old is not None:
            m = jnp.maximum(m, old[0])
        p = jnp.exp2(s - m)
        total = jnp.sum(p, 0, keepdims=True)
        acc = dot(keys_t, p.astype(BF16), ((1,), (0,)))
        if old is not None:
            alpha = jnp.exp2(old[0] - m)
            total = total + alpha * old[1]
            acc = acc + alpha * old[2]
        give(*tile, (m, total, acc))


def tiles_of(low, high, size=512):
    return [(at, min(at + size, high)) for at in range(low, high, size)]


def attention_kernel(n_keys, n_q, n_state, n_out, low, high, *refs):
    keys = joined(refs[:n_keys])
    queries = refs[n_keys : n_keys + n_q]
    state = refs[n_keys + n_q : n_keys + n_q + 3 * n_state]
    outs = refs[n_keys + n_q + 3 * n_state :]

    def old_of(a, b):
        return [read(state[i::3], a, b) for i in range(3)] if n_state else None

    def give(a, b, values):
        for i, value in enumerate(values):
            write(outs[i::3], a - low, b - low, value)

    softmax_tiles(keys, tiles_of(low, high), lambda a, b: read(queries, a, b), old_of, give)


def attention_step(keys, queries, state=(), low=0, high=None):
    widths = [q.shape[1] for q in queries]
    high = sum(widths) if high is None else high
    rows = sum(k.shape[0] for k in keys)
    whole_state = bool(state) and high - low == sum(s[0].shape[1] for s in state)
    outs = [s[0].shape[1] for s in state] if whole_state else [high - low]
    flat = [v for s in state for v in s]
    before = len(keys) + len(queries)
    result = call(
        functools.partial(
            attention_kernel, len(keys), len(queries), len(state), len(outs), low, high
        ),
        [shape for n in outs for shape in (((1, n), F32), ((1, n), F32), ((C, n), F32))],
        *keys,
        *queries,
        *flat,
        name="attention_step",
        flops=4 * rows * (high - low) * C,
        nbytes=6e6,
        aliases={before + i: i for i in range(len(flat))} if whole_state else None,
    )
    return [tuple(result[i : i + 3]) for i in range(0, len(result), 3)]


def gate_kernel(*refs):
    pass


def after(values, *done):
    count = len(values)
    return call(
        gate_kernel,
        [(v.shape, v.dtype) for v in values],
        *values,
        *done,
        name="gate",
        flops=1,
        nbytes=1,
        specs=[ANY] * (count + len(done)),
        out_spec=ANY,
        aliases={i: i for i in range(count)},
    )


def split3(x):
    hi = x.astype(BF16)
    rest = x - hi.astype(F32)
    mid = rest.astype(BF16)
    low = (rest - mid.astype(F32)).astype(BF16)
    return hi, mid, low


def stat_rows(parts):
    n = parts[0].shape[1]
    row = lax.broadcasted_iota(jnp.int32, (STAT, n), 0)
    block = jnp.zeros((STAT, n), F32)
    for i, part in enumerate(parts):
        for j, piece in enumerate(split3(part)):
            block = jnp.where(row == 3 * i + j, piece.astype(F32), block)
    return block.astype(BF16)


def stat_of(block, i):
    b = block.astype(F32)
    return b[3 * i : 3 * i + 1] + b[3 * i + 1 : 3 * i + 2] + b[3 * i + 2 : 3 * i + 3]


def opposite_kernel(n_keys, *refs):
    q, m_old, l_old, acc_old, top, bottom = refs[n_keys:]

    def give(_a, _b, values):
        m, total, acc = values
        out = (acc / total).astype(BF16)
        stats = stat_rows([m + jnp.log2(total)])
        top[:HALF] = out[:HALF]
        top[HALF:] = stats
        bottom[:HALF] = out[HALF:]
        bottom[HALF:] = stats

    old = lambda a, b: (m_old[...], l_old[...], acc_old[...])
    softmax_tiles(joined(refs[:n_keys]), [(0, CELLS)], lambda a, b: q[...], old, give)


def opposite(keys, q_far, state):
    rows = sum(k.shape[0] for k in keys)
    return call(
        functools.partial(opposite_kernel, len(keys)),
        [((HALF + STAT, CELLS), BF16)] * 2,
        *keys,
        q_far,
        *state,
        name="opposite",
        flops=4 * rows * CELLS * C,
        nbytes=2e6,
    )


def merge(parts):
    top = functools.reduce(jnp.maximum, [s for s, _ in parts])
    w = [jnp.exp2(s - top) for s, _ in parts]
    total = functools.reduce(jnp.add, w)
    inverse = 1.0 / total
    out = functools.reduce(jnp.add, [(a * inverse) * o for a, (_, o) in zip(w, parts)])
    return top + jnp.log2(total), out


def relay_kernel(from_low, from_high, m, total, acc, to_low, to_high):
    for side, got, out in ((0, from_high, to_low), (1, from_low, to_high)):
        cols = slice(side * CELLS, (side + 1) * CELLS)
        stat = m[:, cols] + jnp.log2(total[:, cols])
        mine = acc[:, cols] / total[:, cols]
        theirs = (stat_of(got[HALF:], 0), got[:HALF].astype(F32))
        if side == 0:
            stat_t, half_t = stat, mine[:HALF]
            stat_b, half_b = merge([(stat, mine[HALF:]), theirs])
        else:
            stat_t, half_t = merge([(stat, mine[:HALF]), theirs])
            stat_b, half_b = stat, mine[HALF:]
        out[:HALF] = half_t.astype(BF16)
        out[HALF:C] = half_b.astype(BF16)
        out[C:] = stat_rows([stat_t, stat_b])


def finish_kernel(from_low, from_high, m, total, acc, shift, weight, wp, small, block, out):
    c = shift[...]
    stat = m[...] + jnp.log2(total[...]) + c
    mine = acc[...] / total[...]
    halves = []
    for i in range(2):
        rows = slice(i * HALF, (i + 1) * HALF)
        parts = [(stat, mine[rows])] + [
            (stat_of(got[C:], i) + c, got[rows].astype(F32)) for got in (from_low, from_high)
        ]
        halves.append(merge(parts)[1])
    mixed_in = jnp.concatenate(halves, 0).astype(BF16)
    mixed = (dot(mixed_in, weight[:, 2 * C :], ((0,), (0,))) + small[4:5, 2 * C :]).astype(BF16)
    attended = dot(mixed, wp[...], ((1,), (0,))) + small[3:4, :C] + block[...].astype(F32)
    out[...] = attended.astype(BF16)


def pack_kernel(flat, small):
    small[...] = jnp.zeros_like(small)
    at = 0
    for i, n in enumerate((C, C, C, C, 3 * C, OUT)):
        small[i, :n] = flat[at : at + n]
        at += n


def up_phases_kernel(weight, out):
    w = [[weight[b, c].astype(F32) for c in range(3)] for b in range(3)]

    def pairs(a, b, c):
        return ((a, b + c), (a + b, c))

    by_row = [pairs(*(w[b][c] for b in range(3))) for c in range(3)]
    for di in range(2):
        for rt in range(2):
            by_column = pairs(*(by_row[c][di][rt] for c in range(3)))
            for dj in range(2):
                for ct in range(2):
                    value = jnp.concatenate(
                        [by_column[dj][ct], jnp.zeros((256 - OUT, C), F32)], 0
                    )
                    out[di, dj, rt, ct * C : (ct + 1) * C] = value.T.astype(BF16)


def fill_plain(scratch, index, row):
    def store(variant, value):
        scratch[index, :, variant * C : (variant + 1) * C] = value

    col_variants(row.astype(F32), store)


def store_phase(wide, row, dj, value):
    for part in range(2):
        wide[part, row, pl.ds(dj, W, stride=2), :] = value[:, part * 128 : (part + 1) * 128]


def read_row(wide, row):
    return jnp.concatenate([wide[0, row].T, wide[1, row].T[: OUT - 128]], 0)


def up_inner_kernel(body, weight, small, out, edge, scratch, wide):
    for i in range(ROWS):
        fill_plain(scratch, i, body[i])
    b = small[5:6, :256]
    for di in range(2):
        for dj in range(2):
            full = scratch[:, :, dj * C : (dj + 2) * C].reshape(CELLS, 2 * C)
            if di == 0:
                here = dot(full, weight[0, dj, 1], ((1,), (0,))) + b
                beside = dot(full[: 2 * W], weight[0, dj, 0], ((1,), (0,)))
                parts = [here[:W], here[W : 2 * W] + beside[:W], here[2 * W :] + beside[W:]]
            else:
                here = dot(full, weight[1, dj, 0], ((1,), (0,))) + b
                beside = dot(full[W:], weight[1, dj, 1], ((1,), (0,)))
                parts = [here[:W] + beside[:W], here[W : 2 * W] + beside[W:], here[2 * W :]]
            for i, part in enumerate(parts):
                store_phase(wide, 2 * i + di, dj, part)
    for row in range(1, 2 * ROWS - 1):
        out[row] = read_row(wide, row).astype(BF16)
    edge[0] = read_row(wide, 0)
    edge[1] = read_row(wide, 2 * ROWS - 1)


def up_edges_kernel(place, low, high, weight, edge, _start, out, scratch, wide, rows, sem):
    _, _, above, below = inside(place)
    for i, (ref, present) in enumerate(((low, above), (high, below))):
        row = ref[0]
        fill_plain(scratch, i, jnp.where(present, row, jnp.zeros_like(row)))
    copies = []
    for side in range(2):
        for dj in range(2):
            left = scratch[side, :, dj * C : (dj + 2) * C]
            store_phase(wide, side, dj, dot(left, weight[side, dj, side], ((1,), (0,))))
        rows[side] = (edge[side] + read_row(wide, side)).astype(BF16)
        row = out.at[side * (2 * ROWS - 1)]
        copies.append(pltpu.make_async_copy(rows.at[side], row, sem.at[side]))
        copies[side].start()
    for copy in copies:
        copy.wait()


def permute_z(value, by):
    pairs = [(x * ZN + z, x * ZN + (z + by) % ZN) for x in range(XN) for z in range(ZN)]
    return lax.ppermute(value, "rows", pairs)


def permute_x(value, by):
    pairs = [(x * ZN + z, (x + by) % XN * ZN + z) for x in range(XN) for z in range(ZN)]
    return lax.ppermute(value, "rows", pairs)


def to_bands(value, by):
    n = XN * ZN
    return lax.ppermute(value, "rows", [(i, (i + by) % n) for i in range(n)])


def on_device(
    latent,
    norm1_gain,
    conv1_weight,
    conv1_bias,
    attention_gain,
    qkv_weight,
    qkv_bias,
    proj_weight,
    proj_bias,
    up_weight,
    up_bias,
):
    own = latent[0]
    first = lax.iota(jnp.int32, 2) == 0
    place = jnp.where(first, lax.axis_index("tm"), lax.axis_index("rows"))
    two = lax.ppermute(own, "tm", [(t, (t + 2) % TN) for t in range(TN)])
    flat = (norm1_gain, conv1_bias, attention_gain, proj_bias, qkv_bias, up_bias)
    ends = [sum(v.shape[0] for v in flat[: i + 1]) for i in range(len(flat))]
    joined_flat = functools.reduce(
        jnp.add,
        [jnp.pad(v, (end - v.shape[0], ends[-1] - end)) for v, end in zip(flat, ends)],
    )
    small = call(pack_kernel, [((8, 3 * C), F32)], joined_flat, name="pack")
    acc, w_own = conv_band(place, own, small, conv1_weight, 2)
    pairs = [(t, t ^ 1) for t in range(TN)]
    to_next, to_previous, pair = call(
        edge_payload_kernel,
        [((2, W, C), BF16)] * 2 + [((ROWS, W, C), BF16)],
        place,
        own,
        two,
        acc,
        name="edge_payload",
        specs=[SMEM, VM, VM, ANY],
    )
    low, high = to_bands(to_next, 1), to_bands(to_previous, -1)
    one = lax.ppermute(pair, "tm", pairs)
    acc, w_two = conv_band(place, two, small, conv1_weight, 0, acc)
    acc, w_one = conv_band(place, one, small, conv1_weight, 1, acc)
    pair_edges = call(
        pair_edges_kernel,
        [((2, W, C), BF16)],
        place,
        low,
        high,
        acc,
        name="pair_edges",
        specs=[SMEM, VM, VM, ANY],
    )
    one_edges = lax.ppermute(pair_edges, "tm", pairs)
    acc = call(
        conv_edges_kernel,
        [((CELLS, C), F32)],
        place,
        low,
        high,
        small,
        w_own,
        w_two,
        acc,
        name="conv_edges",
        flops=2 * CELLS * 2 * C * C,
        scratch=[pltpu.VMEM((4, W, 3 * C), BF16)],
        specs=[SMEM] + [VM] * 6,
        aliases={6: 0},
    )
    block, normed = call(
        conv_last_kernel,
        [((CELLS, C), BF16)] * 2,
        place,
        one_edges,
        own,
        small,
        w_one,
        acc,
        name="conv_last",
        flops=2 * CELLS * C * C,
        scratch=[pltpu.VMEM((2, W, 3 * C), BF16)],
        specs=[SMEM] + [VM] * 5,
    )

    up, down = permute_z(normed, 1), permute_z(normed, -1)
    query, shift = call(
        query_kernel,
        [((C, CELLS), BF16), ((1, CELLS), F32)],
        normed,
        qkv_weight,
        small,
        name="queries",
        flops=4 * CELLS * C * C,
    )
    q_low, q_high = permute_x(query, 1), permute_x(query, -1)
    q_far = permute_x(query, 2)
    up2, down2 = permute_z(up, 1), permute_z(down, -1)
    early = [normed, up, down]
    near = [q_low, q_high, query]
    (state,) = attention_step(early, near)
    phases = call(
        up_phases_kernel,
        [((2, 2, 2, 2 * C, 256), BF16)],
        up_weight.transpose(0, 1, 3, 2),
        name="up_phases",
        flops=1e7,
        nbytes=4e6,
    )
    up2, down2 = after((up2, down2), state[0], phases)
    up3, down3 = permute_z(up2, 1), permute_z(down2, -1)
    (far,) = attention_step(early, [q_far])
    queries = near + [q_far]
    state, far = attention_step([up2, down2], queries, (state, far))
    up4, down4 = permute_z(up3[: CELLS // 2], 1), permute_z(down3[CELLS // 2 :], -1)
    state, far = attention_step([up3, down3], queries, (state, far))
    last = [up4, down4]
    pay_t, pay_b = opposite(last, q_far, far)
    half_low, half_high = permute_x(pay_t, 1), permute_x(pay_b, -1)
    (sides,) = attention_step(last, near, (state,), 0, 2 * CELLS)
    to_low, to_high = call(
        relay_kernel,
        [((C + STAT, CELLS), BF16)] * 2,
        half_low,
        half_high,
        *sides,
        name="relay",
    )
    from_low, from_high = permute_x(to_high, 1), permute_x(to_low, -1)
    (mine,) = attention_step(last, near, (state,), 2 * CELLS, 3 * CELLS)
    attended = call(
        finish_kernel,
        [((CELLS, C), BF16)],
        from_low,
        from_high,
        *mine,
        shift,
        qkv_weight,
        proj_weight,
        small,
        block,
        name="finish",
        flops=4 * CELLS * C * C,
    ).reshape(ROWS, W, C)
    edge_low, edge_high = to_bands(attended[2:], 1), to_bands(attended[:1], -1)
    inner, edge = call(
        up_inner_kernel,
        [((2 * ROWS, OUT, 2 * W), BF16), ((2, OUT, 2 * W), F32)],
        attended,
        phases,
        small,
        name="up_inner",
        flops=2 * CELLS * 14 * C * OUT,
        scratch=[
            pltpu.VMEM((ROWS, W, 3 * C), BF16),
            pltpu.VMEM((2, 2 * ROWS, 2 * W, 128), F32),
        ],
    )
    result = call(
        up_edges_kernel,
        [((2 * ROWS, OUT, 2 * W), BF16)],
        place,
        edge_low,
        edge_high,
        phases,
        edge,
        inner,
        name="up_edges",
        flops=2 * CELLS * 2 * C * OUT,
        scratch=[
            pltpu.VMEM((2, W, 3 * C), BF16),
            pltpu.VMEM((2, 2, 2 * W, 128), F32),
            pltpu.VMEM((2, OUT, 2 * W), BF16),
            pltpu.SemaphoreType.DMA((2,)),
        ],
        specs=[SMEM, VM, VM, VM, VM, ANY],
        out_spec=ANY,
        aliases={5: 0},
    )
    return result.transpose(0, 2, 1)[None]


def solution(mesh):
    return jax.shard_map(
        on_device,
        mesh=mesh,
        in_specs=(P("tm", "rows", None, None), P(), P(), P(), P(), P(), P(), P(), P(), P(), P()),
        out_specs=P("tm", "rows", None, None),
        check_vma=False,
    )
```

```python
import functools
import math

import jax
import jax.numpy as jnp
from jax import lax
from jax.experimental import pallas as pl
from jax.experimental.pallas import tpu as pltpu
from jax.sharding import PartitionSpec as P

F32 = jnp.float32
BF16 = jnp.bfloat16
ROWS = 3
W = 128
C = 384
OUT = 192
CELLS = ROWS * W
XN, ZN, TN = 4, 8, 8
QALL = XN * CELLS
HALF = C // 2
STAT = 16
LOG2E = math.log2(math.e)


def dot(a, b, dims):
    return lax.dot_general(a, b, (dims, ((), ())), preferred_element_type=F32)


def params(mib=32):
    return pltpu.CompilerParams(vmem_limit_bytes=mib * 2**20)


def cost(flops, bytes_accessed):
    return pl.CostEstimate(flops=int(flops), bytes_accessed=int(bytes_accessed), transcendentals=0)


VM = pl.BlockSpec(memory_space=pltpu.VMEM)
ANY = pl.BlockSpec(memory_space=pl.ANY)
HBM = pl.BlockSpec(memory_space=pltpu.HBM)


def call(body, outs, *args, name, flops=1e6, nbytes=1e6, aliases=None, scratch=(), mib=32, specs=None, out_spec=VM):
    shapes = [jax.ShapeDtypeStruct(shape, dtype) for shape, dtype in outs]
    result = pl.pallas_call(
        body,
        in_specs=specs or [VM] * len(args),
        out_specs=[out_spec] * len(shapes),
        out_shape=shapes,
        input_output_aliases=aliases or {},
        scratch_shapes=list(scratch),
        compiler_params=params(mib),
        cost_estimate=cost(flops, nbytes),
        name=name,
    )(*args)
    return result[0] if len(shapes) == 1 else result


def col_variants(y, store):
    column = lax.broadcasted_iota(jnp.int32, y.shape, 0)
    before = jnp.where(column == 0, 0.0, pltpu.roll(y, 1, 0))
    after = jnp.where(column == W - 1, 0.0, pltpu.roll(y, W - 1, 0))
    store(0, before.astype(BF16))
    store(1, y.astype(BF16))
    store(2, after.astype(BF16))


def activate(row, gain):
    x = row.astype(F32)
    y = x * lax.rsqrt(jnp.mean(x * x, -1, keepdims=True) + 1e-6) * gain
    y = y / (1.0 + jnp.exp(-y))
    return y.astype(BF16).astype(F32)


def inside():
    frame, band = lax.axis_index("tm"), lax.axis_index("rows")
    return frame >= 2, frame >= 1, band >= 1, band < XN * ZN - 1


def fill_rows(scratch, rows, gain, present=None):
    for index, row in enumerate(rows):
        y = activate(row, gain)
        if present is not None:
            y = jnp.where(present[index], y, 0.0)

        def store(variant, value, index=index):
            scratch[index, :, variant * C : (variant + 1) * C] = value

        col_variants(y, store)


def conv_band_kernel(first, time_tap, frame, small, weight, *refs):
    start = None if first else refs[0]
    acc, beside, scratch, middle, sem = refs[-5:]
    copies = [
        pltpu.make_async_copy(weight.at[time_tap, b], target, sem.at[b])
        for b, target in enumerate((beside.at[0], middle, beside.at[1]))
    ]
    for b in (1, 0, 2):
        copies[b].start()
    present = None if first else [inside()[time_tap]] * ROWS
    fill_rows(scratch, [frame[i] for i in range(ROWS)], small[0:1, :C], present)
    band = scratch[...].reshape(CELLS, 3 * C)
    copies[1].wait()
    total = dot(band, middle[...].reshape(3 * C, C), ((1,), (0,)))
    if not first:
        total += start[...]
    copies[0].wait()
    down = dot(band[: 2 * W], beside[0].reshape(3 * C, C), ((1,), (0,)))
    copies[2].wait()
    up = dot(band[W:], beside[1].reshape(3 * C, C), ((1,), (0,)))
    acc[:W] = total[:W] + up[:W]
    acc[W : 2 * W] = total[W : 2 * W] + down[:W] + up[W:]
    acc[2 * W :] = total[2 * W :] + down[W:]


def conv_band(frame, small, weight, time_tap, start=None):
    first = start is None
    return call(
        functools.partial(conv_band_kernel, first, time_tap),
        [((CELLS, C), F32), ((2, 3, C, C), BF16)],
        frame,
        small,
        weight,
        *(() if first else (start,)),
        name="conv_band",
        flops=2 * CELLS * 9 * C * C,
        scratch=[
            pltpu.VMEM((ROWS, W, 3 * C), BF16),
            pltpu.VMEM((3, C, C), BF16),
            pltpu.SemaphoreType.DMA((3,)),
        ],
        specs=[VM, VM, HBM] + ([] if first else [VM]),
        aliases=None if first else {3: 0},
        mib=49,
    )


def edge_taps(scratch, low, high, weight):
    left = dot(scratch[low], weight[0].reshape(3 * C, C), ((1,), (0,)))
    right = dot(scratch[high], weight[1].reshape(3 * C, C), ((1,), (0,)))
    return left, right


def conv_edges_kernel(low, high, small, w_own, w_two, start, acc, scratch):
    two, _, above, below = inside()
    present = [above, above & two, below, below & two]
    fill_rows(scratch, [low[0], low[1], high[0], high[1]], small[0:1, :C], present)
    own = edge_taps(scratch, 0, 2, w_own)
    two = edge_taps(scratch, 1, 3, w_two)
    acc[...] = start[...]
    acc[:W] += own[0] + two[0]
    acc[2 * W :] += own[1] + two[1]


def conv_last_kernel(edges, own, small, weight, start, block, normed, scratch):
    _, one, above, below = inside()
    fill_rows(scratch, [edges[0], edges[1]], small[0:1, :C], [above & one, below & one])
    sides = edge_taps(scratch, 0, 1, weight)
    bias, gain2 = small[1:2, :C], small[2:3, :C]
    for i in range(ROWS):
        rows = slice(i * W, (i + 1) * W)
        total = start[rows] + bias
        if i != 1:
            total += sides[i // 2]
        x = (own[i].astype(F32) + total.astype(BF16).astype(F32)).astype(BF16)
        block[rows] = x
        x = x.astype(F32)
        x = x * lax.rsqrt(jnp.mean(x * x, -1, keepdims=True) + 1e-6) * gain2
        normed[rows] = x.astype(BF16)


def edge_payload_kernel(own, two, _acc, to_next, to_previous, pair):
    to_next[0] = own[ROWS - 1]
    to_next[1] = two[ROWS - 1]
    to_previous[0] = own[0]
    to_previous[1] = two[0]

    odd = lax.rem(lax.axis_index("tm"), 2)

    @pl.when(odd == 0)
    def _():
        pair[...] = own[...]

    @pl.when(odd == 1)
    def _():
        pair[...] = two[...]


def pair_edges_kernel(low, high, _acc, out):
    index = lax.rem(lax.axis_index("tm"), 2)
    out[0] = low[index]
    out[1] = high[index]


def query_kernel(normed, weight, small, out, shift):
    scale = C**-0.5 * LOG2E
    wq, wk = weight[:, :C], weight[:, C : 2 * C]
    q = (dot(normed[...], wq, ((1,), (0,))) + small[4:5, :C]).astype(BF16)
    out[...] = (dot(wk, q, ((1,), (1,))) * scale).astype(BF16)
    bk = jnp.broadcast_to(small[4:5, C : 2 * C], (8, C))
    shift[...] = dot(bk, q.astype(F32), ((1,), (1,)))[:1] * scale


def spans(refs, low, high):
    at = 0
    for ref in refs:
        n = ref.shape[1]
        first, last = max(low, at), min(high, at + n)
        if first < last:
            yield ref, first - at, last - at, first - low, last - low
        at += n


def read(refs, low, high):
    pieces = [ref[:, a:b] for ref, a, b, _, _ in spans(refs, low, high)]
    return pieces[0] if len(pieces) == 1 else jnp.concatenate(pieces, 1)


def write(refs, low, high, value):
    for ref, a, b, first, last in spans(refs, low, high):
        ref[:, a:b] = value[:, first:last]


def joined(refs):
    return refs[0][...] if len(refs) == 1 else jnp.concatenate([r[...] for r in refs], 0)


def softmax_tiles(keys, tiles, q_of, old_of, give):
    keys_t = keys.T

    def scores(tile):
        return dot(keys, q_of(*tile), ((1,), (0,)))

    following = scores(tiles[0])
    for i, tile in enumerate(tiles):
        s = following
        if i + 1 < len(tiles):
            following = scores(tiles[i + 1])
        old = old_of(*tile)
        m = jnp.max(s, 0, keepdims=True)
        if old is not None:
            m = jnp.maximum(m, old[0])
        p = jnp.exp2(s - m)
        total = jnp.sum(p, 0, keepdims=True)
        acc = dot(keys_t, p.astype(BF16), ((1,), (0,)))
        if old is not None:
            alpha = jnp.exp2(old[0] - m)
            total = total + alpha * old[1]
            acc = acc + alpha * old[2]
        give(*tile, (m, total, acc))


def tiles_of(low, high, size=512):
    return [(at, min(at + size, high)) for at in range(low, high, size)]


def attention_kernel(n_keys, n_q, n_state, n_out, low, high, *refs):
    keys = joined(refs[:n_keys])
    queries = refs[n_keys : n_keys + n_q]
    state = refs[n_keys + n_q : n_keys + n_q + 3 * n_state]
    outs = refs[n_keys + n_q + 3 * n_state :]

    def old_of(a, b):
        return [read(state[i::3], a, b) for i in range(3)] if n_state else None

    def give(a, b, values):
        for i, value in enumerate(values):
            write(outs[i::3], a - low, b - low, value)

    softmax_tiles(keys, tiles_of(low, high), lambda a, b: read(queries, a, b), old_of, give)


def attention_step(keys, queries, state=(), low=0, high=None):
    widths = [q.shape[1] for q in queries]
    high = sum(widths) if high is None else high
    rows = sum(k.shape[0] for k in keys)
    whole_state = bool(state) and high - low == sum(s[0].shape[1] for s in state)
    outs = [s[0].shape[1] for s in state] if whole_state else [high - low]
    flat = [v for s in state for v in s]
    before = len(keys) + len(queries)
    result = call(
        functools.partial(
            attention_kernel, len(keys), len(queries), len(state), len(outs), low, high
        ),
        [shape for n in outs for shape in (((1, n), F32), ((1, n), F32), ((C, n), F32))],
        *keys,
        *queries,
        *flat,
        name="attention_step",
        flops=4 * rows * (high - low) * C,
        nbytes=6e6,
        aliases={before + i: i for i in range(len(flat))} if whole_state else None,
    )
    return [tuple(result[i : i + 3]) for i in range(0, len(result), 3)]


def gate_kernel(*refs):
    pass


def after(values, *done):
    count = len(values)
    return call(
        gate_kernel,
        [(v.shape, v.dtype) for v in values],
        *values,
        *done,
        name="gate",
        flops=1,
        nbytes=1,
        specs=[ANY] * (count + len(done)),
        out_spec=ANY,
        aliases={i: i for i in range(count)},
    )


def split3(x):
    hi = x.astype(BF16)
    rest = x - hi.astype(F32)
    mid = rest.astype(BF16)
    low = (rest - mid.astype(F32)).astype(BF16)
    return hi, mid, low


def stat_rows(parts):
    n = parts[0].shape[1]
    row = lax.broadcasted_iota(jnp.int32, (STAT, n), 0)
    block = jnp.zeros((STAT, n), F32)
    for i, part in enumerate(parts):
        for j, piece in enumerate(split3(part)):
            block = jnp.where(row == 3 * i + j, piece.astype(F32), block)
    return block.astype(BF16)


def stat_of(block, i):
    b = block.astype(F32)
    return b[3 * i : 3 * i + 1] + b[3 * i + 1 : 3 * i + 2] + b[3 * i + 2 : 3 * i + 3]


def opposite_kernel(n_keys, *refs):
    q, m_old, l_old, acc_old, top, bottom = refs[n_keys:]

    def give(_a, _b, values):
        m, total, acc = values
        out = (acc / total).astype(BF16)
        stats = stat_rows([m + jnp.log2(total)])
        top[:HALF] = out[:HALF]
        top[HALF:] = stats
        bottom[:HALF] = out[HALF:]
        bottom[HALF:] = stats

    old = lambda a, b: (m_old[...], l_old[...], acc_old[...])
    softmax_tiles(joined(refs[:n_keys]), [(0, CELLS)], lambda a, b: q[...], old, give)


def opposite(keys, q_far, state):
    rows = sum(k.shape[0] for k in keys)
    return call(
        functools.partial(opposite_kernel, len(keys)),
        [((HALF + STAT, CELLS), BF16)] * 2,
        *keys,
        q_far,
        *state,
        name="opposite",
        flops=4 * rows * CELLS * C,
        nbytes=2e6,
    )


def merge(parts):
    top = functools.reduce(jnp.maximum, [s for s, _ in parts])
    w = [jnp.exp2(s - top) for s, _ in parts]
    total = functools.reduce(jnp.add, w)
    inverse = 1.0 / total
    out = functools.reduce(jnp.add, [(a * inverse) * o for a, (_, o) in zip(w, parts)])
    return top + jnp.log2(total), out


def relay_kernel(from_low, from_high, m, total, acc, to_low, to_high):
    for side, got, out in ((0, from_high, to_low), (1, from_low, to_high)):
        cols = slice(side * CELLS, (side + 1) * CELLS)
        stat = m[:, cols] + jnp.log2(total[:, cols])
        mine = acc[:, cols] / total[:, cols]
        theirs = (stat_of(got[HALF:], 0), got[:HALF].astype(F32))
        if side == 0:
            stat_t, half_t = stat, mine[:HALF]
            stat_b, half_b = merge([(stat, mine[HALF:]), theirs])
        else:
            stat_t, half_t = merge([(stat, mine[:HALF]), theirs])
            stat_b, half_b = stat, mine[HALF:]
        out[:HALF] = half_t.astype(BF16)
        out[HALF:C] = half_b.astype(BF16)
        out[C:] = stat_rows([stat_t, stat_b])


def finish_kernel(from_low, from_high, m, total, acc, shift, weight, wp, small, block, out):
    c = shift[...]
    stat = m[...] + jnp.log2(total[...]) + c
    mine = acc[...] / total[...]
    halves = []
    for i in range(2):
        rows = slice(i * HALF, (i + 1) * HALF)
        parts = [(stat, mine[rows])] + [
            (stat_of(got[C:], i) + c, got[rows].astype(F32)) for got in (from_low, from_high)
        ]
        halves.append(merge(parts)[1])
    mixed_in = jnp.concatenate(halves, 0).astype(BF16)
    mixed = (dot(mixed_in, weight[:, 2 * C :], ((0,), (0,))) + small[4:5, 2 * C :]).astype(BF16)
    attended = dot(mixed, wp[...], ((1,), (0,))) + small[3:4, :C] + block[...].astype(F32)
    out[...] = attended.astype(BF16)


def pack_kernel(flat, small):
    small[...] = jnp.zeros_like(small)
    at = 0
    for i, n in enumerate((C, C, C, C, 3 * C, OUT)):
        small[i, :n] = flat[at : at + n]
        at += n


def up_phases_kernel(weight, out):
    w = [[weight[b, c].astype(F32) for c in range(3)] for b in range(3)]

    def pairs(a, b, c):
        return ((a, b + c), (a + b, c))

    by_row = [pairs(*(w[b][c] for b in range(3))) for c in range(3)]
    for di in range(2):
        for rt in range(2):
            by_column = pairs(*(by_row[c][di][rt] for c in range(3)))
            for dj in range(2):
                for ct in range(2):
                    value = jnp.concatenate(
                        [by_column[dj][ct], jnp.zeros((256 - OUT, C), F32)], 0
                    )
                    out[di, dj, rt, ct * C : (ct + 1) * C] = value.T.astype(BF16)


def fill_plain(scratch, index, row):
    def store(variant, value):
        scratch[index, :, variant * C : (variant + 1) * C] = value

    col_variants(row.astype(F32), store)


def store_phase(wide, row, dj, value):
    for part in range(2):
        wide[part, row, pl.ds(dj, W, stride=2), :] = value[:, part * 128 : (part + 1) * 128]


def read_row(wide, row):
    return jnp.concatenate([wide[0, row].T, wide[1, row].T[: OUT - 128]], 0)


def up_inner_kernel(body, weight, small, out, edge, scratch, wide):
    for i in range(ROWS):
        fill_plain(scratch, i, body[i])
    b = small[5:6, :256]
    for di in range(2):
        for dj in range(2):
            full = scratch[:, :, dj * C : (dj + 2) * C].reshape(CELLS, 2 * C)
            if di == 0:
                here = dot(full, weight[0, dj, 1], ((1,), (0,))) + b
                beside = dot(full[: 2 * W], weight[0, dj, 0], ((1,), (0,)))
                parts = [here[:W], here[W : 2 * W] + beside[:W], here[2 * W :] + beside[W:]]
            else:
                here = dot(full, weight[1, dj, 0], ((1,), (0,))) + b
                beside = dot(full[W:], weight[1, dj, 1], ((1,), (0,)))
                parts = [here[:W] + beside[:W], here[W : 2 * W] + beside[W:], here[2 * W :]]
            for i, part in enumerate(parts):
                store_phase(wide, 2 * i + di, dj, part)
    for row in range(1, 2 * ROWS - 1):
        out[row] = read_row(wide, row).astype(BF16)
    edge[0] = read_row(wide, 0)
    edge[1] = read_row(wide, 2 * ROWS - 1)


def up_edges_kernel(low, high, weight, edge, _start, out, scratch, wide, rows, sem):
    _, _, above, below = inside()
    for i, (ref, present) in enumerate(((low, above), (high, below))):
        row = ref[0]
        fill_plain(scratch, i, jnp.where(present, row, jnp.zeros_like(row)))
    copies = []
    for side in range(2):
        for dj in range(2):
            left = scratch[side, :, dj * C : (dj + 2) * C]
            store_phase(wide, side, dj, dot(left, weight[side, dj, side], ((1,), (0,))))
        rows[side] = (edge[side] + read_row(wide, side)).astype(BF16)
        row = out.at[side * (2 * ROWS - 1)]
        copies.append(pltpu.make_async_copy(rows.at[side], row, sem.at[side]))
        copies[side].start()
    for copy in copies:
        copy.wait()


def permute_z(value, by):
    pairs = [(x * ZN + z, x * ZN + (z + by) % ZN) for x in range(XN) for z in range(ZN)]
    return lax.ppermute(value, "rows", pairs)


def permute_x(value, by):
    pairs = [(x * ZN + z, (x + by) % XN * ZN + z) for x in range(XN) for z in range(ZN)]
    return lax.ppermute(value, "rows", pairs)


def to_bands(value, by):
    n = XN * ZN
    return lax.ppermute(value, "rows", [(i, (i + by) % n) for i in range(n)])


def on_device(
    latent,
    norm1_gain,
    conv1_weight,
    conv1_bias,
    attention_gain,
    qkv_weight,
    qkv_bias,
    proj_weight,
    proj_bias,
    up_weight,
    up_bias,
):
    own = latent[0]
    two = lax.ppermute(own, "tm", [(t, (t + 2) % TN) for t in range(TN)])
    flat = (norm1_gain, conv1_bias, attention_gain, proj_bias, qkv_bias, up_bias)
    ends = [sum(v.shape[0] for v in flat[: i + 1]) for i in range(len(flat))]
    joined_flat = functools.reduce(
        jnp.add,
        [jnp.pad(v, (end - v.shape[0], ends[-1] - end)) for v, end in zip(flat, ends)],
    )
    small = call(pack_kernel, [((8, 3 * C), F32)], joined_flat, name="pack")
    acc, w_own = conv_band(own, small, conv1_weight, 2)
    pairs = [(t, t ^ 1) for t in range(TN)]
    to_next, to_previous, pair = call(
        edge_payload_kernel,
        [((2, W, C), BF16)] * 2 + [((ROWS, W, C), BF16)],
        own,
        two,
        acc,
        name="edge_payload",
        specs=[VM, VM, ANY],
    )
    low, high = to_bands(to_next, 1), to_bands(to_previous, -1)
    one = lax.ppermute(pair, "tm", pairs)
    acc, w_two = conv_band(two, small, conv1_weight, 0, acc)
    acc, w_one = conv_band(one, small, conv1_weight, 1, acc)
    pair_edges = call(
        pair_edges_kernel,
        [((2, W, C), BF16)],
        low,
        high,
        acc,
        name="pair_edges",
        specs=[VM, VM, ANY],
    )
    one_edges = lax.ppermute(pair_edges, "tm", pairs)
    acc = call(
        conv_edges_kernel,
        [((CELLS, C), F32)],
        low,
        high,
        small,
        w_own,
        w_two,
        acc,
        name="conv_edges",
        flops=2 * CELLS * 2 * C * C,
        scratch=[pltpu.VMEM((4, W, 3 * C), BF16)],
        aliases={5: 0},
    )
    block, normed = call(
        conv_last_kernel,
        [((CELLS, C), BF16)] * 2,
        one_edges,
        own,
        small,
        w_one,
        acc,
        name="conv_last",
        flops=2 * CELLS * C * C,
        scratch=[pltpu.VMEM((2, W, 3 * C), BF16)],
    )

    up, down = permute_z(normed, 1), permute_z(normed, -1)
    query, shift = call(
        query_kernel,
        [((C, CELLS), BF16), ((1, CELLS), F32)],
        normed,
        qkv_weight,
        small,
        name="queries",
        flops=4 * CELLS * C * C,
    )
    q_low, q_high = permute_x(query, 1), permute_x(query, -1)
    q_far = permute_x(query, 2)
    up2, down2 = permute_z(up, 1), permute_z(down, -1)
    early = [normed, up, down]
    near = [q_low, q_high, query]
    (state,) = attention_step(early, near)
    phases = call(
        up_phases_kernel,
        [((2, 2, 2, 2 * C, 256), BF16)],
        up_weight.transpose(0, 1, 3, 2),
        name="up_phases",
        flops=1e7,
        nbytes=4e6,
    )
    up2, down2 = after((up2, down2), state[0], phases)
    up3, down3 = permute_z(up2, 1), permute_z(down2, -1)
    (far,) = attention_step(early, [q_far])
    queries = near + [q_far]
    state, far = attention_step([up2, down2], queries, (state, far))
    up4, down4 = permute_z(up3[: CELLS // 2], 1), permute_z(down3[CELLS // 2 :], -1)
    state, far = attention_step([up3, down3], queries, (state, far))
    last = [up4, down4]
    pay_t, pay_b = opposite(last, q_far, far)
    half_low, half_high = permute_x(pay_t, 1), permute_x(pay_b, -1)
    (sides,) = attention_step(last, near, (state,), 0, 2 * CELLS)
    to_low, to_high = call(
        relay_kernel,
        [((C + STAT, CELLS), BF16)] * 2,
        half_low,
        half_high,
        *sides,
        name="relay",
    )
    from_low, from_high = permute_x(to_high, 1), permute_x(to_low, -1)
    (mine,) = attention_step(last, near, (state,), 2 * CELLS, 3 * CELLS)
    attended = call(
        finish_kernel,
        [((CELLS, C), BF16)],
        from_low,
        from_high,
        *mine,
        shift,
        qkv_weight,
        proj_weight,
        small,
        block,
        name="finish",
        flops=4 * CELLS * C * C,
    ).reshape(ROWS, W, C)
    edge_low, edge_high = to_bands(attended[2:], 1), to_bands(attended[:1], -1)
    inner, edge = call(
        up_inner_kernel,
        [((2 * ROWS, OUT, 2 * W), BF16), ((2, OUT, 2 * W), F32)],
        attended,
        phases,
        small,
        name="up_inner",
        flops=2 * CELLS * 14 * C * OUT,
        scratch=[
            pltpu.VMEM((ROWS, W, 3 * C), BF16),
            pltpu.VMEM((2, 2 * ROWS, 2 * W, 128), F32),
        ],
    )
    result = call(
        up_edges_kernel,
        [((2 * ROWS, OUT, 2 * W), BF16)],
        edge_low,
        edge_high,
        phases,
        edge,
        inner,
        name="up_edges",
        flops=2 * CELLS * 2 * C * OUT,
        scratch=[
            pltpu.VMEM((2, W, 3 * C), BF16),
            pltpu.VMEM((2, 2, 2 * W, 128), F32),
            pltpu.VMEM((2, OUT, 2 * W), BF16),
            pltpu.SemaphoreType.DMA((2,)),
        ],
        specs=[VM, VM, VM, VM, ANY],
        out_spec=ANY,
        aliases={4: 0},
    )
    return result.transpose(0, 2, 1)[None]


def solution(mesh):
    return jax.shard_map(
        on_device,
        mesh=mesh,
        in_specs=(P("tm", "rows", None, None), P(), P(), P(), P(), P(), P(), P(), P(), P(), P()),
        out_specs=P("tm", "rows", None, None),
        check_vma=False,
    )
```

```python
import functools
import math

import jax
import jax.numpy as jnp
from jax import lax
from jax.experimental import pallas as pl
from jax.experimental.pallas import tpu as pltpu
from jax.sharding import PartitionSpec as P

F32 = jnp.float32
BF16 = jnp.bfloat16
ROWS = 3
W = 128
C = 384
OUT = 192
CELLS = ROWS * W
XN, ZN, TN = 4, 8, 8
QALL = XN * CELLS
HALF = C // 2
STAT = 16
LOG2E = math.log2(math.e)


def dot(a, b, dims):
    return lax.dot_general(a, b, (dims, ((), ())), preferred_element_type=F32)


def params(mib=32):
    return pltpu.CompilerParams(vmem_limit_bytes=mib * 2**20)


def cost(flops, bytes_accessed):
    return pl.CostEstimate(flops=int(flops), bytes_accessed=int(bytes_accessed), transcendentals=0)


VM = pl.BlockSpec(memory_space=pltpu.VMEM)
ANY = pl.BlockSpec(memory_space=pl.ANY)
HBM = pl.BlockSpec(memory_space=pltpu.HBM)


def call(body, outs, *args, name, flops=1e6, nbytes=1e6, aliases=None, scratch=(), mib=32, specs=None, out_spec=VM):
    shapes = [jax.ShapeDtypeStruct(shape, dtype) for shape, dtype in outs]
    result = pl.pallas_call(
        body,
        in_specs=specs or [VM] * len(args),
        out_specs=[out_spec] * len(shapes),
        out_shape=shapes,
        input_output_aliases=aliases or {},
        scratch_shapes=list(scratch),
        compiler_params=params(mib),
        cost_estimate=cost(flops, nbytes),
        name=name,
    )(*args)
    return result[0] if len(shapes) == 1 else result


def col_variants(y, store):
    column = lax.broadcasted_iota(jnp.int32, y.shape, 0)
    before = jnp.where(column == 0, 0.0, pltpu.roll(y, 1, 0))
    after = jnp.where(column == W - 1, 0.0, pltpu.roll(y, W - 1, 0))
    store(0, before.astype(BF16))
    store(1, y.astype(BF16))
    store(2, after.astype(BF16))


def activate(row, gain):
    x = row.astype(F32)
    y = x * lax.rsqrt(jnp.mean(x * x, -1, keepdims=True) + 1e-6) * gain
    y = y / (1.0 + jnp.exp(-y))
    return y.astype(BF16).astype(F32)


def inside():
    frame, band = lax.axis_index("tm"), lax.axis_index("rows")
    return frame >= 2, frame >= 1, band >= 1, band < XN * ZN - 1


def fill_rows(scratch, rows, gain, present=None):
    for index, row in enumerate(rows):
        y = activate(row, gain)
        if present is not None:
            y = jnp.where(present[index], y, 0.0)

        def store(variant, value, index=index):
            scratch[index, :, variant * C : (variant + 1) * C] = value

        col_variants(y, store)


def conv_bands_kernel(first_tap, n, *refs):
    frames, (small, weight) = refs[:n], refs[n : n + 2]
    start = refs[n + 2] if len(refs) == n + 9 else None
    acc, beside, scratch, held, sem, beside_sem = refs[-6:]

    def copy(t, b):
        return pltpu.make_async_copy(weight.at[first_tap + t, b], held.at[t, b], sem.at[t, b])

    for t in range(n):
        for b in range(3):
            copy(t, b).start()
    extra = [
        pltpu.make_async_copy(
            weight.at[first_tap + t, 2 * side], beside.at[t, side], beside_sem.at[t, side]
        )
        for t in range(n)
        for side in range(2)
    ]
    for extra_copy in extra:
        extra_copy.start()
    for t, frame in enumerate(frames):
        zero = jnp.zeros((W, 3 * C), BF16)
        scratch[t, 0] = zero
        scratch[t, 1 + ROWS] = zero
        present = [True] * ROWS if start is None else [inside()[first_tap + t]] * ROWS
        rows = [frame[i] for i in range(ROWS)]
        fill_rows(scratch.at[t, 1 : 1 + ROWS], rows, small[0:1, :C], present)
    acc[...] = jnp.zeros((CELLS, C), F32) if start is None else start[...]

    def step(g, carry):
        t, b = g // 3, g % 3
        copy(t, b).wait()
        left = scratch[t, pl.ds(b, ROWS)].reshape(CELLS, 3 * C)
        acc[...] += dot(left, held[t, b].reshape(3 * C, C), ((1,), (0,)))
        return carry

    lax.fori_loop(0, 3 * n, step, 0)
    for extra_copy in extra:
        extra_copy.wait()


def conv_bands(frames, small, weight, first_tap, start=None):
    n = len(frames)
    return call(
        functools.partial(conv_bands_kernel, first_tap, n),
        [((CELLS, C), F32), ((n, 2, 3, C, C), BF16)],
        *frames,
        small,
        weight,
        *(() if start is None else (start,)),
        name="conv_bands",
        flops=2 * CELLS * 9 * n * C * C,
        scratch=[
            pltpu.VMEM((n, ROWS + 2, W, 3 * C), BF16),
            pltpu.VMEM((n, 3, 3, C, C), BF16),
            pltpu.SemaphoreType.DMA((n, 3)),
            pltpu.SemaphoreType.DMA((n, 2)),
        ],
        specs=[VM] * (n + 1) + [HBM] + ([] if start is None else [VM]),
        aliases=None if start is None else {n + 2: 0},
        mib=49,
    )


def edge_taps(scratch, low, high, weight, t):
    left = dot(scratch[low], weight[t, 0].reshape(3 * C, C), ((1,), (0,)))
    right = dot(scratch[high], weight[t, 1].reshape(3 * C, C), ((1,), (0,)))
    return left, right


def conv_edges_kernel(low, high, small, w_own, w_pair, start, acc, scratch):
    two, _, above, below = inside()
    present = [above, above & two, below, below & two]
    fill_rows(scratch, [low[0], low[1], high[0], high[1]], small[0:1, :C], present)
    own = edge_taps(scratch, 0, 2, w_own, 0)
    two = edge_taps(scratch, 1, 3, w_pair, 0)
    acc[...] = start[...]
    acc[:W] += own[0] + two[0]
    acc[2 * W :] += own[1] + two[1]


def conv_last_kernel(edges, own, small, weight, start, block, normed, scratch):
    _, one, above, below = inside()
    fill_rows(scratch, [edges[0], edges[1]], small[0:1, :C], [above & one, below & one])
    sides = edge_taps(scratch, 0, 1, weight, 1)
    bias, gain2 = small[1:2, :C], small[2:3, :C]
    for i in range(ROWS):
        rows = slice(i * W, (i + 1) * W)
        total = start[rows] + bias
        if i != 1:
            total += sides[i // 2]
        x = (own[i].astype(F32) + total.astype(BF16).astype(F32)).astype(BF16)
        block[rows] = x
        x = x.astype(F32)
        x = x * lax.rsqrt(jnp.mean(x * x, -1, keepdims=True) + 1e-6) * gain2
        normed[rows] = x.astype(BF16)


def edge_payload_kernel(own, two, _acc, to_next, to_previous, pair):
    to_next[0] = own[ROWS - 1]
    to_next[1] = two[ROWS - 1]
    to_previous[0] = own[0]
    to_previous[1] = two[0]

    odd = lax.rem(lax.axis_index("tm"), 2)

    @pl.when(odd == 0)
    def _():
        pair[...] = own[...]

    @pl.when(odd == 1)
    def _():
        pair[...] = two[...]


def pair_edges_kernel(low, high, _acc, out):
    index = lax.rem(lax.axis_index("tm"), 2)
    out[0] = low[index]
    out[1] = high[index]


def query_kernel(normed, weight, small, out, shift):
    scale = C**-0.5 * LOG2E
    wq, wk = weight[:, :C], weight[:, C : 2 * C]
    q = (dot(normed[...], wq, ((1,), (0,))) + small[4:5, :C]).astype(BF16)
    out[...] = (dot(wk, q, ((1,), (1,))) * scale).astype(BF16)
    bk = jnp.broadcast_to(small[4:5, C : 2 * C], (8, C))
    shift[...] = dot(bk, q.astype(F32), ((1,), (1,)))[:1] * scale


def spans(refs, low, high):
    at = 0
    for ref in refs:
        n = ref.shape[1]
        first, last = max(low, at), min(high, at + n)
        if first < last:
            yield ref, first - at, last - at, first - low, last - low
        at += n


def read(refs, low, high):
    pieces = [ref[:, a:b] for ref, a, b, _, _ in spans(refs, low, high)]
    return pieces[0] if len(pieces) == 1 else jnp.concatenate(pieces, 1)


def write(refs, low, high, value):
    for ref, a, b, first, last in spans(refs, low, high):
        ref[:, a:b] = value[:, first:last]


def joined(refs):
    return refs[0][...] if len(refs) == 1 else jnp.concatenate([r[...] for r in refs], 0)


def softmax_tiles(keys, tiles, q_of, old_of, give):
    keys_t = keys.T

    def scores(tile):
        return dot(keys, q_of(*tile), ((1,), (0,)))

    following = scores(tiles[0])
    for i, tile in enumerate(tiles):
        s = following
        if i + 1 < len(tiles):
            following = scores(tiles[i + 1])
        old = old_of(*tile)
        m = jnp.max(s, 0, keepdims=True)
        if old is not None:
            m = jnp.maximum(m, old[0])
        p = jnp.exp2(s - m)
        total = jnp.sum(p, 0, keepdims=True)
        acc = dot(keys_t, p.astype(BF16), ((1,), (0,)))
        if old is not None:
            alpha = jnp.exp2(old[0] - m)
            total = total + alpha * old[1]
            acc = acc + alpha * old[2]
        give(*tile, (m, total, acc))


def tiles_of(low, high, size=512):
    return [(at, min(at + size, high)) for at in range(low, high, size)]


def attention_kernel(n_keys, n_q, n_state, n_out, low, high, *refs):
    keys = joined(refs[:n_keys])
    queries = refs[n_keys : n_keys + n_q]
    state = refs[n_keys + n_q : n_keys + n_q + 3 * n_state]
    outs = refs[n_keys + n_q + 3 * n_state :]

    def old_of(a, b):
        return [read(state[i::3], a, b) for i in range(3)] if n_state else None

    def give(a, b, values):
        for i, value in enumerate(values):
            write(outs[i::3], a - low, b - low, value)

    softmax_tiles(keys, tiles_of(low, high), lambda a, b: read(queries, a, b), old_of, give)


def attention_step(keys, queries, state=(), low=0, high=None):
    widths = [q.shape[1] for q in queries]
    high = sum(widths) if high is None else high
    rows = sum(k.shape[0] for k in keys)
    whole_state = bool(state) and high - low == sum(s[0].shape[1] for s in state)
    outs = [s[0].shape[1] for s in state] if whole_state else [high - low]
    flat = [v for s in state for v in s]
    before = len(keys) + len(queries)
    result = call(
        functools.partial(
            attention_kernel, len(keys), len(queries), len(state), len(outs), low, high
        ),
        [shape for n in outs for shape in (((1, n), F32), ((1, n), F32), ((C, n), F32))],
        *keys,
        *queries,
        *flat,
        name="attention_step",
        flops=4 * rows * (high - low) * C,
        nbytes=6e6,
        aliases={before + i: i for i in range(len(flat))} if whole_state else None,
    )
    return [tuple(result[i : i + 3]) for i in range(0, len(result), 3)]


def gate_kernel(*refs):
    pass


def after(values, *done):
    count = len(values)
    return call(
        gate_kernel,
        [(v.shape, v.dtype) for v in values],
        *values,
        *done,
        name="gate",
        flops=1,
        nbytes=1,
        specs=[ANY] * (count + len(done)),
        out_spec=ANY,
        aliases={i: i for i in range(count)},
    )


def split3(x):
    hi = x.astype(BF16)
    rest = x - hi.astype(F32)
    mid = rest.astype(BF16)
    low = (rest - mid.astype(F32)).astype(BF16)
    return hi, mid, low


def stat_rows(parts):
    n = parts[0].shape[1]
    row = lax.broadcasted_iota(jnp.int32, (STAT, n), 0)
    block = jnp.zeros((STAT, n), F32)
    for i, part in enumerate(parts):
        for j, piece in enumerate(split3(part)):
            block = jnp.where(row == 3 * i + j, piece.astype(F32), block)
    return block.astype(BF16)


def stat_of(block, i):
    b = block.astype(F32)
    return b[3 * i : 3 * i + 1] + b[3 * i + 1 : 3 * i + 2] + b[3 * i + 2 : 3 * i + 3]


def opposite_kernel(n_keys, *refs):
    q, m_old, l_old, acc_old, top, bottom = refs[n_keys:]

    def give(_a, _b, values):
        m, total, acc = values
        out = (acc / total).astype(BF16)
        stats = stat_rows([m + jnp.log2(total)])
        top[:HALF] = out[:HALF]
        top[HALF:] = stats
        bottom[:HALF] = out[HALF:]
        bottom[HALF:] = stats

    old = lambda a, b: (m_old[...], l_old[...], acc_old[...])
    softmax_tiles(joined(refs[:n_keys]), [(0, CELLS)], lambda a, b: q[...], old, give)


def opposite(keys, q_far, state):
    rows = sum(k.shape[0] for k in keys)
    return call(
        functools.partial(opposite_kernel, len(keys)),
        [((HALF + STAT, CELLS), BF16)] * 2,
        *keys,
        q_far,
        *state,
        name="opposite",
        flops=4 * rows * CELLS * C,
        nbytes=2e6,
    )


def merge(parts):
    top = functools.reduce(jnp.maximum, [s for s, _ in parts])
    w = [jnp.exp2(s - top) for s, _ in parts]
    total = functools.reduce(jnp.add, w)
    inverse = 1.0 / total
    out = functools.reduce(jnp.add, [(a * inverse) * o for a, (_, o) in zip(w, parts)])
    return top + jnp.log2(total), out


def relay_kernel(from_low, from_high, m, total, acc, to_low, to_high):
    for side, got, out in ((0, from_high, to_low), (1, from_low, to_high)):
        cols = slice(side * CELLS, (side + 1) * CELLS)
        stat = m[:, cols] + jnp.log2(total[:, cols])
        mine = acc[:, cols] / total[:, cols]
        theirs = (stat_of(got[HALF:], 0), got[:HALF].astype(F32))
        if side == 0:
            stat_t, half_t = stat, mine[:HALF]
            stat_b, half_b = merge([(stat, mine[HALF:]), theirs])
        else:
            stat_t, half_t = merge([(stat, mine[:HALF]), theirs])
            stat_b, half_b = stat, mine[HALF:]
        out[:HALF] = half_t.astype(BF16)
        out[HALF:C] = half_b.astype(BF16)
        out[C:] = stat_rows([stat_t, stat_b])


def finish_kernel(from_low, from_high, m, total, acc, shift, weight, wp, small, block, out):
    c = shift[...]
    stat = m[...] + jnp.log2(total[...]) + c
    mine = acc[...] / total[...]
    halves = []
    for i in range(2):
        rows = slice(i * HALF, (i + 1) * HALF)
        parts = [(stat, mine[rows])] + [
            (stat_of(got[C:], i) + c, got[rows].astype(F32)) for got in (from_low, from_high)
        ]
        halves.append(merge(parts)[1])
    mixed_in = jnp.concatenate(halves, 0).astype(BF16)
    mixed = (dot(mixed_in, weight[:, 2 * C :], ((0,), (0,))) + small[4:5, 2 * C :]).astype(BF16)
    attended = dot(mixed, wp[...], ((1,), (0,))) + small[3:4, :C] + block[...].astype(F32)
    out[...] = attended.astype(BF16)


def pack_kernel(flat, small):
    small[...] = jnp.zeros_like(small)
    at = 0
    for i, n in enumerate((C, C, C, C, 3 * C, OUT)):
        small[i, :n] = flat[at : at + n]
        at += n


def up_phases_kernel(weight, out):
    w = [[weight[b, c].astype(F32) for c in range(3)] for b in range(3)]

    def pairs(a, b, c):
        return ((a, b + c), (a + b, c))

    by_row = [pairs(*(w[b][c] for b in range(3))) for c in range(3)]
    for di in range(2):
        for rt in range(2):
            by_column = pairs(*(by_row[c][di][rt] for c in range(3)))
            for dj in range(2):
                for ct in range(2):
                    value = jnp.concatenate(
                        [by_column[dj][ct], jnp.zeros((256 - OUT, C), F32)], 0
                    )
                    out[di, dj, rt, ct * C : (ct + 1) * C] = value.T.astype(BF16)


def fill_plain(scratch, index, row):
    def store(variant, value):
        scratch[index, :, variant * C : (variant + 1) * C] = value

    col_variants(row.astype(F32), store)


def store_phase(wide, row, dj, value):
    for part in range(2):
        wide[part, row, pl.ds(dj, W, stride=2), :] = value[:, part * 128 : (part + 1) * 128]


def read_row(wide, row):
    return jnp.concatenate([wide[0, row].T, wide[1, row].T[: OUT - 128]], 0)


def up_inner_kernel(body, weight, small, out, edge, scratch, wide):
    for i in range(ROWS):
        fill_plain(scratch, i, body[i])
    b = small[5:6, :256]
    for di in range(2):
        for dj in range(2):
            full = scratch[:, :, dj * C : (dj + 2) * C].reshape(CELLS, 2 * C)
            if di == 0:
                here = dot(full, weight[0, dj, 1], ((1,), (0,))) + b
                beside = dot(full[: 2 * W], weight[0, dj, 0], ((1,), (0,)))
                parts = [here[:W], here[W : 2 * W] + beside[:W], here[2 * W :] + beside[W:]]
            else:
                here = dot(full, weight[1, dj, 0], ((1,), (0,))) + b
                beside = dot(full[W:], weight[1, dj, 1], ((1,), (0,)))
                parts = [here[:W] + beside[:W], here[W : 2 * W] + beside[W:], here[2 * W :]]
            for i, part in enumerate(parts):
                store_phase(wide, 2 * i + di, dj, part)
    for row in range(1, 2 * ROWS - 1):
        out[row] = read_row(wide, row).astype(BF16)
    edge[0] = read_row(wide, 0)
    edge[1] = read_row(wide, 2 * ROWS - 1)


def up_edges_kernel(low, high, weight, edge, _start, out, scratch, wide, rows, sem):
    _, _, above, below = inside()
    for i, (ref, present) in enumerate(((low, above), (high, below))):
        row = ref[0]
        fill_plain(scratch, i, jnp.where(present, row, jnp.zeros_like(row)))
    copies = []
    for side in range(2):
        for dj in range(2):
            left = scratch[side, :, dj * C : (dj + 2) * C]
            store_phase(wide, side, dj, dot(left, weight[side, dj, side], ((1,), (0,))))
        rows[side] = (edge[side] + read_row(wide, side)).astype(BF16)
        row = out.at[side * (2 * ROWS - 1)]
        copies.append(pltpu.make_async_copy(rows.at[side], row, sem.at[side]))
        copies[side].start()
    for copy in copies:
        copy.wait()


def permute_z(value, by):
    pairs = [(x * ZN + z, x * ZN + (z + by) % ZN) for x in range(XN) for z in range(ZN)]
    return lax.ppermute(value, "rows", pairs)


def permute_x(value, by):
    pairs = [(x * ZN + z, (x + by) % XN * ZN + z) for x in range(XN) for z in range(ZN)]
    return lax.ppermute(value, "rows", pairs)


def to_bands(value, by):
    n = XN * ZN
    return lax.ppermute(value, "rows", [(i, (i + by) % n) for i in range(n)])


def on_device(
    latent,
    norm1_gain,
    conv1_weight,
    conv1_bias,
    attention_gain,
    qkv_weight,
    qkv_bias,
    proj_weight,
    proj_bias,
    up_weight,
    up_bias,
):
    own = latent[0]
    two = lax.ppermute(own, "tm", [(t, (t + 2) % TN) for t in range(TN)])
    flat = (norm1_gain, conv1_bias, attention_gain, proj_bias, qkv_bias, up_bias)
    ends = [sum(v.shape[0] for v in flat[: i + 1]) for i in range(len(flat))]
    joined_flat = functools.reduce(
        jnp.add,
        [jnp.pad(v, (end - v.shape[0], ends[-1] - end)) for v, end in zip(flat, ends)],
    )
    small = call(pack_kernel, [((8, 3 * C), F32)], joined_flat, name="pack")
    acc, w_own = conv_bands([own], small, conv1_weight, 2)
    pairs = [(t, t ^ 1) for t in range(TN)]
    to_next, to_previous, pair = call(
        edge_payload_kernel,
        [((2, W, C), BF16)] * 2 + [((ROWS, W, C), BF16)],
        own,
        two,
        acc,
        name="edge_payload",
        specs=[VM, VM, ANY],
    )
    low, high = to_bands(to_next, 1), to_bands(to_previous, -1)
    one = lax.ppermute(pair, "tm", pairs)
    acc, w_pair = conv_bands([two, one], small, conv1_weight, 0, acc)
    pair_edges = call(
        pair_edges_kernel,
        [((2, W, C), BF16)],
        low,
        high,
        acc,
        name="pair_edges",
        specs=[VM, VM, ANY],
    )
    one_edges = lax.ppermute(pair_edges, "tm", pairs)
    acc = call(
        conv_edges_kernel,
        [((CELLS, C), F32)],
        low,
        high,
        small,
        w_own,
        w_pair,
        acc,
        name="conv_edges",
        flops=2 * CELLS * 2 * C * C,
        scratch=[pltpu.VMEM((4, W, 3 * C), BF16)],
        aliases={5: 0},
    )
    block, normed = call(
        conv_last_kernel,
        [((CELLS, C), BF16)] * 2,
        one_edges,
        own,
        small,
        w_pair,
        acc,
        name="conv_last",
        flops=2 * CELLS * C * C,
        scratch=[pltpu.VMEM((2, W, 3 * C), BF16)],
    )

    up, down = permute_z(normed, 1), permute_z(normed, -1)
    query, shift = call(
        query_kernel,
        [((C, CELLS), BF16), ((1, CELLS), F32)],
        normed,
        qkv_weight,
        small,
        name="queries",
        flops=4 * CELLS * C * C,
    )
    q_low, q_high = permute_x(query, 1), permute_x(query, -1)
    q_far = permute_x(query, 2)
    up2, down2 = permute_z(up, 1), permute_z(down, -1)
    early = [normed, up, down]
    near = [q_low, q_high, query]
    (state,) = attention_step(early, near)
    phases = call(
        up_phases_kernel,
        [((2, 2, 2, 2 * C, 256), BF16)],
        up_weight.transpose(0, 1, 3, 2),
        name="up_phases",
        flops=1e7,
        nbytes=4e6,
    )
    up2, down2 = after((up2, down2), state[0], phases)
    up3, down3 = permute_z(up2, 1), permute_z(down2, -1)
    (far,) = attention_step(early, [q_far])
    queries = near + [q_far]
    state, far = attention_step([up2, down2], queries, (state, far))
    up4, down4 = permute_z(up3[: CELLS // 2], 1), permute_z(down3[CELLS // 2 :], -1)
    state, far = attention_step([up3, down3], queries, (state, far))
    last = [up4, down4]
    pay_t, pay_b = opposite(last, q_far, far)
    half_low, half_high = permute_x(pay_t, 1), permute_x(pay_b, -1)
    (sides,) = attention_step(last, near, (state,), 0, 2 * CELLS)
    to_low, to_high = call(
        relay_kernel,
        [((C + STAT, CELLS), BF16)] * 2,
        half_low,
        half_high,
        *sides,
        name="relay",
    )
    from_low, from_high = permute_x(to_high, 1), permute_x(to_low, -1)
    (mine,) = attention_step(last, near, (state,), 2 * CELLS, 3 * CELLS)
    attended = call(
        finish_kernel,
        [((CELLS, C), BF16)],
        from_low,
        from_high,
        *mine,
        shift,
        qkv_weight,
        proj_weight,
        small,
        block,
        name="finish",
        flops=4 * CELLS * C * C,
    ).reshape(ROWS, W, C)
    edge_low, edge_high = to_bands(attended[2:], 1), to_bands(attended[:1], -1)
    inner, edge = call(
        up_inner_kernel,
        [((2 * ROWS, OUT, 2 * W), BF16), ((2, OUT, 2 * W), F32)],
        attended,
        phases,
        small,
        name="up_inner",
        flops=2 * CELLS * 14 * C * OUT,
        scratch=[
            pltpu.VMEM((ROWS, W, 3 * C), BF16),
            pltpu.VMEM((2, 2 * ROWS, 2 * W, 128), F32),
        ],
    )
    result = call(
        up_edges_kernel,
        [((2 * ROWS, OUT, 2 * W), BF16)],
        edge_low,
        edge_high,
        phases,
        edge,
        inner,
        name="up_edges",
        flops=2 * CELLS * 2 * C * OUT,
        scratch=[
            pltpu.VMEM((2, W, 3 * C), BF16),
            pltpu.VMEM((2, 2, 2 * W, 128), F32),
            pltpu.VMEM((2, OUT, 2 * W), BF16),
            pltpu.SemaphoreType.DMA((2,)),
        ],
        specs=[VM, VM, VM, VM, ANY],
        out_spec=ANY,
        aliases={4: 0},
    )
    return result.transpose(0, 2, 1)[None]


def solution(mesh):
    return jax.shard_map(
        on_device,
        mesh=mesh,
        in_specs=(P("tm", "rows", None, None), P(), P(), P(), P(), P(), P(), P(), P(), P(), P()),
        out_specs=P("tm", "rows", None, None),
        check_vma=False,
    )
```

```python
import functools
import math

import jax
import jax.numpy as jnp
from jax import lax
from jax.experimental import pallas as pl
from jax.experimental.pallas import tpu as pltpu
from jax.sharding import PartitionSpec as P

F32 = jnp.float32
BF16 = jnp.bfloat16
ROWS = 3
W = 128
C = 384
OUT = 192
CELLS = ROWS * W
XN, ZN, TN = 4, 8, 8
QALL = XN * CELLS
HALF = C // 2
STAT = 16
LOG2E = math.log2(math.e)


def dot(a, b, dims):
    return lax.dot_general(a, b, (dims, ((), ())), preferred_element_type=F32)


def params(mib=32):
    return pltpu.CompilerParams(vmem_limit_bytes=mib * 2**20)


def cost(flops, bytes_accessed):
    return pl.CostEstimate(flops=int(flops), bytes_accessed=int(bytes_accessed), transcendentals=0)


VM = pl.BlockSpec(memory_space=pltpu.VMEM)
ANY = pl.BlockSpec(memory_space=pl.ANY)
HBM = pl.BlockSpec(memory_space=pltpu.HBM)


def call(body, outs, *args, name, flops=1e6, nbytes=1e6, aliases=None, scratch=(), mib=32, specs=None, out_spec=VM):
    shapes = [jax.ShapeDtypeStruct(shape, dtype) for shape, dtype in outs]
    result = pl.pallas_call(
        body,
        in_specs=specs or [VM] * len(args),
        out_specs=[out_spec] * len(shapes),
        out_shape=shapes,
        input_output_aliases=aliases or {},
        scratch_shapes=list(scratch),
        compiler_params=params(mib),
        cost_estimate=cost(flops, nbytes),
        name=name,
    )(*args)
    return result[0] if len(shapes) == 1 else result


def col_variants(y, store):
    column = lax.broadcasted_iota(jnp.int32, y.shape, 0)
    before = jnp.where(column == 0, 0.0, pltpu.roll(y, 1, 0))
    after = jnp.where(column == W - 1, 0.0, pltpu.roll(y, W - 1, 0))
    store(0, before.astype(BF16))
    store(1, y.astype(BF16))
    store(2, after.astype(BF16))


def activate(row, gain):
    x = row.astype(F32)
    y = x * lax.rsqrt(jnp.mean(x * x, -1, keepdims=True) + 1e-6) * gain
    y = y / (1.0 + jnp.exp(-y))
    return y.astype(BF16).astype(F32)


def inside():
    frame, band = lax.axis_index("tm"), lax.axis_index("rows")
    return frame >= 2, frame >= 1, band >= 1, band < XN * ZN - 1


def fill_rows(scratch, rows, gain, present=None):
    for index, row in enumerate(rows):
        y = activate(row, gain)
        if present is not None:
            y = jnp.where(present[index], y, 0.0)

        def store(variant, value, index=index):
            scratch[index, :, variant * C : (variant + 1) * C] = value

        col_variants(y, store)


def band_rows(scratch, t, frame, gain, present=None):
    zero = jnp.zeros((W, 3 * C), BF16)
    scratch[t, 0] = zero
    scratch[t, 1 + ROWS] = zero
    present = None if present is None else [present] * ROWS
    fill_rows(scratch.at[t, 1 : 1 + ROWS], [frame[i] for i in range(ROWS)], gain, present)


def band_tap(scratch, t, b, weight):
    left = scratch[t, pl.ds(b, ROWS)].reshape(CELLS, 3 * C)
    return dot(left, weight.reshape(3 * C, C), ((1,), (0,)))


def conv_own_kernel(own, small, weight, acc, beside, earlier, scratch, held, sem, rest_sem):
    def copy(b):
        return pltpu.make_async_copy(weight.at[2, b], held.at[b], sem.at[b])

    for b in range(3):
        copy(b).start()
    rest = [
        pltpu.make_async_copy(weight.at[2, 0], beside.at[0], rest_sem.at[0]),
        pltpu.make_async_copy(weight.at[2, 2], beside.at[1], rest_sem.at[1]),
        pltpu.make_async_copy(weight.at[:2], earlier, rest_sem.at[2]),
    ]
    for one in rest:
        one.start()
    band_rows(scratch, 0, own, small[0:1, :C])
    acc[...] = jnp.zeros((CELLS, C), F32)

    def step(b, carry):
        copy(b).wait()
        acc[...] += band_tap(scratch, 0, b, held[b])
        return carry

    lax.fori_loop(0, 3, step, 0)
    for one in rest:
        one.wait()


def conv_own(own, small, weight):
    return call(
        conv_own_kernel,
        [((CELLS, C), F32), ((2, 3, C, C), BF16), ((2, 3, 3, C, C), BF16)],
        own,
        small,
        weight,
        name="conv_own",
        flops=2 * CELLS * 9 * C * C,
        scratch=[
            pltpu.VMEM((1, ROWS + 2, W, 3 * C), BF16),
            pltpu.VMEM((3, 3, C, C), BF16),
            pltpu.SemaphoreType.DMA((3,)),
            pltpu.SemaphoreType.DMA((3,)),
        ],
        specs=[VM, VM, HBM],
        mib=46,
    )


def conv_earlier_kernel(two, one, small, weight, start, acc, scratch):
    has_two, has_one, _, _ = inside()
    band_rows(scratch, 0, two, small[0:1, :C], has_two)
    band_rows(scratch, 1, one, small[0:1, :C], has_one)
    acc[...] = start[...]

    def step(g, carry):
        t, b = g // 3, g % 3
        acc[...] += band_tap(scratch, t, b, weight[t, b])
        return carry

    lax.fori_loop(0, 6, step, 0)


def conv_earlier(two, one, small, weight, start):
    return call(
        conv_earlier_kernel,
        [((CELLS, C), F32)],
        two,
        one,
        small,
        weight,
        start,
        name="conv_earlier",
        flops=2 * CELLS * 18 * C * C,
        scratch=[pltpu.VMEM((2, ROWS + 2, W, 3 * C), BF16)],
        aliases={4: 0},
    )


def edge_taps(scratch, low, high, first, last):
    left = dot(scratch[low], first[...].reshape(3 * C, C), ((1,), (0,)))
    right = dot(scratch[high], last[...].reshape(3 * C, C), ((1,), (0,)))
    return left, right


def conv_edges_kernel(low, high, small, w_own, w_pair, start, acc, scratch):
    two, _, above, below = inside()
    present = [above, above & two, below, below & two]
    fill_rows(scratch, [low[0], low[1], high[0], high[1]], small[0:1, :C], present)
    own = edge_taps(scratch, 0, 2, w_own.at[0], w_own.at[1])
    two = edge_taps(scratch, 1, 3, w_pair.at[0, 0], w_pair.at[0, 2])
    acc[...] = start[...]
    acc[:W] += own[0] + two[0]
    acc[2 * W :] += own[1] + two[1]


def conv_last_kernel(edges, own, small, weight, start, block, normed, scratch):
    _, one, above, below = inside()
    fill_rows(scratch, [edges[0], edges[1]], small[0:1, :C], [above & one, below & one])
    sides = edge_taps(scratch, 0, 1, weight.at[1, 0], weight.at[1, 2])
    bias, gain2 = small[1:2, :C], small[2:3, :C]
    for i in range(ROWS):
        rows = slice(i * W, (i + 1) * W)
        total = start[rows] + bias
        if i != 1:
            total += sides[i // 2]
        x = (own[i].astype(F32) + total.astype(BF16).astype(F32)).astype(BF16)
        block[rows] = x
        x = x.astype(F32)
        x = x * lax.rsqrt(jnp.mean(x * x, -1, keepdims=True) + 1e-6) * gain2
        normed[rows] = x.astype(BF16)


def edge_payload_kernel(own, two, _acc, to_next, to_previous, pair):
    to_next[0] = own[ROWS - 1]
    to_next[1] = two[ROWS - 1]
    to_previous[0] = own[0]
    to_previous[1] = two[0]

    odd = lax.rem(lax.axis_index("tm"), 2)

    @pl.when(odd == 0)
    def _():
        pair[...] = own[...]

    @pl.when(odd == 1)
    def _():
        pair[...] = two[...]


def pair_edges_kernel(low, high, _acc, out):
    index = lax.rem(lax.axis_index("tm"), 2)
    out[0] = low[index]
    out[1] = high[index]


def query_kernel(normed, weight, small, out, shift):
    scale = C**-0.5 * LOG2E
    wq, wk = weight[:, :C], weight[:, C : 2 * C]
    q = (dot(normed[...], wq, ((1,), (0,))) + small[4:5, :C]).astype(BF16)
    out[...] = (dot(wk, q, ((1,), (1,))) * scale).astype(BF16)
    bk = jnp.broadcast_to(small[4:5, C : 2 * C], (8, C))
    shift[...] = dot(bk, q.astype(F32), ((1,), (1,)))[:1] * scale


def spans(refs, low, high):
    at = 0
    for ref in refs:
        n = ref.shape[1]
        first, last = max(low, at), min(high, at + n)
        if first < last:
            yield ref, first - at, last - at, first - low, last - low
        at += n


def read(refs, low, high):
    pieces = [ref[:, a:b] for ref, a, b, _, _ in spans(refs, low, high)]
    return pieces[0] if len(pieces) == 1 else jnp.concatenate(pieces, 1)


def write(refs, low, high, value):
    for ref, a, b, first, last in spans(refs, low, high):
        ref[:, a:b] = value[:, first:last]


def joined(refs):
    return refs[0][...] if len(refs) == 1 else jnp.concatenate([r[...] for r in refs], 0)


def softmax_tiles(keys, tiles, q_of, old_of, give):
    keys_t = keys.T

    def scores(tile):
        return dot(keys, q_of(*tile), ((1,), (0,)))

    following = scores(tiles[0])
    for i, tile in enumerate(tiles):
        s = following
        if i + 1 < len(tiles):
            following = scores(tiles[i + 1])
        old = old_of(*tile)
        m = jnp.max(s, 0, keepdims=True)
        if old is not None:
            m = jnp.maximum(m, old[0])
        p = jnp.exp2(s - m)
        total = jnp.sum(p, 0, keepdims=True)
        acc = dot(keys_t, p.astype(BF16), ((1,), (0,)))
        if old is not None:
            alpha = jnp.exp2(old[0] - m)
            total = total + alpha * old[1]
            acc = acc + alpha * old[2]
        give(*tile, (m, total, acc))


def tiles_of(low, high, size=512):
    return [(at, min(at + size, high)) for at in range(low, high, size)]


def attention_kernel(n_keys, n_q, n_state, n_out, low, high, *refs):
    keys = joined(refs[:n_keys])
    queries = refs[n_keys : n_keys + n_q]
    state = refs[n_keys + n_q : n_keys + n_q + 3 * n_state]
    outs = refs[n_keys + n_q + 3 * n_state :]

    def old_of(a, b):
        return [read(state[i::3], a, b) for i in range(3)] if n_state else None

    def give(a, b, values):
        for i, value in enumerate(values):
            write(outs[i::3], a - low, b - low, value)

    softmax_tiles(keys, tiles_of(low, high), lambda a, b: read(queries, a, b), old_of, give)


def attention_step(keys, queries, state=(), low=0, high=None):
    widths = [q.shape[1] for q in queries]
    high = sum(widths) if high is None else high
    rows = sum(k.shape[0] for k in keys)
    whole_state = bool(state) and high - low == sum(s[0].shape[1] for s in state)
    outs = [s[0].shape[1] for s in state] if whole_state else [high - low]
    flat = [v for s in state for v in s]
    before = len(keys) + len(queries)
    result = call(
        functools.partial(
            attention_kernel, len(keys), len(queries), len(state), len(outs), low, high
        ),
        [shape for n in outs for shape in (((1, n), F32), ((1, n), F32), ((C, n), F32))],
        *keys,
        *queries,
        *flat,
        name="attention_step",
        flops=4 * rows * (high - low) * C,
        nbytes=6e6,
        aliases={before + i: i for i in range(len(flat))} if whole_state else None,
    )
    return [tuple(result[i : i + 3]) for i in range(0, len(result), 3)]


def gate_kernel(*refs):
    pass


def after(values, *done):
    count = len(values)
    return call(
        gate_kernel,
        [(v.shape, v.dtype) for v in values],
        *values,
        *done,
        name="gate",
        flops=1,
        nbytes=1,
        specs=[ANY] * (count + len(done)),
        out_spec=ANY,
        aliases={i: i for i in range(count)},
    )


def split3(x):
    hi = x.astype(BF16)
    rest = x - hi.astype(F32)
    mid = rest.astype(BF16)
    low = (rest - mid.astype(F32)).astype(BF16)
    return hi, mid, low


def stat_rows(parts):
    n = parts[0].shape[1]
    row = lax.broadcasted_iota(jnp.int32, (STAT, n), 0)
    block = jnp.zeros((STAT, n), F32)
    for i, part in enumerate(parts):
        for j, piece in enumerate(split3(part)):
            block = jnp.where(row == 3 * i + j, piece.astype(F32), block)
    return block.astype(BF16)


def stat_of(block, i):
    b = block.astype(F32)
    return b[3 * i : 3 * i + 1] + b[3 * i + 1 : 3 * i + 2] + b[3 * i + 2 : 3 * i + 3]


def opposite_kernel(n_keys, *refs):
    q, m_old, l_old, acc_old, top, bottom = refs[n_keys:]

    def give(_a, _b, values):
        m, total, acc = values
        out = (acc / total).astype(BF16)
        stats = stat_rows([m + jnp.log2(total)])
        top[:HALF] = out[:HALF]
        top[HALF:] = stats
        bottom[:HALF] = out[HALF:]
        bottom[HALF:] = stats

    old = lambda a, b: (m_old[...], l_old[...], acc_old[...])
    softmax_tiles(joined(refs[:n_keys]), [(0, CELLS)], lambda a, b: q[...], old, give)


def opposite(keys, q_far, state):
    rows = sum(k.shape[0] for k in keys)
    return call(
        functools.partial(opposite_kernel, len(keys)),
        [((HALF + STAT, CELLS), BF16)] * 2,
        *keys,
        q_far,
        *state,
        name="opposite",
        flops=4 * rows * CELLS * C,
        nbytes=2e6,
    )


def merge(parts):
    top = functools.reduce(jnp.maximum, [s for s, _ in parts])
    w = [jnp.exp2(s - top) for s, _ in parts]
    total = functools.reduce(jnp.add, w)
    inverse = 1.0 / total
    out = functools.reduce(jnp.add, [(a * inverse) * o for a, (_, o) in zip(w, parts)])
    return top + jnp.log2(total), out


def relay_kernel(from_low, from_high, m, total, acc, _phases, to_low, to_high):
    for side, got, out in ((0, from_high, to_low), (1, from_low, to_high)):
        cols = slice(side * CELLS, (side + 1) * CELLS)
        stat = m[:, cols] + jnp.log2(total[:, cols])
        mine = acc[:, cols] / total[:, cols]
        theirs = (stat_of(got[HALF:], 0), got[:HALF].astype(F32))
        if side == 0:
            stat_t, half_t = stat, mine[:HALF]
            stat_b, half_b = merge([(stat, mine[HALF:]), theirs])
        else:
            stat_t, half_t = merge([(stat, mine[:HALF]), theirs])
            stat_b, half_b = stat, mine[HALF:]
        out[:HALF] = half_t.astype(BF16)
        out[HALF:C] = half_b.astype(BF16)
        out[C:] = stat_rows([stat_t, stat_b])


def finish_kernel(from_low, from_high, m, total, acc, shift, weight, wp, small, block, out):
    c = shift[...]
    stat = m[...] + jnp.log2(total[...]) + c
    mine = acc[...] / total[...]
    halves = []
    for i in range(2):
        rows = slice(i * HALF, (i + 1) * HALF)
        parts = [(stat, mine[rows])] + [
            (stat_of(got[C:], i) + c, got[rows].astype(F32)) for got in (from_low, from_high)
        ]
        halves.append(merge(parts)[1])
    mixed_in = jnp.concatenate(halves, 0).astype(BF16)
    mixed = (dot(mixed_in, weight[:, 2 * C :], ((0,), (0,))) + small[4:5, 2 * C :]).astype(BF16)
    attended = dot(mixed, wp[...], ((1,), (0,))) + small[3:4, :C] + block[...].astype(F32)
    out[...] = attended.astype(BF16)


def pack_kernel(flat, small):
    small[...] = jnp.zeros_like(small)
    at = 0
    for i, n in enumerate((C, C, C, C, 3 * C, OUT)):
        small[i, :n] = flat[at : at + n]
        at += n


def up_phases_kernel(weight, out):
    w = [[weight[b, c].astype(F32) for c in range(3)] for b in range(3)]

    def pairs(a, b, c):
        return ((a, b + c), (a + b, c))

    by_row = [pairs(*(w[b][c] for b in range(3))) for c in range(3)]
    for di in range(2):
        for rt in range(2):
            by_column = pairs(*(by_row[c][di][rt] for c in range(3)))
            for dj in range(2):
                for ct in range(2):
                    value = jnp.concatenate(
                        [by_column[dj][ct], jnp.zeros((256 - OUT, C), F32)], 0
                    )
                    out[di, dj, rt, ct * C : (ct + 1) * C] = value.T.astype(BF16)


def fill_plain(scratch, index, row):
    def store(variant, value):
        scratch[index, :, variant * C : (variant + 1) * C] = value

    col_variants(row.astype(F32), store)


def store_phase(wide, row, dj, value):
    for part in range(2):
        wide[part, row, pl.ds(dj, W, stride=2), :] = value[:, part * 128 : (part + 1) * 128]


def read_row(wide, row):
    return jnp.concatenate([wide[0, row].T, wide[1, row].T[: OUT - 128]], 0)


def up_inner_kernel(body, weight, small, out, edge, scratch, wide):
    for i in range(ROWS):
        fill_plain(scratch, i, body[i])
    b = small[5:6, :256]
    for di in range(2):
        for dj in range(2):
            full = scratch[:, :, dj * C : (dj + 2) * C].reshape(CELLS, 2 * C)
            if di == 0:
                here = dot(full, weight[0, dj, 1], ((1,), (0,))) + b
                beside = dot(full[: 2 * W], weight[0, dj, 0], ((1,), (0,)))
                parts = [here[:W], here[W : 2 * W] + beside[:W], here[2 * W :] + beside[W:]]
            else:
                here = dot(full, weight[1, dj, 0], ((1,), (0,))) + b
                beside = dot(full[W:], weight[1, dj, 1], ((1,), (0,)))
                parts = [here[:W] + beside[:W], here[W : 2 * W] + beside[W:], here[2 * W :]]
            for i, part in enumerate(parts):
                store_phase(wide, 2 * i + di, dj, part)
    for row in range(1, 2 * ROWS - 1):
        out[row] = read_row(wide, row).astype(BF16)
    edge[0] = read_row(wide, 0)
    edge[1] = read_row(wide, 2 * ROWS - 1)


def up_edges_kernel(low, high, weight, edge, _start, out, scratch, wide, rows, sem):
    _, _, above, below = inside()
    for i, (ref, present) in enumerate(((low, above), (high, below))):
        row = ref[0]
        fill_plain(scratch, i, jnp.where(present, row, jnp.zeros_like(row)))
    copies = []
    for side in range(2):
        for dj in range(2):
            left = scratch[side, :, dj * C : (dj + 2) * C]
            store_phase(wide, side, dj, dot(left, weight[side, dj, side], ((1,), (0,))))
        rows[side] = (edge[side] + read_row(wide, side)).astype(BF16)
        row = out.at[side * (2 * ROWS - 1)]
        copies.append(pltpu.make_async_copy(rows.at[side], row, sem.at[side]))
        copies[side].start()
    for copy in copies:
        copy.wait()


def permute_z(value, by):
    pairs = [(x * ZN + z, x * ZN + (z + by) % ZN) for x in range(XN) for z in range(ZN)]
    return lax.ppermute(value, "rows", pairs)


def permute_x(value, by):
    pairs = [(x * ZN + z, (x + by) % XN * ZN + z) for x in range(XN) for z in range(ZN)]
    return lax.ppermute(value, "rows", pairs)


def to_bands(value, by):
    n = XN * ZN
    return lax.ppermute(value, "rows", [(i, (i + by) % n) for i in range(n)])


def on_device(
    latent,
    norm1_gain,
    conv1_weight,
    conv1_bias,
    attention_gain,
    qkv_weight,
    qkv_bias,
    proj_weight,
    proj_bias,
    up_weight,
    up_bias,
):
    own = latent[0]
    two = lax.ppermute(own, "tm", [(t, (t + 2) % TN) for t in range(TN)])
    flat = (norm1_gain, conv1_bias, attention_gain, proj_bias, qkv_bias, up_bias)
    ends = [sum(v.shape[0] for v in flat[: i + 1]) for i in range(len(flat))]
    joined_flat = functools.reduce(
        jnp.add,
        [jnp.pad(v, (end - v.shape[0], ends[-1] - end)) for v, end in zip(flat, ends)],
    )
    small = call(pack_kernel, [((8, 3 * C), F32)], joined_flat, name="pack")
    acc, w_own, w_pair = conv_own(own, small, conv1_weight)
    pairs = [(t, t ^ 1) for t in range(TN)]
    to_next, to_previous, pair = call(
        edge_payload_kernel,
        [((2, W, C), BF16)] * 2 + [((ROWS, W, C), BF16)],
        own,
        two,
        acc,
        name="edge_payload",
        specs=[VM, VM, ANY],
    )
    low, high = to_bands(to_next, 1), to_bands(to_previous, -1)
    one = lax.ppermute(pair, "tm", pairs)
    acc = conv_earlier(two, one, small, w_pair, acc)
    pair_edges = call(
        pair_edges_kernel,
        [((2, W, C), BF16)],
        low,
        high,
        acc,
        name="pair_edges",
        specs=[VM, VM, ANY],
    )
    one_edges = lax.ppermute(pair_edges, "tm", pairs)
    acc = call(
        conv_edges_kernel,
        [((CELLS, C), F32)],
        low,
        high,
        small,
        w_own,
        w_pair,
        acc,
        name="conv_edges",
        flops=2 * CELLS * 2 * C * C,
        scratch=[pltpu.VMEM((4, W, 3 * C), BF16)],
        aliases={5: 0},
    )
    block, normed = call(
        conv_last_kernel,
        [((CELLS, C), BF16)] * 2,
        one_edges,
        own,
        small,
        w_pair,
        acc,
        name="conv_last",
        flops=2 * CELLS * C * C,
        scratch=[pltpu.VMEM((2, W, 3 * C), BF16)],
    )

    up, down = permute_z(normed, 1), permute_z(normed, -1)
    query, shift = call(
        query_kernel,
        [((C, CELLS), BF16), ((1, CELLS), F32)],
        normed,
        qkv_weight,
        small,
        name="queries",
        flops=4 * CELLS * C * C,
    )
    q_low, q_high = permute_x(query, 1), permute_x(query, -1)
    q_far = permute_x(query, 2)
    up2, down2 = permute_z(up, 1), permute_z(down, -1)
    early = [normed, up, down]
    near = [q_low, q_high, query]
    (state,) = attention_step(early, near)
    up2, down2 = after((up2, down2), state[0])
    up3, down3 = permute_z(up2, 1), permute_z(down2, -1)
    (far,) = attention_step(early, [q_far])
    queries = near + [q_far]
    state, far = attention_step([up2, down2], queries, (state, far))
    up4, down4 = permute_z(up3[: CELLS // 2], 1), permute_z(down3[CELLS // 2 :], -1)
    state, far = attention_step([up3, down3], queries, (state, far))
    last = [up4, down4]
    pay_t, pay_b = opposite(last, q_far, far)
    half_low, half_high = permute_x(pay_t, 1), permute_x(pay_b, -1)
    (sides,) = attention_step(last, near, (state,), 0, 2 * CELLS)
    phases = call(
        up_phases_kernel,
        [((2, 2, 2, 2 * C, 256), BF16)],
        up_weight.transpose(0, 1, 3, 2),
        name="up_phases",
        flops=1e7,
        nbytes=4e6,
    )
    to_low, to_high = call(
        relay_kernel,
        [((C + STAT, CELLS), BF16)] * 2,
        half_low,
        half_high,
        *sides,
        phases,
        name="relay",
        specs=[VM] * 5 + [ANY],
    )
    from_low, from_high = permute_x(to_high, 1), permute_x(to_low, -1)
    (mine,) = attention_step(last, near, (state,), 2 * CELLS, 3 * CELLS)
    attended = call(
        finish_kernel,
        [((CELLS, C), BF16)],
        from_low,
        from_high,
        *mine,
        shift,
        qkv_weight,
        proj_weight,
        small,
        block,
        name="finish",
        flops=4 * CELLS * C * C,
    ).reshape(ROWS, W, C)
    edge_low, edge_high = to_bands(attended[2:], 1), to_bands(attended[:1], -1)
    inner, edge = call(
        up_inner_kernel,
        [((2 * ROWS, OUT, 2 * W), BF16), ((2, OUT, 2 * W), F32)],
        attended,
        phases,
        small,
        name="up_inner",
        flops=2 * CELLS * 14 * C * OUT,
        scratch=[
            pltpu.VMEM((ROWS, W, 3 * C), BF16),
            pltpu.VMEM((2, 2 * ROWS, 2 * W, 128), F32),
        ],
    )
    result = call(
        up_edges_kernel,
        [((2 * ROWS, OUT, 2 * W), BF16)],
        edge_low,
        edge_high,
        phases,
        edge,
        inner,
        name="up_edges",
        flops=2 * CELLS * 2 * C * OUT,
        scratch=[
            pltpu.VMEM((2, W, 3 * C), BF16),
            pltpu.VMEM((2, 2, 2 * W, 128), F32),
            pltpu.VMEM((2, OUT, 2 * W), BF16),
            pltpu.SemaphoreType.DMA((2,)),
        ],
        specs=[VM, VM, VM, VM, ANY],
        out_spec=ANY,
        aliases={4: 0},
    )
    return result.transpose(0, 2, 1)[None]


def solution(mesh):
    return jax.shard_map(
        on_device,
        mesh=mesh,
        in_specs=(P("tm", "rows", None, None), P(), P(), P(), P(), P(), P(), P(), P(), P(), P()),
        out_specs=P("tm", "rows", None, None),
        check_vma=False,
    )
```

```python
import functools
import math

import jax
import jax.numpy as jnp
from jax import lax
from jax.experimental import pallas as pl
from jax.experimental.pallas import tpu as pltpu
from jax.sharding import PartitionSpec as P

F32 = jnp.float32
BF16 = jnp.bfloat16
ROWS = 3
W = 128
C = 384
OUT = 192
CELLS = ROWS * W
XN, ZN, TN = 4, 8, 8
QALL = XN * CELLS
HALF = C // 2
STAT = 16
LOG2E = math.log2(math.e)


def dot(a, b, dims):
    return lax.dot_general(a, b, (dims, ((), ())), preferred_element_type=F32)


def params(mib=32):
    return pltpu.CompilerParams(vmem_limit_bytes=mib * 2**20)


def cost(flops, bytes_accessed):
    return pl.CostEstimate(flops=int(flops), bytes_accessed=int(bytes_accessed), transcendentals=0)


VM = pl.BlockSpec(memory_space=pltpu.VMEM)
ANY = pl.BlockSpec(memory_space=pl.ANY)
HBM = pl.BlockSpec(memory_space=pltpu.HBM)


def call(body, outs, *args, name, flops=1e6, nbytes=1e6, aliases=None, scratch=(), mib=32, specs=None, out_spec=VM):
    shapes = [jax.ShapeDtypeStruct(shape, dtype) for shape, dtype in outs]
    result = pl.pallas_call(
        body,
        in_specs=specs or [VM] * len(args),
        out_specs=[out_spec] * len(shapes),
        out_shape=shapes,
        input_output_aliases=aliases or {},
        scratch_shapes=list(scratch),
        compiler_params=params(mib),
        cost_estimate=cost(flops, nbytes),
        name=name,
    )(*args)
    return result[0] if len(shapes) == 1 else result


def col_variants(y, store):
    column = lax.broadcasted_iota(jnp.int32, y.shape, 0)
    before = jnp.where(column == 0, 0.0, pltpu.roll(y, 1, 0))
    after = jnp.where(column == W - 1, 0.0, pltpu.roll(y, W - 1, 0))
    store(0, before.astype(BF16))
    store(1, y.astype(BF16))
    store(2, after.astype(BF16))


def activate(row, gain):
    x = row.astype(F32)
    y = x * lax.rsqrt(jnp.mean(x * x, -1, keepdims=True) + 1e-6) * gain
    y = y / (1.0 + jnp.exp(-y))
    return y.astype(BF16).astype(F32)


def inside():
    frame, band = lax.axis_index("tm"), lax.axis_index("rows")
    return frame >= 2, frame >= 1, band >= 1, band < XN * ZN - 1


def fill_rows(scratch, rows, gain, present=None):
    for index, row in enumerate(rows):
        y = activate(row, gain)
        if present is not None:
            y = jnp.where(present[index], y, 0.0)

        def store(variant, value, index=index):
            scratch[index, :, variant * C : (variant + 1) * C] = value

        col_variants(y, store)


def band_rows(scratch, t, frame, gain, present=None):
    zero = jnp.zeros((W, 3 * C), BF16)
    scratch[t, 0] = zero
    scratch[t, 1 + ROWS] = zero
    present = None if present is None else [present] * ROWS
    fill_rows(scratch.at[t, 1 : 1 + ROWS], [frame[i] for i in range(ROWS)], gain, present)


def band_tap(scratch, t, b, weight):
    left = scratch[t, pl.ds(b, ROWS)].reshape(CELLS, 3 * C)
    return dot(left, weight.reshape(3 * C, C), ((1,), (0,)))


def conv_own_kernel(own, small, weight, acc, beside, earlier, scratch, held, sem, rest_sem):
    def copy(b):
        return pltpu.make_async_copy(weight.at[2, b], held.at[b], sem.at[b])

    for b in range(3):
        copy(b).start()
    rest = [
        pltpu.make_async_copy(weight.at[2, 0], beside.at[0], rest_sem.at[0]),
        pltpu.make_async_copy(weight.at[2, 2], beside.at[1], rest_sem.at[1]),
        pltpu.make_async_copy(weight.at[:2], earlier, rest_sem.at[2]),
    ]
    for one in rest:
        one.start()
    band_rows(scratch, 0, own, small[0:1, :C])
    acc[...] = jnp.zeros((CELLS, C), F32)

    def step(b, carry):
        copy(b).wait()
        acc[...] += band_tap(scratch, 0, b, held[b])
        return carry

    lax.fori_loop(0, 3, step, 0)
    for one in rest:
        one.wait()


def conv_own(own, small, weight):
    return call(
        conv_own_kernel,
        [((CELLS, C), F32), ((2, 3, C, C), BF16), ((2, 3, 3, C, C), BF16)],
        own,
        small,
        weight,
        name="conv_own",
        flops=2 * CELLS * 9 * C * C,
        scratch=[
            pltpu.VMEM((1, ROWS + 2, W, 3 * C), BF16),
            pltpu.VMEM((3, 3, C, C), BF16),
            pltpu.SemaphoreType.DMA((3,)),
            pltpu.SemaphoreType.DMA((3,)),
        ],
        specs=[VM, VM, HBM],
        mib=46,
    )


def conv_earlier_kernel(two, one, small, weight, start, acc, scratch):
    has_two, has_one, _, _ = inside()
    band_rows(scratch, 0, two, small[0:1, :C], has_two)
    band_rows(scratch, 1, one, small[0:1, :C], has_one)
    acc[...] = start[...]

    def step(g, carry):
        t, b = g // 3, g % 3
        acc[...] += band_tap(scratch, t, b, weight[t, b])
        return carry

    lax.fori_loop(0, 6, step, 0)


def conv_earlier(two, one, small, weight, start):
    return call(
        conv_earlier_kernel,
        [((CELLS, C), F32)],
        two,
        one,
        small,
        weight,
        start,
        name="conv_earlier",
        flops=2 * CELLS * 18 * C * C,
        scratch=[pltpu.VMEM((2, ROWS + 2, W, 3 * C), BF16)],
        aliases={4: 0},
    )


def edge_taps(scratch, low, high, first, last):
    left = dot(scratch[low], first[...].reshape(3 * C, C), ((1,), (0,)))
    right = dot(scratch[high], last[...].reshape(3 * C, C), ((1,), (0,)))
    return left, right


def conv_edges_kernel(low, high, small, w_own, w_pair, start, acc, scratch):
    two, _, above, below = inside()
    present = [above, above & two, below, below & two]
    fill_rows(scratch, [low[0], low[1], high[0], high[1]], small[0:1, :C], present)
    own = edge_taps(scratch, 0, 2, w_own.at[0], w_own.at[1])
    two = edge_taps(scratch, 1, 3, w_pair.at[0, 0], w_pair.at[0, 2])
    acc[...] = start[...]
    acc[:W] += own[0] + two[0]
    acc[2 * W :] += own[1] + two[1]


def conv_last_kernel(edges, own, small, weight, start, block, normed, scratch):
    _, one, above, below = inside()
    fill_rows(scratch, [edges[0], edges[1]], small[0:1, :C], [above & one, below & one])
    sides = edge_taps(scratch, 0, 1, weight.at[1, 0], weight.at[1, 2])
    bias, gain2 = small[1:2, :C], small[2:3, :C]
    for i in range(ROWS):
        rows = slice(i * W, (i + 1) * W)
        total = start[rows] + bias
        if i != 1:
            total += sides[i // 2]
        x = (own[i].astype(F32) + total.astype(BF16).astype(F32)).astype(BF16)
        block[rows] = x
        x = x.astype(F32)
        x = x * lax.rsqrt(jnp.mean(x * x, -1, keepdims=True) + 1e-6) * gain2
        normed[rows] = x.astype(BF16)


def edge_payload_kernel(own, two, _acc, to_next, to_previous, pair):
    to_next[0] = own[ROWS - 1]
    to_next[1] = two[ROWS - 1]
    to_previous[0] = own[0]
    to_previous[1] = two[0]

    odd = lax.rem(lax.axis_index("tm"), 2)

    @pl.when(odd == 0)
    def _():
        pair[...] = own[...]

    @pl.when(odd == 1)
    def _():
        pair[...] = two[...]


def pair_edges_kernel(low, high, _acc, out):
    index = lax.rem(lax.axis_index("tm"), 2)
    out[0] = low[index]
    out[1] = high[index]


def query_kernel(normed, weight, small, out, shift):
    scale = C**-0.5 * LOG2E
    wq, wk = weight[:, :C], weight[:, C : 2 * C]
    q = (dot(normed[...], wq, ((1,), (0,))) + small[4:5, :C]).astype(BF16)
    out[...] = (dot(wk, q, ((1,), (1,))) * scale).astype(BF16)
    bk = jnp.broadcast_to(small[4:5, C : 2 * C], (8, C))
    shift[...] = dot(bk, q.astype(F32), ((1,), (1,)))[:1] * scale


def spans(refs, low, high):
    at = 0
    for ref in refs:
        n = ref.shape[1]
        first, last = max(low, at), min(high, at + n)
        if first < last:
            yield ref, first - at, last - at, first - low, last - low
        at += n


def read(refs, low, high):
    pieces = [ref[:, a:b] for ref, a, b, _, _ in spans(refs, low, high)]
    return pieces[0] if len(pieces) == 1 else jnp.concatenate(pieces, 1)


def write(refs, low, high, value):
    for ref, a, b, first, last in spans(refs, low, high):
        ref[:, a:b] = value[:, first:last]


def joined(refs):
    return refs[0][...] if len(refs) == 1 else jnp.concatenate([r[...] for r in refs], 0)


def softmax_tiles(keys, tiles, q_of, old_of, give):
    keys_t = keys.T

    def scores(tile):
        return dot(keys, q_of(*tile), ((1,), (0,)))

    following = scores(tiles[0])
    for i, tile in enumerate(tiles):
        s = following
        if i + 1 < len(tiles):
            following = scores(tiles[i + 1])
        old = old_of(*tile)
        m = jnp.max(s, 0, keepdims=True)
        if old is not None:
            m = jnp.maximum(m, old[0])
        p = jnp.exp2(s - m)
        total = jnp.sum(p, 0, keepdims=True)
        acc = dot(keys_t, p.astype(BF16), ((1,), (0,)))
        if old is not None:
            alpha = jnp.exp2(old[0] - m)
            total = total + alpha * old[1]
            acc = acc + alpha * old[2]
        give(*tile, (m, total, acc))


def tiles_of(low, high, size=512):
    return [(at, min(at + size, high)) for at in range(low, high, size)]


def attention_kernel(n_keys, n_q, n_state, n_out, low, high, *refs):
    keys = joined(refs[:n_keys])
    queries = refs[n_keys : n_keys + n_q]
    state = refs[n_keys + n_q : n_keys + n_q + 3 * n_state]
    outs = refs[n_keys + n_q + 3 * n_state :]

    def old_of(a, b):
        return [read(state[i::3], a, b) for i in range(3)] if n_state else None

    def give(a, b, values):
        for i, value in enumerate(values):
            write(outs[i::3], a - low, b - low, value)

    softmax_tiles(keys, tiles_of(low, high), lambda a, b: read(queries, a, b), old_of, give)


def attention_step(keys, queries, state=(), low=0, high=None):
    widths = [q.shape[1] for q in queries]
    high = sum(widths) if high is None else high
    rows = sum(k.shape[0] for k in keys)
    whole_state = bool(state) and high - low == sum(s[0].shape[1] for s in state)
    outs = [s[0].shape[1] for s in state] if whole_state else [high - low]
    flat = [v for s in state for v in s]
    before = len(keys) + len(queries)
    result = call(
        functools.partial(
            attention_kernel, len(keys), len(queries), len(state), len(outs), low, high
        ),
        [shape for n in outs for shape in (((1, n), F32), ((1, n), F32), ((C, n), F32))],
        *keys,
        *queries,
        *flat,
        name="attention_step",
        flops=4 * rows * (high - low) * C,
        nbytes=6e6,
        aliases={before + i: i for i in range(len(flat))} if whole_state else None,
    )
    return [tuple(result[i : i + 3]) for i in range(0, len(result), 3)]


def gate_kernel(*refs):
    pass


def after(values, *done):
    count = len(values)
    return call(
        gate_kernel,
        [(v.shape, v.dtype) for v in values],
        *values,
        *done,
        name="gate",
        flops=1,
        nbytes=1,
        specs=[ANY] * (count + len(done)),
        out_spec=ANY,
        aliases={i: i for i in range(count)},
    )


def split3(x):
    hi = x.astype(BF16)
    rest = x - hi.astype(F32)
    mid = rest.astype(BF16)
    low = (rest - mid.astype(F32)).astype(BF16)
    return hi, mid, low


def stat_rows(parts):
    n = parts[0].shape[1]
    row = lax.broadcasted_iota(jnp.int32, (STAT, n), 0)
    block = jnp.zeros((STAT, n), F32)
    for i, part in enumerate(parts):
        for j, piece in enumerate(split3(part)):
            block = jnp.where(row == 3 * i + j, piece.astype(F32), block)
    return block.astype(BF16)


def stat_of(block, i):
    b = block.astype(F32)
    return b[3 * i : 3 * i + 1] + b[3 * i + 1 : 3 * i + 2] + b[3 * i + 2 : 3 * i + 3]


def opposite_kernel(n_keys, *refs):
    q, m_old, l_old, acc_old, top, bottom = refs[n_keys:]

    def give(_a, _b, values):
        m, total, acc = values
        out = (acc / total).astype(BF16)
        stats = stat_rows([m + jnp.log2(total)])
        top[:HALF] = out[:HALF]
        top[HALF:] = stats
        bottom[:HALF] = out[HALF:]
        bottom[HALF:] = stats

    old = lambda a, b: (m_old[...], l_old[...], acc_old[...])
    softmax_tiles(joined(refs[:n_keys]), [(0, CELLS)], lambda a, b: q[...], old, give)


def opposite(keys, q_far, state):
    rows = sum(k.shape[0] for k in keys)
    return call(
        functools.partial(opposite_kernel, len(keys)),
        [((HALF + STAT, CELLS), BF16)] * 2,
        *keys,
        q_far,
        *state,
        name="opposite",
        flops=4 * rows * CELLS * C,
        nbytes=2e6,
    )


def merge(parts):
    top = functools.reduce(jnp.maximum, [s for s, _ in parts])
    w = [jnp.exp2(s - top) for s, _ in parts]
    total = functools.reduce(jnp.add, w)
    inverse = 1.0 / total
    out = functools.reduce(jnp.add, [(a * inverse) * o for a, (_, o) in zip(w, parts)])
    return top + jnp.log2(total), out


def relay_kernel(from_low, from_high, m, total, acc, _phases, to_low, to_high):
    for side, got, out in ((0, from_high, to_low), (1, from_low, to_high)):
        cols = slice(side * CELLS, (side + 1) * CELLS)
        stat = m[:, cols] + jnp.log2(total[:, cols])
        mine = acc[:, cols] / total[:, cols]
        theirs = (stat_of(got[HALF:], 0), got[:HALF].astype(F32))
        if side == 0:
            stat_t, half_t = stat, mine[:HALF]
            stat_b, half_b = merge([(stat, mine[HALF:]), theirs])
        else:
            stat_t, half_t = merge([(stat, mine[:HALF]), theirs])
            stat_b, half_b = stat, mine[HALF:]
        out[:HALF] = half_t.astype(BF16)
        out[HALF:C] = half_b.astype(BF16)
        out[C:] = stat_rows([stat_t, stat_b])


def finish_kernel(from_low, from_high, m, total, acc, shift, weight, wp, small, block, out):
    c = shift[...]
    stat = m[...] + jnp.log2(total[...]) + c
    mine = acc[...] / total[...]
    halves = []
    for i in range(2):
        rows = slice(i * HALF, (i + 1) * HALF)
        parts = [(stat, mine[rows])] + [
            (stat_of(got[C:], i) + c, got[rows].astype(F32)) for got in (from_low, from_high)
        ]
        halves.append(merge(parts)[1])
    mixed_in = jnp.concatenate(halves, 0).astype(BF16)
    mixed = (dot(mixed_in, weight[:, 2 * C :], ((0,), (0,))) + small[4:5, 2 * C :]).astype(BF16)
    attended = dot(mixed, wp[...], ((1,), (0,))) + small[3:4, :C] + block[...].astype(F32)
    out[...] = attended.astype(BF16)


def pack_kernel(flat, small):
    small[...] = jnp.zeros_like(small)
    at = 0
    for i, n in enumerate((C, C, C, C, 3 * C, OUT)):
        small[i, :n] = flat[at : at + n]
        at += n


def up_phases_kernel(weight, out):
    w = [[weight[b, c].astype(F32) for c in range(3)] for b in range(3)]

    def pairs(a, b, c):
        return ((a, b + c), (a + b, c))

    by_row = [pairs(*(w[b][c] for b in range(3))) for c in range(3)]
    for di in range(2):
        for rt in range(2):
            by_column = pairs(*(by_row[c][di][rt] for c in range(3)))
            for dj in range(2):
                for ct in range(2):
                    value = jnp.concatenate(
                        [by_column[dj][ct], jnp.zeros((256 - OUT, C), F32)], 0
                    )
                    out[di, dj, rt, ct * C : (ct + 1) * C] = value.T.astype(BF16)


def fill_plain(scratch, index, row):
    def store(variant, value):
        scratch[index, :, variant * C : (variant + 1) * C] = value

    col_variants(row.astype(F32), store)


def store_phase(wide, row, dj, value):
    for part in range(2):
        wide[part, row, pl.ds(dj, W, stride=2), :] = value[:, part * 128 : (part + 1) * 128]


def read_row(wide, row):
    return jnp.concatenate([wide[0, row].T, wide[1, row].T[: OUT - 128]], 0)


def up_inner_kernel(body, weight, small, out, edge, scratch, wide):
    for i in range(ROWS):
        fill_plain(scratch, i, body[i])
    b = small[5:6, :256]
    for di in range(2):
        for dj in range(2):
            full = scratch[:, :, dj * C : (dj + 2) * C].reshape(CELLS, 2 * C)
            if di == 0:
                here = dot(full, weight[0, dj, 1], ((1,), (0,))) + b
                beside = dot(full[: 2 * W], weight[0, dj, 0], ((1,), (0,)))
                parts = [here[:W], here[W : 2 * W] + beside[:W], here[2 * W :] + beside[W:]]
            else:
                here = dot(full, weight[1, dj, 0], ((1,), (0,))) + b
                beside = dot(full[W:], weight[1, dj, 1], ((1,), (0,)))
                parts = [here[:W] + beside[:W], here[W : 2 * W] + beside[W:], here[2 * W :]]
            for i, part in enumerate(parts):
                store_phase(wide, 2 * i + di, dj, part)
    for row in range(1, 2 * ROWS - 1):
        out[row] = read_row(wide, row).astype(BF16)
    edge[0] = read_row(wide, 0)
    edge[1] = read_row(wide, 2 * ROWS - 1)


def up_edges_kernel(low, high, weight, edge, _start, out, scratch, wide, rows, sem):
    _, _, above, below = inside()
    for i, (ref, present) in enumerate(((low, above), (high, below))):
        row = ref[0]
        fill_plain(scratch, i, jnp.where(present, row, jnp.zeros_like(row)))
    copies = []
    for side in range(2):
        for dj in range(2):
            left = scratch[side, :, dj * C : (dj + 2) * C]
            store_phase(wide, side, dj, dot(left, weight[side, dj, side], ((1,), (0,))))
        rows[side] = (edge[side] + read_row(wide, side)).astype(BF16)
        row = out.at[side * (2 * ROWS - 1)]
        copies.append(pltpu.make_async_copy(rows.at[side], row, sem.at[side]))
        copies[side].start()
    for copy in copies:
        copy.wait()


def ring_permute(value, move):
    bands = XN * ZN
    pairs = []
    for t in range(TN):
        sign = 1 if t % 2 == 0 else -1
        for band in range(bands):
            x, z = move(band // ZN, band % ZN, sign)
            pairs.append((t * bands + band, t * bands + x % XN * ZN + z % ZN))
    return lax.ppermute(value, ("tm", "rows"), pairs)


def permute_z(value, by):
    return ring_permute(value, lambda x, z, sign: (x, z + sign * by))


def permute_x(value, by):
    return ring_permute(value, lambda x, z, sign: (x + sign * by, z))


def to_bands(value, by):
    n = XN * ZN
    return lax.ppermute(value, "rows", [(i, (i + by) % n) for i in range(n)])


def on_device(
    latent,
    norm1_gain,
    conv1_weight,
    conv1_bias,
    attention_gain,
    qkv_weight,
    qkv_bias,
    proj_weight,
    proj_bias,
    up_weight,
    up_bias,
):
    own = latent[0]
    two = lax.ppermute(own, "tm", [(t, (t + 2) % TN) for t in range(TN)])
    flat = (norm1_gain, conv1_bias, attention_gain, proj_bias, qkv_bias, up_bias)
    ends = [sum(v.shape[0] for v in flat[: i + 1]) for i in range(len(flat))]
    joined_flat = functools.reduce(
        jnp.add,
        [jnp.pad(v, (end - v.shape[0], ends[-1] - end)) for v, end in zip(flat, ends)],
    )
    small = call(pack_kernel, [((8, 3 * C), F32)], joined_flat, name="pack")
    acc, w_own, w_pair = conv_own(own, small, conv1_weight)
    pairs = [(t, t ^ 1) for t in range(TN)]
    to_next, to_previous, pair = call(
        edge_payload_kernel,
        [((2, W, C), BF16)] * 2 + [((ROWS, W, C), BF16)],
        own,
        two,
        acc,
        name="edge_payload",
        specs=[VM, VM, ANY],
    )
    low, high = to_bands(to_next, 1), to_bands(to_previous, -1)
    one = lax.ppermute(pair, "tm", pairs)
    acc = conv_earlier(two, one, small, w_pair, acc)
    pair_edges = call(
        pair_edges_kernel,
        [((2, W, C), BF16)],
        low,
        high,
        acc,
        name="pair_edges",
        specs=[VM, VM, ANY],
    )
    one_edges = lax.ppermute(pair_edges, "tm", pairs)
    acc = call(
        conv_edges_kernel,
        [((CELLS, C), F32)],
        low,
        high,
        small,
        w_own,
        w_pair,
        acc,
        name="conv_edges",
        flops=2 * CELLS * 2 * C * C,
        scratch=[pltpu.VMEM((4, W, 3 * C), BF16)],
        aliases={5: 0},
    )
    block, normed = call(
        conv_last_kernel,
        [((CELLS, C), BF16)] * 2,
        one_edges,
        own,
        small,
        w_pair,
        acc,
        name="conv_last",
        flops=2 * CELLS * C * C,
        scratch=[pltpu.VMEM((2, W, 3 * C), BF16)],
    )

    up, down = permute_z(normed, 1), permute_z(normed, -1)
    query, shift = call(
        query_kernel,
        [((C, CELLS), BF16), ((1, CELLS), F32)],
        normed,
        qkv_weight,
        small,
        name="queries",
        flops=4 * CELLS * C * C,
    )
    q_low, q_high = permute_x(query, 1), permute_x(query, -1)
    q_far = permute_x(query, 2)
    up2, down2 = permute_z(up, 1), permute_z(down, -1)
    early = [normed, up, down]
    near = [q_low, q_high, query]
    (state,) = attention_step(early, near)
    up2, down2 = after((up2, down2), state[0])
    up3, down3 = permute_z(up2, 1), permute_z(down2, -1)
    (far,) = attention_step(early, [q_far])
    queries = near + [q_far]
    state, far = attention_step([up2, down2], queries, (state, far))
    up4, down4 = permute_z(up3[: CELLS // 2], 1), permute_z(down3[CELLS // 2 :], -1)
    state, far = attention_step([up3, down3], queries, (state, far))
    last = [up4, down4]
    pay_t, pay_b = opposite(last, q_far, far)
    half_low, half_high = permute_x(pay_t, 1), permute_x(pay_b, -1)
    (sides,) = attention_step(last, near, (state,), 0, 2 * CELLS)
    phases = call(
        up_phases_kernel,
        [((2, 2, 2, 2 * C, 256), BF16)],
        up_weight.transpose(0, 1, 3, 2),
        name="up_phases",
        flops=1e7,
        nbytes=4e6,
    )
    to_low, to_high = call(
        relay_kernel,
        [((C + STAT, CELLS), BF16)] * 2,
        half_low,
        half_high,
        *sides,
        phases,
        name="relay",
        specs=[VM] * 5 + [ANY],
    )
    from_low, from_high = permute_x(to_high, 1), permute_x(to_low, -1)
    (mine,) = attention_step(last, near, (state,), 2 * CELLS, 3 * CELLS)
    attended = call(
        finish_kernel,
        [((CELLS, C), BF16)],
        from_low,
        from_high,
        *mine,
        shift,
        qkv_weight,
        proj_weight,
        small,
        block,
        name="finish",
        flops=4 * CELLS * C * C,
    ).reshape(ROWS, W, C)
    edge_low, edge_high = to_bands(attended[2:], 1), to_bands(attended[:1], -1)
    inner, edge = call(
        up_inner_kernel,
        [((2 * ROWS, OUT, 2 * W), BF16), ((2, OUT, 2 * W), F32)],
        attended,
        phases,
        small,
        name="up_inner",
        flops=2 * CELLS * 14 * C * OUT,
        scratch=[
            pltpu.VMEM((ROWS, W, 3 * C), BF16),
            pltpu.VMEM((2, 2 * ROWS, 2 * W, 128), F32),
        ],
    )
    result = call(
        up_edges_kernel,
        [((2 * ROWS, OUT, 2 * W), BF16)],
        edge_low,
        edge_high,
        phases,
        edge,
        inner,
        name="up_edges",
        flops=2 * CELLS * 2 * C * OUT,
        scratch=[
            pltpu.VMEM((2, W, 3 * C), BF16),
            pltpu.VMEM((2, 2, 2 * W, 128), F32),
            pltpu.VMEM((2, OUT, 2 * W), BF16),
            pltpu.SemaphoreType.DMA((2,)),
        ],
        specs=[VM, VM, VM, VM, ANY],
        out_spec=ANY,
        aliases={4: 0},
    )
    return result.transpose(0, 2, 1)[None]


def solution(mesh):
    return jax.shard_map(
        on_device,
        mesh=mesh,
        in_specs=(P("tm", "rows", None, None), P(), P(), P(), P(), P(), P(), P(), P(), P(), P()),
        out_specs=P("tm", "rows", None, None),
        check_vma=False,
    )
```

```python
import functools
import math

import jax
import jax.numpy as jnp
from jax import lax
from jax.experimental import pallas as pl
from jax.experimental.pallas import tpu as pltpu
from jax.sharding import PartitionSpec as P

F32 = jnp.float32
BF16 = jnp.bfloat16
ROWS = 3
W = 128
C = 384
OUT = 192
CELLS = ROWS * W
XN, ZN, TN = 4, 8, 8
QALL = XN * CELLS
HALF = C // 2
STAT = 16
LOG2E = math.log2(math.e)


def dot(a, b, dims):
    return lax.dot_general(a, b, (dims, ((), ())), preferred_element_type=F32)


def params(mib=32):
    return pltpu.CompilerParams(vmem_limit_bytes=mib * 2**20)


def cost(flops, bytes_accessed):
    return pl.CostEstimate(flops=int(flops), bytes_accessed=int(bytes_accessed), transcendentals=0)


VM = pl.BlockSpec(memory_space=pltpu.VMEM)
ANY = pl.BlockSpec(memory_space=pl.ANY)
HBM = pl.BlockSpec(memory_space=pltpu.HBM)


def call(body, outs, *args, name, flops=1e6, nbytes=1e6, aliases=None, scratch=(), mib=32, specs=None, out_spec=VM):
    shapes = [jax.ShapeDtypeStruct(shape, dtype) for shape, dtype in outs]
    result = pl.pallas_call(
        body,
        in_specs=specs or [VM] * len(args),
        out_specs=[out_spec] * len(shapes),
        out_shape=shapes,
        input_output_aliases=aliases or {},
        scratch_shapes=list(scratch),
        compiler_params=params(mib),
        cost_estimate=cost(flops, nbytes),
        name=name,
    )(*args)
    return result[0] if len(shapes) == 1 else result


def col_variants(y, store):
    column = lax.broadcasted_iota(jnp.int32, y.shape, 0)
    before = jnp.where(column == 0, 0.0, pltpu.roll(y, 1, 0))
    after = jnp.where(column == W - 1, 0.0, pltpu.roll(y, W - 1, 0))
    store(0, before.astype(BF16))
    store(1, y.astype(BF16))
    store(2, after.astype(BF16))


def activate(row, gain):
    x = row.astype(F32)
    y = x * lax.rsqrt(jnp.mean(x * x, -1, keepdims=True) + 1e-6) * gain
    y = y / (1.0 + jnp.exp(-y))
    return y.astype(BF16).astype(F32)


def inside():
    frame, band = lax.axis_index("tm"), lax.axis_index("rows")
    return frame >= 2, frame >= 1, band >= 1, band < XN * ZN - 1


def fill_rows(scratch, rows, gain, present=None):
    for index, row in enumerate(rows):
        y = activate(row, gain)
        if present is not None:
            y = jnp.where(present[index], y, 0.0)

        def store(variant, value, index=index):
            scratch[index, :, variant * C : (variant + 1) * C] = value

        col_variants(y, store)


def band_rows(scratch, t, frame, gain, present=None):
    zero = jnp.zeros((W, 3 * C), BF16)
    scratch[t, 0] = zero
    scratch[t, 1 + ROWS] = zero
    present = None if present is None else [present] * ROWS
    fill_rows(scratch.at[t, 1 : 1 + ROWS], [frame[i] for i in range(ROWS)], gain, present)


def band_tap(scratch, t, b, weight):
    left = scratch[t, pl.ds(b, ROWS)].reshape(CELLS, 3 * C)
    return dot(left, weight.reshape(3 * C, C), ((1,), (0,)))


def conv_own_kernel(own, small, weight, acc, beside, earlier, scratch, held, sem, rest_sem):
    def copy(b):
        return pltpu.make_async_copy(weight.at[2, b], held.at[b], sem.at[b])

    for b in range(3):
        copy(b).start()
    rest = [
        pltpu.make_async_copy(weight.at[2, 0], beside.at[0], rest_sem.at[0]),
        pltpu.make_async_copy(weight.at[2, 2], beside.at[1], rest_sem.at[1]),
        pltpu.make_async_copy(weight.at[:2], earlier, rest_sem.at[2]),
    ]
    for one in rest:
        one.start()
    band_rows(scratch, 0, own, small[0:1, :C])
    acc[...] = jnp.zeros((CELLS, C), F32)

    def step(b, carry):
        copy(b).wait()
        acc[...] += band_tap(scratch, 0, b, held[b])
        return carry

    lax.fori_loop(0, 3, step, 0)
    for one in rest:
        one.wait()


def conv_own(own, small, weight):
    return call(
        conv_own_kernel,
        [((CELLS, C), F32), ((2, 3, C, C), BF16), ((2, 3, 3, C, C), BF16)],
        own,
        small,
        weight,
        name="conv_own",
        flops=2 * CELLS * 9 * C * C,
        scratch=[
            pltpu.VMEM((1, ROWS + 2, W, 3 * C), BF16),
            pltpu.VMEM((3, 3, C, C), BF16),
            pltpu.SemaphoreType.DMA((3,)),
            pltpu.SemaphoreType.DMA((3,)),
        ],
        specs=[VM, VM, HBM],
        mib=46,
    )


def conv_earlier_kernel(two, one, small, weight, start, acc, scratch):
    has_two, has_one, _, _ = inside()
    band_rows(scratch, 0, two, small[0:1, :C], has_two)
    band_rows(scratch, 1, one, small[0:1, :C], has_one)
    acc[...] = start[...]

    def step(g, carry):
        t, b = g // 3, g % 3
        acc[...] += band_tap(scratch, t, b, weight[t, b])
        return carry

    lax.fori_loop(0, 6, step, 0)


def conv_earlier(two, one, small, weight, start):
    return call(
        conv_earlier_kernel,
        [((CELLS, C), F32)],
        two,
        one,
        small,
        weight,
        start,
        name="conv_earlier",
        flops=2 * CELLS * 18 * C * C,
        scratch=[pltpu.VMEM((2, ROWS + 2, W, 3 * C), BF16)],
        aliases={4: 0},
    )


def edge_taps(scratch, low, high, first, last):
    left = dot(scratch[low], first[...].reshape(3 * C, C), ((1,), (0,)))
    right = dot(scratch[high], last[...].reshape(3 * C, C), ((1,), (0,)))
    return left, right


def conv_edges_kernel(low, high, small, w_own, w_pair, start, acc, scratch):
    two, _, above, below = inside()
    present = [above, above & two, below, below & two]
    fill_rows(scratch, [low[0], low[1], high[0], high[1]], small[0:1, :C], present)
    own = edge_taps(scratch, 0, 2, w_own.at[0], w_own.at[1])
    two = edge_taps(scratch, 1, 3, w_pair.at[0, 0], w_pair.at[0, 2])
    acc[...] = start[...]
    acc[:W] += own[0] + two[0]
    acc[2 * W :] += own[1] + two[1]


def conv_last_kernel(edges, own, small, weight, start, up, block, normed, phases, scratch):
    _, one, above, below = inside()
    fill_rows(scratch, [edges[0], edges[1]], small[0:1, :C], [above & one, below & one])
    sides = edge_taps(scratch, 0, 1, weight.at[1, 0], weight.at[1, 2])
    bias, gain2 = small[1:2, :C], small[2:3, :C]
    for i in range(ROWS):
        rows = slice(i * W, (i + 1) * W)
        total = start[rows] + bias
        if i != 1:
            total += sides[i // 2]
        x = (own[i].astype(F32) + total.astype(BF16).astype(F32)).astype(BF16)
        block[rows] = x
        x = x.astype(F32)
        x = x * lax.rsqrt(jnp.mean(x * x, -1, keepdims=True) + 1e-6) * gain2
        normed[rows] = x.astype(BF16)

    @pl.when(lax.rem(lax.axis_index("tm"), 2) == 0)
    def _():
        up_phases(up, phases)


def edge_payload_kernel(own, two, _acc, to_next, to_previous, pair):
    to_next[0] = own[ROWS - 1]
    to_next[1] = two[ROWS - 1]
    to_previous[0] = own[0]
    to_previous[1] = two[0]

    odd = lax.rem(lax.axis_index("tm"), 2)

    @pl.when(odd == 0)
    def _():
        pair[...] = own[...]

    @pl.when(odd == 1)
    def _():
        pair[...] = two[...]


def pair_edges_kernel(low, high, _acc, out):
    index = lax.rem(lax.axis_index("tm"), 2)
    out[0] = low[index]
    out[1] = high[index]


def query_kernel(normed, weight, small, out, shift):
    scale = C**-0.5 * LOG2E
    wq, wk = weight[:, :C], weight[:, C : 2 * C]
    q = (dot(normed[...], wq, ((1,), (0,))) + small[4:5, :C]).astype(BF16)
    out[...] = (dot(wk, q, ((1,), (1,))) * scale).astype(BF16)
    bk = jnp.broadcast_to(small[4:5, C : 2 * C], (8, C))
    shift[...] = dot(bk, q.astype(F32), ((1,), (1,)))[:1] * scale


def spans(refs, low, high):
    at = 0
    for ref in refs:
        n = ref.shape[1]
        first, last = max(low, at), min(high, at + n)
        if first < last:
            yield ref, first - at, last - at, first - low, last - low
        at += n


def read(refs, low, high):
    pieces = [ref[:, a:b] for ref, a, b, _, _ in spans(refs, low, high)]
    return pieces[0] if len(pieces) == 1 else jnp.concatenate(pieces, 1)


def write(refs, low, high, value):
    for ref, a, b, first, last in spans(refs, low, high):
        ref[:, a:b] = value[:, first:last]


def joined(refs):
    return refs[0][...] if len(refs) == 1 else jnp.concatenate([r[...] for r in refs], 0)


def softmax_tiles(keys, tiles, q_of, old_of, give):
    keys_t = keys.T

    def scores(tile):
        return dot(keys, q_of(*tile), ((1,), (0,)))

    following = scores(tiles[0])
    for i, tile in enumerate(tiles):
        s = following
        if i + 1 < len(tiles):
            following = scores(tiles[i + 1])
        old = old_of(*tile)
        m = jnp.max(s, 0, keepdims=True)
        if old is not None:
            m = jnp.maximum(m, old[0])
        p = jnp.exp2(s - m)
        total = jnp.sum(p, 0, keepdims=True)
        acc = dot(keys_t, p.astype(BF16), ((1,), (0,)))
        if old is not None:
            alpha = jnp.exp2(old[0] - m)
            total = total + alpha * old[1]
            acc = acc + alpha * old[2]
        give(*tile, (m, total, acc))


def tiles_of(low, high, size=512):
    return [(at, min(at + size, high)) for at in range(low, high, size)]


def attention_kernel(n_keys, n_q, n_state, n_out, low, high, *refs):
    keys = joined(refs[:n_keys])
    queries = refs[n_keys : n_keys + n_q]
    state = refs[n_keys + n_q : n_keys + n_q + 3 * n_state]
    outs = refs[n_keys + n_q + 3 * n_state :]

    def old_of(a, b):
        return [read(state[i::3], a, b) for i in range(3)] if n_state else None

    def give(a, b, values):
        for i, value in enumerate(values):
            write(outs[i::3], a - low, b - low, value)

    softmax_tiles(keys, tiles_of(low, high), lambda a, b: read(queries, a, b), old_of, give)


def attention_step(keys, queries, state=(), low=0, high=None):
    widths = [q.shape[1] for q in queries]
    high = sum(widths) if high is None else high
    rows = sum(k.shape[0] for k in keys)
    whole_state = bool(state) and high - low == sum(s[0].shape[1] for s in state)
    outs = [s[0].shape[1] for s in state] if whole_state else [high - low]
    flat = [v for s in state for v in s]
    before = len(keys) + len(queries)
    result = call(
        functools.partial(
            attention_kernel, len(keys), len(queries), len(state), len(outs), low, high
        ),
        [shape for n in outs for shape in (((1, n), F32), ((1, n), F32), ((C, n), F32))],
        *keys,
        *queries,
        *flat,
        name="attention_step",
        flops=4 * rows * (high - low) * C,
        nbytes=6e6,
        aliases={before + i: i for i in range(len(flat))} if whole_state else None,
    )
    return [tuple(result[i : i + 3]) for i in range(0, len(result), 3)]


def gate_kernel(*refs):
    pass


def after(values, *done):
    count = len(values)
    return call(
        gate_kernel,
        [(v.shape, v.dtype) for v in values],
        *values,
        *done,
        name="gate",
        flops=1,
        nbytes=1,
        specs=[ANY] * (count + len(done)),
        out_spec=ANY,
        aliases={i: i for i in range(count)},
    )


def split3(x):
    hi = x.astype(BF16)
    rest = x - hi.astype(F32)
    mid = rest.astype(BF16)
    low = (rest - mid.astype(F32)).astype(BF16)
    return hi, mid, low


def stat_rows(parts):
    n = parts[0].shape[1]
    row = lax.broadcasted_iota(jnp.int32, (STAT, n), 0)
    block = jnp.zeros((STAT, n), F32)
    for i, part in enumerate(parts):
        for j, piece in enumerate(split3(part)):
            block = jnp.where(row == 3 * i + j, piece.astype(F32), block)
    return block.astype(BF16)


def stat_of(block, i):
    b = block.astype(F32)
    return b[3 * i : 3 * i + 1] + b[3 * i + 1 : 3 * i + 2] + b[3 * i + 2 : 3 * i + 3]


def opposite_kernel(n_keys, *refs):
    q, m_old, l_old, acc_old, top, bottom = refs[n_keys:]

    def give(_a, _b, values):
        m, total, acc = values
        out = (acc / total).astype(BF16)
        stats = stat_rows([m + jnp.log2(total)])
        top[:HALF] = out[:HALF]
        top[HALF:] = stats
        bottom[:HALF] = out[HALF:]
        bottom[HALF:] = stats

    old = lambda a, b: (m_old[...], l_old[...], acc_old[...])
    softmax_tiles(joined(refs[:n_keys]), [(0, CELLS)], lambda a, b: q[...], old, give)


def opposite(keys, q_far, state):
    rows = sum(k.shape[0] for k in keys)
    return call(
        functools.partial(opposite_kernel, len(keys)),
        [((HALF + STAT, CELLS), BF16)] * 2,
        *keys,
        q_far,
        *state,
        name="opposite",
        flops=4 * rows * CELLS * C,
        nbytes=2e6,
    )


def merge(parts):
    top = functools.reduce(jnp.maximum, [s for s, _ in parts])
    w = [jnp.exp2(s - top) for s, _ in parts]
    total = functools.reduce(jnp.add, w)
    inverse = 1.0 / total
    out = functools.reduce(jnp.add, [(a * inverse) * o for a, (_, o) in zip(w, parts)])
    return top + jnp.log2(total), out


def relay_kernel(from_low, from_high, m, total, acc, _phases, to_low, to_high):
    for side, got, out in ((0, from_high, to_low), (1, from_low, to_high)):
        cols = slice(side * CELLS, (side + 1) * CELLS)
        stat = m[:, cols] + jnp.log2(total[:, cols])
        mine = acc[:, cols] / total[:, cols]
        theirs = (stat_of(got[HALF:], 0), got[:HALF].astype(F32))
        if side == 0:
            stat_t, half_t = stat, mine[:HALF]
            stat_b, half_b = merge([(stat, mine[HALF:]), theirs])
        else:
            stat_t, half_t = merge([(stat, mine[:HALF]), theirs])
            stat_b, half_b = stat, mine[HALF:]
        out[:HALF] = half_t.astype(BF16)
        out[HALF:C] = half_b.astype(BF16)
        out[C:] = stat_rows([stat_t, stat_b])


def finish_kernel(from_low, from_high, m, total, acc, shift, weight, wp, small, block, out):
    c = shift[...]
    stat = m[...] + jnp.log2(total[...]) + c
    mine = acc[...] / total[...]
    halves = []
    for i in range(2):
        rows = slice(i * HALF, (i + 1) * HALF)
        parts = [(stat, mine[rows])] + [
            (stat_of(got[C:], i) + c, got[rows].astype(F32)) for got in (from_low, from_high)
        ]
        halves.append(merge(parts)[1])
    mixed_in = jnp.concatenate(halves, 0).astype(BF16)
    mixed = (dot(mixed_in, weight[:, 2 * C :], ((0,), (0,))) + small[4:5, 2 * C :]).astype(BF16)
    attended = dot(mixed, wp[...], ((1,), (0,))) + small[3:4, :C] + block[...].astype(F32)
    out[...] = attended.astype(BF16)


def pack_kernel(flat, small):
    small[...] = jnp.zeros_like(small)
    at = 0
    for i, n in enumerate((C, C, C, C, 3 * C, OUT)):
        small[i, :n] = flat[at : at + n]
        at += n


def up_phases(weight, out):
    w = [[weight[b, c].astype(F32) for c in range(3)] for b in range(3)]

    def pairs(a, b, c):
        return ((a, b + c), (a + b, c))

    by_row = [pairs(*(w[b][c] for b in range(3))) for c in range(3)]
    for di in range(2):
        for rt in range(2):
            by_column = pairs(*(by_row[c][di][rt] for c in range(3)))
            for dj in range(2):
                for ct in range(2):
                    value = jnp.concatenate(
                        [by_column[dj][ct], jnp.zeros((256 - OUT, C), F32)], 0
                    )
                    out[di, dj, rt, ct * C : (ct + 1) * C] = value.T.astype(BF16)


def up_phases_kernel(weight, early, out):
    odd = lax.rem(lax.axis_index("tm"), 2)

    @pl.when(odd == 0)
    def _():
        out[...] = early[...]

    @pl.when(odd == 1)
    def _():
        up_phases(weight, out)


def fill_plain(scratch, index, row):
    def store(variant, value):
        scratch[index, :, variant * C : (variant + 1) * C] = value

    col_variants(row.astype(F32), store)


def store_phase(wide, row, dj, value):
    for part in range(2):
        wide[part, row, pl.ds(dj, W, stride=2), :] = value[:, part * 128 : (part + 1) * 128]


def read_row(wide, row):
    return jnp.concatenate([wide[0, row].T, wide[1, row].T[: OUT - 128]], 0)


def up_inner_kernel(body, weight, small, out, edge, scratch, wide):
    for i in range(ROWS):
        fill_plain(scratch, i, body[i])
    b = small[5:6, :256]
    for di in range(2):
        for dj in range(2):
            full = scratch[:, :, dj * C : (dj + 2) * C].reshape(CELLS, 2 * C)
            if di == 0:
                here = dot(full, weight[0, dj, 1], ((1,), (0,))) + b
                beside = dot(full[: 2 * W], weight[0, dj, 0], ((1,), (0,)))
                parts = [here[:W], here[W : 2 * W] + beside[:W], here[2 * W :] + beside[W:]]
            else:
                here = dot(full, weight[1, dj, 0], ((1,), (0,))) + b
                beside = dot(full[W:], weight[1, dj, 1], ((1,), (0,)))
                parts = [here[:W] + beside[:W], here[W : 2 * W] + beside[W:], here[2 * W :]]
            for i, part in enumerate(parts):
                store_phase(wide, 2 * i + di, dj, part)
    for row in range(1, 2 * ROWS - 1):
        out[row] = read_row(wide, row).astype(BF16)
    edge[0] = read_row(wide, 0)
    edge[1] = read_row(wide, 2 * ROWS - 1)


def up_edges_kernel(low, high, weight, edge, _start, out, scratch, wide, rows, sem):
    _, _, above, below = inside()
    for i, (ref, present) in enumerate(((low, above), (high, below))):
        row = ref[0]
        fill_plain(scratch, i, jnp.where(present, row, jnp.zeros_like(row)))
    copies = []
    for side in range(2):
        for dj in range(2):
            left = scratch[side, :, dj * C : (dj + 2) * C]
            store_phase(wide, side, dj, dot(left, weight[side, dj, side], ((1,), (0,))))
        rows[side] = (edge[side] + read_row(wide, side)).astype(BF16)
        row = out.at[side * (2 * ROWS - 1)]
        copies.append(pltpu.make_async_copy(rows.at[side], row, sem.at[side]))
        copies[side].start()
    for copy in copies:
        copy.wait()


def permute_z(value, by):
    pairs = [(x * ZN + z, x * ZN + (z + by) % ZN) for x in range(XN) for z in range(ZN)]
    return lax.ppermute(value, "rows", pairs)


def permute_x(value, by):
    pairs = [(x * ZN + z, (x + by) % XN * ZN + z) for x in range(XN) for z in range(ZN)]
    return lax.ppermute(value, "rows", pairs)


def to_bands(value, by):
    n = XN * ZN
    return lax.ppermute(value, "rows", [(i, (i + by) % n) for i in range(n)])


def on_device(
    latent,
    norm1_gain,
    conv1_weight,
    conv1_bias,
    attention_gain,
    qkv_weight,
    qkv_bias,
    proj_weight,
    proj_bias,
    up_weight,
    up_bias,
):
    own = latent[0]
    two = lax.ppermute(own, "tm", [(t, (t + 2) % TN) for t in range(TN)])
    flat = (norm1_gain, conv1_bias, attention_gain, proj_bias, qkv_bias, up_bias)
    ends = [sum(v.shape[0] for v in flat[: i + 1]) for i in range(len(flat))]
    joined_flat = functools.reduce(
        jnp.add,
        [jnp.pad(v, (end - v.shape[0], ends[-1] - end)) for v, end in zip(flat, ends)],
    )
    small = call(pack_kernel, [((8, 3 * C), F32)], joined_flat, name="pack")
    acc, w_own, w_pair = conv_own(own, small, conv1_weight)
    pairs = [(t, t ^ 1) for t in range(TN)]
    to_next, to_previous, pair = call(
        edge_payload_kernel,
        [((2, W, C), BF16)] * 2 + [((ROWS, W, C), BF16)],
        own,
        two,
        acc,
        name="edge_payload",
        specs=[VM, VM, ANY],
    )
    low, high = to_bands(to_next, 1), to_bands(to_previous, -1)
    one = lax.ppermute(pair, "tm", pairs)
    acc = conv_earlier(two, one, small, w_pair, acc)
    pair_edges = call(
        pair_edges_kernel,
        [((2, W, C), BF16)],
        low,
        high,
        acc,
        name="pair_edges",
        specs=[VM, VM, ANY],
    )
    one_edges = lax.ppermute(pair_edges, "tm", pairs)
    acc = call(
        conv_edges_kernel,
        [((CELLS, C), F32)],
        low,
        high,
        small,
        w_own,
        w_pair,
        acc,
        name="conv_edges",
        flops=2 * CELLS * 2 * C * C,
        scratch=[pltpu.VMEM((4, W, 3 * C), BF16)],
        aliases={5: 0},
    )
    up_transposed = up_weight.transpose(0, 1, 3, 2)
    phases_shape = ((2, 2, 2, 2 * C, 256), BF16)
    block, normed, early_phases = call(
        conv_last_kernel,
        [((CELLS, C), BF16)] * 2 + [phases_shape],
        one_edges,
        own,
        small,
        w_pair,
        acc,
        up_transposed,
        name="conv_last",
        flops=2 * CELLS * C * C,
        scratch=[pltpu.VMEM((2, W, 3 * C), BF16)],
    )

    up, down = permute_z(normed, 1), permute_z(normed, -1)
    query, shift = call(
        query_kernel,
        [((C, CELLS), BF16), ((1, CELLS), F32)],
        normed,
        qkv_weight,
        small,
        name="queries",
        flops=4 * CELLS * C * C,
    )
    q_low, q_high = permute_x(query, 1), permute_x(query, -1)
    q_far = permute_x(query, 2)
    up2, down2 = permute_z(up, 1), permute_z(down, -1)
    early = [normed, up, down]
    near = [q_low, q_high, query]
    (state,) = attention_step(early, near)
    up2, down2 = after((up2, down2), state[0])
    up3, down3 = permute_z(up2, 1), permute_z(down2, -1)
    (far,) = attention_step(early, [q_far])
    queries = near + [q_far]
    state, far = attention_step([up2, down2], queries, (state, far))
    up4, down4 = permute_z(up3[: CELLS // 2], 1), permute_z(down3[CELLS // 2 :], -1)
    state, far = attention_step([up3, down3], queries, (state, far))
    last = [up4, down4]
    pay_t, pay_b = opposite(last, q_far, far)
    half_low, half_high = permute_x(pay_t, 1), permute_x(pay_b, -1)
    (sides,) = attention_step(last, near, (state,), 0, 2 * CELLS)
    phases = call(
        up_phases_kernel,
        [phases_shape],
        up_transposed,
        early_phases,
        name="up_phases",
        flops=1e7,
        nbytes=4e6,
    )
    to_low, to_high = call(
        relay_kernel,
        [((C + STAT, CELLS), BF16)] * 2,
        half_low,
        half_high,
        *sides,
        phases,
        name="relay",
        specs=[VM] * 5 + [ANY],
    )
    from_low, from_high = permute_x(to_high, 1), permute_x(to_low, -1)
    (mine,) = attention_step(last, near, (state,), 2 * CELLS, 3 * CELLS)
    attended = call(
        finish_kernel,
        [((CELLS, C), BF16)],
        from_low,
        from_high,
        *mine,
        shift,
        qkv_weight,
        proj_weight,
        small,
        block,
        name="finish",
        flops=4 * CELLS * C * C,
    ).reshape(ROWS, W, C)
    edge_low, edge_high = to_bands(attended[2:], 1), to_bands(attended[:1], -1)
    inner, edge = call(
        up_inner_kernel,
        [((2 * ROWS, OUT, 2 * W), BF16), ((2, OUT, 2 * W), F32)],
        attended,
        phases,
        small,
        name="up_inner",
        flops=2 * CELLS * 14 * C * OUT,
        scratch=[
            pltpu.VMEM((ROWS, W, 3 * C), BF16),
            pltpu.VMEM((2, 2 * ROWS, 2 * W, 128), F32),
        ],
    )
    result = call(
        up_edges_kernel,
        [((2 * ROWS, OUT, 2 * W), BF16)],
        edge_low,
        edge_high,
        phases,
        edge,
        inner,
        name="up_edges",
        flops=2 * CELLS * 2 * C * OUT,
        scratch=[
            pltpu.VMEM((2, W, 3 * C), BF16),
            pltpu.VMEM((2, 2, 2 * W, 128), F32),
            pltpu.VMEM((2, OUT, 2 * W), BF16),
            pltpu.SemaphoreType.DMA((2,)),
        ],
        specs=[VM, VM, VM, VM, ANY],
        out_spec=ANY,
        aliases={4: 0},
    )
    return result.transpose(0, 2, 1)[None]


def solution(mesh):
    return jax.shard_map(
        on_device,
        mesh=mesh,
        in_specs=(P("tm", "rows", None, None), P(), P(), P(), P(), P(), P(), P(), P(), P(), P()),
        out_specs=P("tm", "rows", None, None),
        check_vma=False,
    )
```

```python
import functools
import math

import jax
import jax.numpy as jnp
from jax import lax
from jax.experimental import pallas as pl
from jax.experimental.pallas import tpu as pltpu
from jax.sharding import PartitionSpec as P

F32 = jnp.float32
BF16 = jnp.bfloat16
ROWS = 3
W = 128
C = 384
OUT = 192
CELLS = ROWS * W
XN, ZN, TN = 4, 8, 8
QALL = XN * CELLS
HALF = C // 2
STAT = 16
LOG2E = math.log2(math.e)


def dot(a, b, dims):
    return lax.dot_general(a, b, (dims, ((), ())), preferred_element_type=F32)


def params(mib=32):
    return pltpu.CompilerParams(vmem_limit_bytes=mib * 2**20)


def cost(flops, bytes_accessed):
    return pl.CostEstimate(flops=int(flops), bytes_accessed=int(bytes_accessed), transcendentals=0)


VM = pl.BlockSpec(memory_space=pltpu.VMEM)
ANY = pl.BlockSpec(memory_space=pl.ANY)
HBM = pl.BlockSpec(memory_space=pltpu.HBM)


def call(body, outs, *args, name, flops=1e6, nbytes=1e6, aliases=None, scratch=(), mib=32, specs=None, out_spec=VM):
    shapes = [jax.ShapeDtypeStruct(shape, dtype) for shape, dtype in outs]
    result = pl.pallas_call(
        body,
        in_specs=specs or [VM] * len(args),
        out_specs=[out_spec] * len(shapes),
        out_shape=shapes,
        input_output_aliases=aliases or {},
        scratch_shapes=list(scratch),
        compiler_params=params(mib),
        cost_estimate=cost(flops, nbytes),
        name=name,
    )(*args)
    return result[0] if len(shapes) == 1 else result


def col_variants(y, store):
    column = lax.broadcasted_iota(jnp.int32, y.shape, 0)
    before = jnp.where(column == 0, 0.0, pltpu.roll(y, 1, 0))
    after = jnp.where(column == W - 1, 0.0, pltpu.roll(y, W - 1, 0))
    store(0, before.astype(BF16))
    store(1, y.astype(BF16))
    store(2, after.astype(BF16))


def activate(row, gain):
    x = row.astype(F32)
    y = x * lax.rsqrt(jnp.mean(x * x, -1, keepdims=True) + 1e-6) * gain
    y = y / (1.0 + jnp.exp(-y))
    return y.astype(BF16).astype(F32)


def inside():
    frame, band = lax.axis_index("tm"), lax.axis_index("rows")
    return frame >= 2, frame >= 1, band >= 1, band < XN * ZN - 1


def fill_rows(scratch, rows, gain, present=None):
    for index, row in enumerate(rows):
        y = activate(row, gain)
        if present is not None:
            y = jnp.where(present[index], y, 0.0)

        def store(variant, value, index=index):
            scratch[index, :, variant * C : (variant + 1) * C] = value

        col_variants(y, store)


def band_rows(scratch, t, frame, gain, present=None):
    zero = jnp.zeros((W, 3 * C), BF16)
    scratch[t, 0] = zero
    scratch[t, 1 + ROWS] = zero
    present = None if present is None else [present] * ROWS
    fill_rows(scratch.at[t, 1 : 1 + ROWS], [frame[i] for i in range(ROWS)], gain, present)


def band_tap(scratch, t, b, weight):
    left = scratch[t, pl.ds(b, ROWS)].reshape(CELLS, 3 * C)
    return dot(left, weight.reshape(3 * C, C), ((1,), (0,)))


def conv_own_kernel(own, small, weight, acc, beside, earlier, scratch, held, sem, rest_sem):
    def copy(b):
        return pltpu.make_async_copy(weight.at[2, b], held.at[b], sem.at[b])

    for b in range(3):
        copy(b).start()
    rest = [
        pltpu.make_async_copy(weight.at[2, 0], beside.at[0], rest_sem.at[0]),
        pltpu.make_async_copy(weight.at[2, 2], beside.at[1], rest_sem.at[1]),
        pltpu.make_async_copy(weight.at[:2], earlier, rest_sem.at[2]),
    ]
    for one in rest:
        one.start()
    band_rows(scratch, 0, own, small[0:1, :C])
    acc[...] = jnp.zeros((CELLS, C), F32)

    def step(b, carry):
        copy(b).wait()
        acc[...] += band_tap(scratch, 0, b, held[b])
        return carry

    lax.fori_loop(0, 3, step, 0)
    for one in rest:
        one.wait()


def conv_own(own, small, weight):
    return call(
        conv_own_kernel,
        [((CELLS, C), F32), ((2, 3, C, C), BF16), ((2, 3, 3, C, C), BF16)],
        own,
        small,
        weight,
        name="conv_own",
        flops=2 * CELLS * 9 * C * C,
        scratch=[
            pltpu.VMEM((1, ROWS + 2, W, 3 * C), BF16),
            pltpu.VMEM((3, 3, C, C), BF16),
            pltpu.SemaphoreType.DMA((3,)),
            pltpu.SemaphoreType.DMA((3,)),
        ],
        specs=[VM, VM, HBM],
        mib=46,
    )


def conv_earlier_kernel(two, one, small, weight, start, acc, scratch):
    has_two, has_one, _, _ = inside()
    band_rows(scratch, 0, two, small[0:1, :C], has_two)
    band_rows(scratch, 1, one, small[0:1, :C], has_one)
    acc[...] = start[...]

    def step(g, carry):
        t, b = g // 3, g % 3
        acc[...] += band_tap(scratch, t, b, weight[t, b])
        return carry

    lax.fori_loop(0, 6, step, 0)


def conv_earlier(two, one, small, weight, start):
    return call(
        conv_earlier_kernel,
        [((CELLS, C), F32)],
        two,
        one,
        small,
        weight,
        start,
        name="conv_earlier",
        flops=2 * CELLS * 18 * C * C,
        scratch=[pltpu.VMEM((2, ROWS + 2, W, 3 * C), BF16)],
        aliases={4: 0},
    )


def edge_taps(scratch, low, high, first, last):
    left = dot(scratch[low], first[...].reshape(3 * C, C), ((1,), (0,)))
    right = dot(scratch[high], last[...].reshape(3 * C, C), ((1,), (0,)))
    return left, right


def conv_edges_kernel(low, high, small, w_own, w_pair, start, acc, scratch):
    two, _, above, below = inside()
    present = [above, above & two, below, below & two]
    fill_rows(scratch, [low[0], low[1], high[0], high[1]], small[0:1, :C], present)
    own = edge_taps(scratch, 0, 2, w_own.at[0], w_own.at[1])
    two = edge_taps(scratch, 1, 3, w_pair.at[0, 0], w_pair.at[0, 2])
    acc[...] = start[...]
    acc[:W] += own[0] + two[0]
    acc[2 * W :] += own[1] + two[1]


def conv_last_kernel(edges, own, small, weight, start, block, normed, scratch):
    _, one, above, below = inside()
    fill_rows(scratch, [edges[0], edges[1]], small[0:1, :C], [above & one, below & one])
    sides = edge_taps(scratch, 0, 1, weight.at[1, 0], weight.at[1, 2])
    bias, gain2 = small[1:2, :C], small[2:3, :C]
    for i in range(ROWS):
        rows = slice(i * W, (i + 1) * W)
        total = start[rows] + bias
        if i != 1:
            total += sides[i // 2]
        x = (own[i].astype(F32) + total.astype(BF16).astype(F32)).astype(BF16)
        block[rows] = x
        x = x.astype(F32)
        x = x * lax.rsqrt(jnp.mean(x * x, -1, keepdims=True) + 1e-6) * gain2
        normed[rows] = x.astype(BF16)


def edge_payload_kernel(own, two, _acc, to_next, to_previous, pair):
    to_next[0] = own[ROWS - 1]
    to_next[1] = two[ROWS - 1]
    to_previous[0] = own[0]
    to_previous[1] = two[0]

    odd = lax.rem(lax.axis_index("tm"), 2)

    @pl.when(odd == 0)
    def _():
        pair[...] = own[...]

    @pl.when(odd == 1)
    def _():
        pair[...] = two[...]


def pair_edges_kernel(low, high, _acc, out):
    index = lax.rem(lax.axis_index("tm"), 2)
    out[0] = low[index]
    out[1] = high[index]


def query_kernel(normed, weight, small, out, shift):
    scale = C**-0.5 * LOG2E
    wq, wk = weight[:, :C], weight[:, C : 2 * C]
    q = (dot(normed[...], wq, ((1,), (0,))) + small[4:5, :C]).astype(BF16)
    out[...] = (dot(wk, q, ((1,), (1,))) * scale).astype(BF16)
    bk = jnp.broadcast_to(small[4:5, C : 2 * C], (8, C))
    shift[...] = dot(bk, q.astype(F32), ((1,), (1,)))[:1] * scale


def spans(refs, low, high):
    at = 0
    for ref in refs:
        n = ref.shape[1]
        first, last = max(low, at), min(high, at + n)
        if first < last:
            yield ref, first - at, last - at, first - low, last - low
        at += n


def read(refs, low, high):
    pieces = [ref[:, a:b] for ref, a, b, _, _ in spans(refs, low, high)]
    return pieces[0] if len(pieces) == 1 else jnp.concatenate(pieces, 1)


def write(refs, low, high, value):
    for ref, a, b, first, last in spans(refs, low, high):
        ref[:, a:b] = value[:, first:last]


def joined(refs):
    return refs[0][...] if len(refs) == 1 else jnp.concatenate([r[...] for r in refs], 0)


def softmax_tiles(keys, tiles, q_of, old_of, give):
    keys_t = keys.T

    def scores(tile):
        return dot(keys, q_of(*tile), ((1,), (0,)))

    following = scores(tiles[0])
    for i, tile in enumerate(tiles):
        s = following
        if i + 1 < len(tiles):
            following = scores(tiles[i + 1])
        old = old_of(*tile)
        m = jnp.max(s, 0, keepdims=True)
        if old is not None:
            m = jnp.maximum(m, old[0])
        p = jnp.exp2(s - m)
        total = jnp.sum(p, 0, keepdims=True)
        acc = dot(keys_t, p.astype(BF16), ((1,), (0,)))
        if old is not None:
            alpha = jnp.exp2(old[0] - m)
            total = total + alpha * old[1]
            acc = acc + alpha * old[2]
        give(*tile, (m, total, acc))


def tiles_of(low, high, size=512):
    return [(at, min(at + size, high)) for at in range(low, high, size)]


def attention_kernel(n_keys, n_q, n_state, n_out, low, high, *refs):
    keys = joined(refs[:n_keys])
    queries = refs[n_keys : n_keys + n_q]
    state = refs[n_keys + n_q : n_keys + n_q + 3 * n_state]
    outs = refs[n_keys + n_q + 3 * n_state :]

    def old_of(a, b):
        return [read(state[i::3], a, b) for i in range(3)] if n_state else None

    def give(a, b, values):
        for i, value in enumerate(values):
            write(outs[i::3], a - low, b - low, value)

    softmax_tiles(keys, tiles_of(low, high), lambda a, b: read(queries, a, b), old_of, give)


def attention_step(keys, queries, state=(), low=0, high=None):
    widths = [q.shape[1] for q in queries]
    high = sum(widths) if high is None else high
    rows = sum(k.shape[0] for k in keys)
    whole_state = bool(state) and high - low == sum(s[0].shape[1] for s in state)
    outs = [s[0].shape[1] for s in state] if whole_state else [high - low]
    flat = [v for s in state for v in s]
    before = len(keys) + len(queries)
    result = call(
        functools.partial(
            attention_kernel, len(keys), len(queries), len(state), len(outs), low, high
        ),
        [shape for n in outs for shape in (((1, n), F32), ((1, n), F32), ((C, n), F32))],
        *keys,
        *queries,
        *flat,
        name="attention_step",
        flops=4 * rows * (high - low) * C,
        nbytes=6e6,
        aliases={before + i: i for i in range(len(flat))} if whole_state else None,
    )
    return [tuple(result[i : i + 3]) for i in range(0, len(result), 3)]


def gate_kernel(*refs):
    pass


def after(values, *done):
    count = len(values)
    return call(
        gate_kernel,
        [(v.shape, v.dtype) for v in values],
        *values,
        *done,
        name="gate",
        flops=1,
        nbytes=1,
        specs=[ANY] * (count + len(done)),
        out_spec=ANY,
        aliases={i: i for i in range(count)},
    )


def split3(x):
    hi = x.astype(BF16)
    rest = x - hi.astype(F32)
    mid = rest.astype(BF16)
    low = (rest - mid.astype(F32)).astype(BF16)
    return hi, mid, low


def stat_rows(parts):
    n = parts[0].shape[1]
    row = lax.broadcasted_iota(jnp.int32, (STAT, n), 0)
    block = jnp.zeros((STAT, n), F32)
    for i, part in enumerate(parts):
        for j, piece in enumerate(split3(part)):
            block = jnp.where(row == 3 * i + j, piece.astype(F32), block)
    return block.astype(BF16)


def stat_of(block, i):
    b = block.astype(F32)
    return b[3 * i : 3 * i + 1] + b[3 * i + 1 : 3 * i + 2] + b[3 * i + 2 : 3 * i + 3]


def opposite_kernel(n_keys, *refs):
    q, m_old, l_old, acc_old, top, bottom = refs[n_keys:]

    def give(_a, _b, values):
        m, total, acc = values
        out = (acc / total).astype(BF16)
        stats = stat_rows([m + jnp.log2(total)])
        top[:HALF] = out[:HALF]
        top[HALF:] = stats
        bottom[:HALF] = out[HALF:]
        bottom[HALF:] = stats

    old = lambda a, b: (m_old[...], l_old[...], acc_old[...])
    softmax_tiles(joined(refs[:n_keys]), [(0, CELLS)], lambda a, b: q[...], old, give)


def opposite(keys, q_far, state):
    rows = sum(k.shape[0] for k in keys)
    return call(
        functools.partial(opposite_kernel, len(keys)),
        [((HALF + STAT, CELLS), BF16)] * 2,
        *keys,
        q_far,
        *state,
        name="opposite",
        flops=4 * rows * CELLS * C,
        nbytes=2e6,
    )


def merge(parts):
    top = functools.reduce(jnp.maximum, [s for s, _ in parts])
    w = [jnp.exp2(s - top) for s, _ in parts]
    total = functools.reduce(jnp.add, w)
    inverse = 1.0 / total
    out = functools.reduce(jnp.add, [(a * inverse) * o for a, (_, o) in zip(w, parts)])
    return top + jnp.log2(total), out


def relay_kernel(from_low, from_high, m, total, acc, _phases, to_low, to_high):
    for side, got, out in ((0, from_high, to_low), (1, from_low, to_high)):
        cols = slice(side * CELLS, (side + 1) * CELLS)
        stat = m[:, cols] + jnp.log2(total[:, cols])
        mine = acc[:, cols] / total[:, cols]
        theirs = (stat_of(got[HALF:], 0), got[:HALF].astype(F32))
        if side == 0:
            stat_t, half_t = stat, mine[:HALF]
            stat_b, half_b = merge([(stat, mine[HALF:]), theirs])
        else:
            stat_t, half_t = merge([(stat, mine[:HALF]), theirs])
            stat_b, half_b = stat, mine[HALF:]
        out[:HALF] = half_t.astype(BF16)
        out[HALF:C] = half_b.astype(BF16)
        out[C:] = stat_rows([stat_t, stat_b])


def finish_kernel(from_low, from_high, m, total, acc, shift, weight, wp, small, block, out):
    c = shift[...]
    stat = m[...] + jnp.log2(total[...]) + c
    mine = acc[...] / total[...]
    halves = []
    for i in range(2):
        rows = slice(i * HALF, (i + 1) * HALF)
        parts = [(stat, mine[rows])] + [
            (stat_of(got[C:], i) + c, got[rows].astype(F32)) for got in (from_low, from_high)
        ]
        halves.append(merge(parts)[1])
    mixed_in = jnp.concatenate(halves, 0).astype(BF16)
    mixed = (dot(mixed_in, weight[:, 2 * C :], ((0,), (0,))) + small[4:5, 2 * C :]).astype(BF16)
    attended = dot(mixed, wp[...], ((1,), (0,))) + small[3:4, :C] + block[...].astype(F32)
    out[...] = attended.astype(BF16)


def pack_kernel(flat, small):
    small[...] = jnp.zeros_like(small)
    at = 0
    for i, n in enumerate((C, C, C, C, 3 * C, OUT)):
        small[i, :n] = flat[at : at + n]
        at += n


def up_phases_kernel(weight, out):
    w = [[weight[b, c].astype(F32) for c in range(3)] for b in range(3)]

    def pairs(a, b, c):
        return ((a, b + c), (a + b, c))

    by_row = [pairs(*(w[b][c] for b in range(3))) for c in range(3)]
    for di in range(2):
        for rt in range(2):
            by_column = pairs(*(by_row[c][di][rt] for c in range(3)))
            for dj in range(2):
                for ct in range(2):
                    value = jnp.concatenate(
                        [by_column[dj][ct], jnp.zeros((256 - OUT, C), F32)], 0
                    )
                    out[di, dj, rt, ct * C : (ct + 1) * C] = value.T.astype(BF16)


def fill_plain(scratch, index, row):
    def store(variant, value):
        scratch[index, :, variant * C : (variant + 1) * C] = value

    col_variants(row.astype(F32), store)


def store_phase(wide, row, dj, value):
    for part in range(2):
        wide[part, row, pl.ds(dj, W, stride=2), :] = value[:, part * 128 : (part + 1) * 128]


def read_row(wide, row):
    return jnp.concatenate([wide[0, row].T, wide[1, row].T[: OUT - 128]], 0)


def up_inner_kernel(body, weight, small, out, edge, scratch, wide):
    for i in range(ROWS):
        fill_plain(scratch, i, body[i])
    b = small[5:6, :256]
    for di in range(2):
        for dj in range(2):
            full = scratch[:, :, dj * C : (dj + 2) * C].reshape(CELLS, 2 * C)
            if di == 0:
                here = dot(full, weight[0, dj, 1], ((1,), (0,))) + b
                beside = dot(full[: 2 * W], weight[0, dj, 0], ((1,), (0,)))
                parts = [here[:W], here[W : 2 * W] + beside[:W], here[2 * W :] + beside[W:]]
            else:
                here = dot(full, weight[1, dj, 0], ((1,), (0,))) + b
                beside = dot(full[W:], weight[1, dj, 1], ((1,), (0,)))
                parts = [here[:W] + beside[:W], here[W : 2 * W] + beside[W:], here[2 * W :]]
            for i, part in enumerate(parts):
                store_phase(wide, 2 * i + di, dj, part)
    for row in range(1, 2 * ROWS - 1):
        out[row] = read_row(wide, row).astype(BF16)
    edge[0] = read_row(wide, 0)
    edge[1] = read_row(wide, 2 * ROWS - 1)


def up_edges_kernel(low, high, weight, edge, _start, out, scratch, wide, rows, sem):
    _, _, above, below = inside()
    for i, (ref, present) in enumerate(((low, above), (high, below))):
        row = ref[0]
        fill_plain(scratch, i, jnp.where(present, row, jnp.zeros_like(row)))
    copies = []
    for side in range(2):
        for dj in range(2):
            left = scratch[side, :, dj * C : (dj + 2) * C]
            store_phase(wide, side, dj, dot(left, weight[side, dj, side], ((1,), (0,))))
        rows[side] = (edge[side] + read_row(wide, side)).astype(BF16)
        row = out.at[side * (2 * ROWS - 1)]
        copies.append(pltpu.make_async_copy(rows.at[side], row, sem.at[side]))
        copies[side].start()
    for copy in copies:
        copy.wait()


def permute_z(value, by):
    pairs = [(x * ZN + z, x * ZN + (z + by) % ZN) for x in range(XN) for z in range(ZN)]
    return lax.ppermute(value, "rows", pairs)


def permute_x(value, by):
    pairs = [(x * ZN + z, (x + by) % XN * ZN + z) for x in range(XN) for z in range(ZN)]
    return lax.ppermute(value, "rows", pairs)


def to_bands(value, by):
    n = XN * ZN
    return lax.ppermute(value, "rows", [(i, (i + by) % n) for i in range(n)])


def on_device(
    latent,
    norm1_gain,
    conv1_weight,
    conv1_bias,
    attention_gain,
    qkv_weight,
    qkv_bias,
    proj_weight,
    proj_bias,
    up_weight,
    up_bias,
):
    own = latent[0]
    two = lax.ppermute(own, "tm", [(t, (t + 2) % TN) for t in range(TN)])
    flat = (norm1_gain, conv1_bias, attention_gain, proj_bias, qkv_bias, up_bias)
    ends = [sum(v.shape[0] for v in flat[: i + 1]) for i in range(len(flat))]
    joined_flat = functools.reduce(
        jnp.add,
        [jnp.pad(v, (end - v.shape[0], ends[-1] - end)) for v, end in zip(flat, ends)],
    )
    small = call(pack_kernel, [((8, 3 * C), F32)], joined_flat, name="pack")
    acc, w_own, w_pair = conv_own(own, small, conv1_weight)
    pairs = [(t, t ^ 1) for t in range(TN)]
    to_next, to_previous, pair = call(
        edge_payload_kernel,
        [((2, W, C), BF16)] * 2 + [((ROWS, W, C), BF16)],
        own,
        two,
        acc,
        name="edge_payload",
        specs=[VM, VM, ANY],
    )
    low, high = to_bands(to_next, 1), to_bands(to_previous, -1)
    one = lax.ppermute(pair, "tm", pairs)
    acc = conv_earlier(two, one, small, w_pair, acc)
    pair_edges = call(
        pair_edges_kernel,
        [((2, W, C), BF16)],
        low,
        high,
        acc,
        name="pair_edges",
        specs=[VM, VM, ANY],
    )
    one_edges = lax.ppermute(pair_edges, "tm", pairs)
    acc = call(
        conv_edges_kernel,
        [((CELLS, C), F32)],
        low,
        high,
        small,
        w_own,
        w_pair,
        acc,
        name="conv_edges",
        flops=2 * CELLS * 2 * C * C,
        scratch=[pltpu.VMEM((4, W, 3 * C), BF16)],
        aliases={5: 0},
    )
    block, normed = call(
        conv_last_kernel,
        [((CELLS, C), BF16)] * 2,
        one_edges,
        own,
        small,
        w_pair,
        acc,
        name="conv_last",
        flops=2 * CELLS * C * C,
        scratch=[pltpu.VMEM((2, W, 3 * C), BF16)],
    )

    up, down = permute_z(normed, 1), permute_z(normed, -1)
    query, shift = call(
        query_kernel,
        [((C, CELLS), BF16), ((1, CELLS), F32)],
        normed,
        qkv_weight,
        small,
        name="queries",
        flops=4 * CELLS * C * C,
    )
    q_low, q_high = permute_x(query, 1), permute_x(query, -1)
    q_far = permute_x(query, 2)
    up2, down2 = permute_z(up, 1), permute_z(down, -1)
    early = [normed, up, down]
    near = [q_low, q_high, query]
    (state,) = attention_step(early, near)
    up2, down2 = after((up2, down2), state[0], q_far)
    up3, down3 = permute_z(up2, 1), permute_z(down2, -1)
    (far,) = attention_step(early, [q_far])
    queries = near + [q_far]
    state, far = attention_step([up2, down2], queries, (state, far))
    up4, down4 = permute_z(up3[: CELLS // 2], 1), permute_z(down3[CELLS // 2 :], -1)
    state, far = attention_step([up3, down3], queries, (state, far))
    last = [up4, down4]
    pay_t, pay_b = opposite(last, q_far, far)
    half_low, half_high = permute_x(pay_t, 1), permute_x(pay_b, -1)
    (sides,) = attention_step(last, near, (state,), 0, 2 * CELLS)
    phases = call(
        up_phases_kernel,
        [((2, 2, 2, 2 * C, 256), BF16)],
        up_weight.transpose(0, 1, 3, 2),
        name="up_phases",
        flops=1e7,
        nbytes=4e6,
    )
    to_low, to_high = call(
        relay_kernel,
        [((C + STAT, CELLS), BF16)] * 2,
        half_low,
        half_high,
        *sides,
        phases,
        name="relay",
        specs=[VM] * 5 + [ANY],
    )
    from_low, from_high = permute_x(to_high, 1), permute_x(to_low, -1)
    (mine,) = attention_step(last, near, (state,), 2 * CELLS, 3 * CELLS)
    attended = call(
        finish_kernel,
        [((CELLS, C), BF16)],
        from_low,
        from_high,
        *mine,
        shift,
        qkv_weight,
        proj_weight,
        small,
        block,
        name="finish",
        flops=4 * CELLS * C * C,
    ).reshape(ROWS, W, C)
    edge_low, edge_high = to_bands(attended[2:], 1), to_bands(attended[:1], -1)
    inner, edge = call(
        up_inner_kernel,
        [((2 * ROWS, OUT, 2 * W), BF16), ((2, OUT, 2 * W), F32)],
        attended,
        phases,
        small,
        name="up_inner",
        flops=2 * CELLS * 14 * C * OUT,
        scratch=[
            pltpu.VMEM((ROWS, W, 3 * C), BF16),
            pltpu.VMEM((2, 2 * ROWS, 2 * W, 128), F32),
        ],
    )
    result = call(
        up_edges_kernel,
        [((2 * ROWS, OUT, 2 * W), BF16)],
        edge_low,
        edge_high,
        phases,
        edge,
        inner,
        name="up_edges",
        flops=2 * CELLS * 2 * C * OUT,
        scratch=[
            pltpu.VMEM((2, W, 3 * C), BF16),
            pltpu.VMEM((2, 2, 2 * W, 128), F32),
            pltpu.VMEM((2, OUT, 2 * W), BF16),
            pltpu.SemaphoreType.DMA((2,)),
        ],
        specs=[VM, VM, VM, VM, ANY],
        out_spec=ANY,
        aliases={4: 0},
    )
    return result.transpose(0, 2, 1)[None]


def solution(mesh):
    return jax.shard_map(
        on_device,
        mesh=mesh,
        in_specs=(P("tm", "rows", None, None), P(), P(), P(), P(), P(), P(), P(), P(), P(), P()),
        out_specs=P("tm", "rows", None, None),
        check_vma=False,
    )
```

```python
import functools
import math

import jax
import jax.numpy as jnp
from jax import lax
from jax.experimental import pallas as pl
from jax.experimental.pallas import tpu as pltpu
from jax.sharding import PartitionSpec as P

F32 = jnp.float32
BF16 = jnp.bfloat16
ROWS = 3
W = 128
C = 384
OUT = 192
CELLS = ROWS * W
XN, ZN, TN = 4, 8, 8
QALL = XN * CELLS
HALF = C // 2
STAT = 16
LOG2E = math.log2(math.e)


def dot(a, b, dims):
    return lax.dot_general(a, b, (dims, ((), ())), preferred_element_type=F32)


def params(mib=32):
    return pltpu.CompilerParams(vmem_limit_bytes=mib * 2**20)


def cost(flops, bytes_accessed):
    return pl.CostEstimate(flops=int(flops), bytes_accessed=int(bytes_accessed), transcendentals=0)


VM = pl.BlockSpec(memory_space=pltpu.VMEM)
ANY = pl.BlockSpec(memory_space=pl.ANY)
HBM = pl.BlockSpec(memory_space=pltpu.HBM)


def call(body, outs, *args, name, flops=1e6, nbytes=1e6, aliases=None, scratch=(), mib=32, specs=None, out_spec=VM):
    shapes = [jax.ShapeDtypeStruct(shape, dtype) for shape, dtype in outs]
    result = pl.pallas_call(
        body,
        in_specs=specs or [VM] * len(args),
        out_specs=[out_spec] * len(shapes),
        out_shape=shapes,
        input_output_aliases=aliases or {},
        scratch_shapes=list(scratch),
        compiler_params=params(mib),
        cost_estimate=cost(flops, nbytes),
        name=name,
    )(*args)
    return result[0] if len(shapes) == 1 else result


def col_variants(y, store):
    column = lax.broadcasted_iota(jnp.int32, y.shape, 0)
    before = jnp.where(column == 0, 0.0, pltpu.roll(y, 1, 0))
    after = jnp.where(column == W - 1, 0.0, pltpu.roll(y, W - 1, 0))
    store(0, before.astype(BF16))
    store(1, y.astype(BF16))
    store(2, after.astype(BF16))


def activate(row, gain):
    x = row.astype(F32)
    y = x * lax.rsqrt(jnp.mean(x * x, -1, keepdims=True) + 1e-6) * gain
    y = y / (1.0 + jnp.exp(-y))
    return y.astype(BF16).astype(F32)


def inside():
    frame, band = lax.axis_index("tm"), lax.axis_index("rows")
    return frame >= 2, frame >= 1, band >= 1, band < XN * ZN - 1


def fill_rows(scratch, rows, gain, present=None):
    for index, row in enumerate(rows):
        y = activate(row, gain)
        if present is not None:
            y = jnp.where(present[index], y, 0.0)

        def store(variant, value, index=index):
            scratch[index, :, variant * C : (variant + 1) * C] = value

        col_variants(y, store)


def band_rows(scratch, t, frame, gain, present=None):
    zero = jnp.zeros((W, 3 * C), BF16)
    scratch[t, 0] = zero
    scratch[t, 1 + ROWS] = zero
    present = None if present is None else [present] * ROWS
    fill_rows(scratch.at[t, 1 : 1 + ROWS], [frame[i] for i in range(ROWS)], gain, present)


def band_tap(scratch, t, b, weight):
    left = scratch[t, pl.ds(b, ROWS)].reshape(CELLS, 3 * C)
    return dot(left, weight.reshape(3 * C, C), ((1,), (0,)))


def conv_own_kernel(own, small, weight, acc, beside, earlier, scratch, held, sem, rest_sem):
    def copy(b):
        return pltpu.make_async_copy(weight.at[2, b], held.at[b], sem.at[b])

    for b in range(3):
        copy(b).start()
    rest = [
        pltpu.make_async_copy(weight.at[2, 0], beside.at[0], rest_sem.at[0]),
        pltpu.make_async_copy(weight.at[2, 2], beside.at[1], rest_sem.at[1]),
        pltpu.make_async_copy(weight.at[:2], earlier, rest_sem.at[2]),
    ]
    for one in rest:
        one.start()
    band_rows(scratch, 0, own, small[0:1, :C])
    acc[...] = jnp.zeros((CELLS, C), F32)

    def step(b, carry):
        copy(b).wait()
        acc[...] += band_tap(scratch, 0, b, held[b])
        return carry

    lax.fori_loop(0, 3, step, 0)
    for one in rest:
        one.wait()


def conv_own(own, small, weight):
    return call(
        conv_own_kernel,
        [((CELLS, C), F32), ((2, 3, C, C), BF16), ((2, 3, 3, C, C), BF16)],
        own,
        small,
        weight,
        name="conv_own",
        flops=2 * CELLS * 9 * C * C,
        scratch=[
            pltpu.VMEM((1, ROWS + 2, W, 3 * C), BF16),
            pltpu.VMEM((3, 3, C, C), BF16),
            pltpu.SemaphoreType.DMA((3,)),
            pltpu.SemaphoreType.DMA((3,)),
        ],
        specs=[VM, VM, HBM],
        mib=46,
    )


def conv_earlier_kernel(two, one, small, weight, start, acc, scratch):
    has_two, has_one, _, _ = inside()
    band_rows(scratch, 0, two, small[0:1, :C], has_two)
    band_rows(scratch, 1, one, small[0:1, :C], has_one)
    acc[...] = start[...]

    def step(g, carry):
        t, b = g // 3, g % 3
        acc[...] += band_tap(scratch, t, b, weight[t, b])
        return carry

    lax.fori_loop(0, 6, step, 0)


def conv_earlier(two, one, small, weight, start):
    return call(
        conv_earlier_kernel,
        [((CELLS, C), F32)],
        two,
        one,
        small,
        weight,
        start,
        name="conv_earlier",
        flops=2 * CELLS * 18 * C * C,
        scratch=[pltpu.VMEM((2, ROWS + 2, W, 3 * C), BF16)],
        aliases={4: 0},
    )


def edge_taps(scratch, low, high, first, last):
    left = dot(scratch[low], first[...].reshape(3 * C, C), ((1,), (0,)))
    right = dot(scratch[high], last[...].reshape(3 * C, C), ((1,), (0,)))
    return left, right


def conv_edges_kernel(low, high, small, w_own, w_pair, start, acc, scratch):
    two, _, above, below = inside()
    present = [above, above & two, below, below & two]
    fill_rows(scratch, [low[0], low[1], high[0], high[1]], small[0:1, :C], present)
    own = edge_taps(scratch, 0, 2, w_own.at[0], w_own.at[1])
    two = edge_taps(scratch, 1, 3, w_pair.at[0, 0], w_pair.at[0, 2])
    acc[...] = start[...]
    acc[:W] += own[0] + two[0]
    acc[2 * W :] += own[1] + two[1]


def conv_last_kernel(edges, own, small, weight, start, block, normed, scratch):
    _, one, above, below = inside()
    fill_rows(scratch, [edges[0], edges[1]], small[0:1, :C], [above & one, below & one])
    sides = edge_taps(scratch, 0, 1, weight.at[1, 0], weight.at[1, 2])
    bias, gain2 = small[1:2, :C], small[2:3, :C]
    for i in range(ROWS):
        rows = slice(i * W, (i + 1) * W)
        total = start[rows] + bias
        if i != 1:
            total += sides[i // 2]
        x = (own[i].astype(F32) + total.astype(BF16).astype(F32)).astype(BF16)
        block[rows] = x
        x = x.astype(F32)
        x = x * lax.rsqrt(jnp.mean(x * x, -1, keepdims=True) + 1e-6) * gain2
        normed[rows] = x.astype(BF16)


def edge_payload_kernel(own, two, _acc, to_next, to_previous, pair):
    to_next[0] = own[ROWS - 1]
    to_next[1] = two[ROWS - 1]
    to_previous[0] = own[0]
    to_previous[1] = two[0]

    odd = lax.rem(lax.axis_index("tm"), 2)

    @pl.when(odd == 0)
    def _():
        pair[...] = own[...]

    @pl.when(odd == 1)
    def _():
        pair[...] = two[...]


def pair_edges_kernel(low, high, _acc, out):
    index = lax.rem(lax.axis_index("tm"), 2)
    out[0] = low[index]
    out[1] = high[index]


def query_kernel(normed, weight, small, out, shift):
    scale = C**-0.5 * LOG2E
    wq, wk = weight[:, :C], weight[:, C : 2 * C]
    q = (dot(normed[...], wq, ((1,), (0,))) + small[4:5, :C]).astype(BF16)
    out[...] = (dot(wk, q, ((1,), (1,))) * scale).astype(BF16)
    bk = jnp.broadcast_to(small[4:5, C : 2 * C], (8, C))
    shift[...] = dot(bk, q.astype(F32), ((1,), (1,)))[:1] * scale


def spans(refs, low, high):
    at = 0
    for ref in refs:
        n = ref.shape[1]
        first, last = max(low, at), min(high, at + n)
        if first < last:
            yield ref, first - at, last - at, first - low, last - low
        at += n


def read(refs, low, high):
    pieces = [ref[:, a:b] for ref, a, b, _, _ in spans(refs, low, high)]
    return pieces[0] if len(pieces) == 1 else jnp.concatenate(pieces, 1)


def write(refs, low, high, value):
    for ref, a, b, first, last in spans(refs, low, high):
        ref[:, a:b] = value[:, first:last]


def joined(refs):
    return refs[0][...] if len(refs) == 1 else jnp.concatenate([r[...] for r in refs], 0)


def softmax_tiles(keys, tiles, q_of, old_of, give):
    keys_t = keys.T

    def scores(tile):
        return dot(keys, q_of(*tile), ((1,), (0,)))

    following = scores(tiles[0])
    for i, tile in enumerate(tiles):
        s = following
        if i + 1 < len(tiles):
            following = scores(tiles[i + 1])
        old = old_of(*tile)
        m = jnp.max(s, 0, keepdims=True)
        if old is not None:
            m = jnp.maximum(m, old[0])
        p = jnp.exp2(s - m)
        total = jnp.sum(p, 0, keepdims=True)
        acc = dot(keys_t, p.astype(BF16), ((1,), (0,)))
        if old is not None:
            alpha = jnp.exp2(old[0] - m)
            total = total + alpha * old[1]
            acc = acc + alpha * old[2]
        give(*tile, (m, total, acc))


def tiles_of(low, high, size=512):
    return [(at, min(at + size, high)) for at in range(low, high, size)]


def attention_kernel(n_keys, n_q, n_state, n_out, low, high, *refs):
    keys = joined(refs[:n_keys])
    queries = refs[n_keys : n_keys + n_q]
    state = refs[n_keys + n_q : n_keys + n_q + 3 * n_state]
    outs = refs[n_keys + n_q + 3 * n_state :]

    def old_of(a, b):
        return [read(state[i::3], a, b) for i in range(3)] if n_state else None

    def give(a, b, values):
        for i, value in enumerate(values):
            write(outs[i::3], a - low, b - low, value)

    softmax_tiles(keys, tiles_of(low, high), lambda a, b: read(queries, a, b), old_of, give)


def attention_step(keys, queries, state=(), low=0, high=None):
    widths = [q.shape[1] for q in queries]
    high = sum(widths) if high is None else high
    rows = sum(k.shape[0] for k in keys)
    whole_state = bool(state) and high - low == sum(s[0].shape[1] for s in state)
    outs = [s[0].shape[1] for s in state] if whole_state else [high - low]
    flat = [v for s in state for v in s]
    before = len(keys) + len(queries)
    result = call(
        functools.partial(
            attention_kernel, len(keys), len(queries), len(state), len(outs), low, high
        ),
        [shape for n in outs for shape in (((1, n), F32), ((1, n), F32), ((C, n), F32))],
        *keys,
        *queries,
        *flat,
        name="attention_step",
        flops=4 * rows * (high - low) * C,
        nbytes=6e6,
        aliases={before + i: i for i in range(len(flat))} if whole_state else None,
    )
    return [tuple(result[i : i + 3]) for i in range(0, len(result), 3)]


def gate_kernel(*refs):
    pass


def after(values, *done):
    count = len(values)
    return call(
        gate_kernel,
        [(v.shape, v.dtype) for v in values],
        *values,
        *done,
        name="gate",
        flops=1,
        nbytes=1,
        specs=[ANY] * (count + len(done)),
        out_spec=ANY,
        aliases={i: i for i in range(count)},
    )


def split3(x):
    hi = x.astype(BF16)
    rest = x - hi.astype(F32)
    mid = rest.astype(BF16)
    low = (rest - mid.astype(F32)).astype(BF16)
    return hi, mid, low


def stat_rows(parts):
    n = parts[0].shape[1]
    row = lax.broadcasted_iota(jnp.int32, (STAT, n), 0)
    block = jnp.zeros((STAT, n), F32)
    for i, part in enumerate(parts):
        for j, piece in enumerate(split3(part)):
            block = jnp.where(row == 3 * i + j, piece.astype(F32), block)
    return block.astype(BF16)


def stat_of(block, i):
    b = block.astype(F32)
    return b[3 * i : 3 * i + 1] + b[3 * i + 1 : 3 * i + 2] + b[3 * i + 2 : 3 * i + 3]


def opposite_kernel(n_keys, *refs):
    q, m_old, l_old, acc_old, top, bottom = refs[n_keys:]

    def give(_a, _b, values):
        m, total, acc = values
        out = (acc / total).astype(BF16)
        stats = stat_rows([m + jnp.log2(total)])
        top[:HALF] = out[:HALF]
        top[HALF:] = stats
        bottom[:HALF] = out[HALF:]
        bottom[HALF:] = stats

    old = lambda a, b: (m_old[...], l_old[...], acc_old[...])
    softmax_tiles(joined(refs[:n_keys]), [(0, CELLS)], lambda a, b: q[...], old, give)


def opposite(keys, q_far, state):
    rows = sum(k.shape[0] for k in keys)
    return call(
        functools.partial(opposite_kernel, len(keys)),
        [((HALF + STAT, CELLS), BF16)] * 2,
        *keys,
        q_far,
        *state,
        name="opposite",
        flops=4 * rows * CELLS * C,
        nbytes=2e6,
    )


def merge(parts):
    top = functools.reduce(jnp.maximum, [s for s, _ in parts])
    w = [jnp.exp2(s - top) for s, _ in parts]
    total = functools.reduce(jnp.add, w)
    inverse = 1.0 / total
    out = functools.reduce(jnp.add, [(a * inverse) * o for a, (_, o) in zip(w, parts)])
    return top + jnp.log2(total), out


def relay_kernel(from_low, from_high, m, total, acc, _phases, to_low, to_high):
    for side, got, out in ((0, from_high, to_low), (1, from_low, to_high)):
        cols = slice(side * CELLS, (side + 1) * CELLS)
        stat = m[:, cols] + jnp.log2(total[:, cols])
        mine = acc[:, cols] / total[:, cols]
        theirs = (stat_of(got[HALF:], 0), got[:HALF].astype(F32))
        if side == 0:
            stat_t, half_t = stat, mine[:HALF]
            stat_b, half_b = merge([(stat, mine[HALF:]), theirs])
        else:
            stat_t, half_t = merge([(stat, mine[:HALF]), theirs])
            stat_b, half_b = stat, mine[HALF:]
        out[:HALF] = half_t.astype(BF16)
        out[HALF:C] = half_b.astype(BF16)
        out[C:] = stat_rows([stat_t, stat_b])


def finish_kernel(from_low, from_high, m, total, acc, shift, weight, wp, small, block, out, to_next, to_previous):
    c = shift[...]
    stat = m[...] + jnp.log2(total[...]) + c
    mine = acc[...] / total[...]
    halves = []
    for i in range(2):
        rows = slice(i * HALF, (i + 1) * HALF)
        parts = [(stat, mine[rows])] + [
            (stat_of(got[C:], i) + c, got[rows].astype(F32)) for got in (from_low, from_high)
        ]
        halves.append(merge(parts)[1])
    mixed_in = jnp.concatenate(halves, 0).astype(BF16)
    mixed = (dot(mixed_in, weight[:, 2 * C :], ((0,), (0,))) + small[4:5, 2 * C :]).astype(BF16)
    attended = dot(mixed, wp[...], ((1,), (0,))) + small[3:4, :C] + block[...].astype(F32)
    attended = attended.astype(BF16)
    out[...] = attended
    to_next[0] = attended[2 * W :]
    to_previous[0] = attended[:W]


def pack_kernel(flat, small):
    small[...] = jnp.zeros_like(small)
    at = 0
    for i, n in enumerate((C, C, C, C, 3 * C, OUT)):
        small[i, :n] = flat[at : at + n]
        at += n


def up_phases_kernel(weight, out):
    w = [[weight[b, c].astype(F32) for c in range(3)] for b in range(3)]

    def pairs(a, b, c):
        return ((a, b + c), (a + b, c))

    by_row = [pairs(*(w[b][c] for b in range(3))) for c in range(3)]
    for di in range(2):
        for rt in range(2):
            by_column = pairs(*(by_row[c][di][rt] for c in range(3)))
            for dj in range(2):
                for ct in range(2):
                    value = jnp.concatenate(
                        [by_column[dj][ct], jnp.zeros((256 - OUT, C), F32)], 0
                    )
                    out[di, dj, rt, ct * C : (ct + 1) * C] = value.T.astype(BF16)


def fill_plain(scratch, index, row):
    def store(variant, value):
        scratch[index, :, variant * C : (variant + 1) * C] = value

    col_variants(row.astype(F32), store)


def store_phase(wide, row, dj, value):
    for part in range(2):
        wide[part, row, pl.ds(dj, W, stride=2), :] = value[:, part * 128 : (part + 1) * 128]


def read_row(wide, row):
    return jnp.concatenate([wide[0, row].T, wide[1, row].T[: OUT - 128]], 0)


def up_inner_kernel(body, weight, small, out, edge, scratch, wide):
    for i in range(ROWS):
        fill_plain(scratch, i, body[i])
    b = small[5:6, :256]
    for di in range(2):
        for dj in range(2):
            full = scratch[:, :, dj * C : (dj + 2) * C].reshape(CELLS, 2 * C)
            if di == 0:
                here = dot(full, weight[0, dj, 1], ((1,), (0,))) + b
                beside = dot(full[: 2 * W], weight[0, dj, 0], ((1,), (0,)))
                parts = [here[:W], here[W : 2 * W] + beside[:W], here[2 * W :] + beside[W:]]
            else:
                here = dot(full, weight[1, dj, 0], ((1,), (0,))) + b
                beside = dot(full[W:], weight[1, dj, 1], ((1,), (0,)))
                parts = [here[:W] + beside[:W], here[W : 2 * W] + beside[W:], here[2 * W :]]
            for i, part in enumerate(parts):
                store_phase(wide, 2 * i + di, dj, part)
    for row in range(1, 2 * ROWS - 1):
        out[row] = read_row(wide, row).astype(BF16)
    edge[0] = read_row(wide, 0)
    edge[1] = read_row(wide, 2 * ROWS - 1)


def up_edges_kernel(low, high, weight, edge, _start, out, scratch, wide, rows, sem):
    _, _, above, below = inside()
    for i, (ref, present) in enumerate(((low, above), (high, below))):
        row = ref[0]
        fill_plain(scratch, i, jnp.where(present, row, jnp.zeros_like(row)))
    copies = []
    for side in range(2):
        for dj in range(2):
            left = scratch[side, :, dj * C : (dj + 2) * C]
            store_phase(wide, side, dj, dot(left, weight[side, dj, side], ((1,), (0,))))
        rows[side] = (edge[side] + read_row(wide, side)).astype(BF16)
        row = out.at[side * (2 * ROWS - 1)]
        copies.append(pltpu.make_async_copy(rows.at[side], row, sem.at[side]))
        copies[side].start()
    for copy in copies:
        copy.wait()


def permute_z(value, by):
    pairs = [(x * ZN + z, x * ZN + (z + by) % ZN) for x in range(XN) for z in range(ZN)]
    return lax.ppermute(value, "rows", pairs)


def permute_x(value, by):
    pairs = [(x * ZN + z, (x + by) % XN * ZN + z) for x in range(XN) for z in range(ZN)]
    return lax.ppermute(value, "rows", pairs)


def to_bands(value, by):
    n = XN * ZN
    return lax.ppermute(value, "rows", [(i, (i + by) % n) for i in range(n)])


def on_device(
    latent,
    norm1_gain,
    conv1_weight,
    conv1_bias,
    attention_gain,
    qkv_weight,
    qkv_bias,
    proj_weight,
    proj_bias,
    up_weight,
    up_bias,
):
    own = latent[0]
    two = lax.ppermute(own, "tm", [(t, (t + 2) % TN) for t in range(TN)])
    flat = (norm1_gain, conv1_bias, attention_gain, proj_bias, qkv_bias, up_bias)
    ends = [sum(v.shape[0] for v in flat[: i + 1]) for i in range(len(flat))]
    joined_flat = functools.reduce(
        jnp.add,
        [jnp.pad(v, (end - v.shape[0], ends[-1] - end)) for v, end in zip(flat, ends)],
    )
    small = call(pack_kernel, [((8, 3 * C), F32)], joined_flat, name="pack")
    acc, w_own, w_pair = conv_own(own, small, conv1_weight)
    pairs = [(t, t ^ 1) for t in range(TN)]
    to_next, to_previous, pair = call(
        edge_payload_kernel,
        [((2, W, C), BF16)] * 2 + [((ROWS, W, C), BF16)],
        own,
        two,
        acc,
        name="edge_payload",
        specs=[VM, VM, ANY],
    )
    low, high = to_bands(to_next, 1), to_bands(to_previous, -1)
    one = lax.ppermute(pair, "tm", pairs)
    acc = conv_earlier(two, one, small, w_pair, acc)
    pair_edges = call(
        pair_edges_kernel,
        [((2, W, C), BF16)],
        low,
        high,
        acc,
        name="pair_edges",
        specs=[VM, VM, ANY],
    )
    one_edges = lax.ppermute(pair_edges, "tm", pairs)
    acc = call(
        conv_edges_kernel,
        [((CELLS, C), F32)],
        low,
        high,
        small,
        w_own,
        w_pair,
        acc,
        name="conv_edges",
        flops=2 * CELLS * 2 * C * C,
        scratch=[pltpu.VMEM((4, W, 3 * C), BF16)],
        aliases={5: 0},
    )
    block, normed = call(
        conv_last_kernel,
        [((CELLS, C), BF16)] * 2,
        one_edges,
        own,
        small,
        w_pair,
        acc,
        name="conv_last",
        flops=2 * CELLS * C * C,
        scratch=[pltpu.VMEM((2, W, 3 * C), BF16)],
    )

    up, down = permute_z(normed, 1), permute_z(normed, -1)
    query, shift = call(
        query_kernel,
        [((C, CELLS), BF16), ((1, CELLS), F32)],
        normed,
        qkv_weight,
        small,
        name="queries",
        flops=4 * CELLS * C * C,
    )
    q_low, q_high = permute_x(query, 1), permute_x(query, -1)
    q_far = permute_x(query, 2)
    up2, down2 = permute_z(up, 1), permute_z(down, -1)
    early = [normed, up, down]
    near = [q_low, q_high, query]
    (state,) = attention_step(early, near)
    up2, down2 = after((up2, down2), state[0])
    up3, down3 = permute_z(up2, 1), permute_z(down2, -1)
    (far,) = attention_step(early, [q_far])
    queries = near + [q_far]
    state, far = attention_step([up2, down2], queries, (state, far))
    up4, down4 = permute_z(up3[: CELLS // 2], 1), permute_z(down3[CELLS // 2 :], -1)
    state, far = attention_step([up3, down3], queries, (state, far))
    last = [up4, down4]
    pay_t, pay_b = opposite(last, q_far, far)
    half_low, half_high = permute_x(pay_t, 1), permute_x(pay_b, -1)
    (sides,) = attention_step(last, near, (state,), 0, 2 * CELLS)
    phases = call(
        up_phases_kernel,
        [((2, 2, 2, 2 * C, 256), BF16)],
        up_weight.transpose(0, 1, 3, 2),
        name="up_phases",
        flops=1e7,
        nbytes=4e6,
    )
    to_low, to_high = call(
        relay_kernel,
        [((C + STAT, CELLS), BF16)] * 2,
        half_low,
        half_high,
        *sides,
        phases,
        name="relay",
        specs=[VM] * 5 + [ANY],
    )
    from_low, from_high = permute_x(to_high, 1), permute_x(to_low, -1)
    (mine,) = attention_step(last, near, (state,), 2 * CELLS, 3 * CELLS)
    attended, to_next, to_previous = call(
        finish_kernel,
        [((CELLS, C), BF16)] + [((1, W, C), BF16)] * 2,
        from_low,
        from_high,
        *mine,
        shift,
        qkv_weight,
        proj_weight,
        small,
        block,
        name="finish",
        flops=4 * CELLS * C * C,
    )
    attended = attended.reshape(ROWS, W, C)
    edge_low, edge_high = to_bands(to_next, 1), to_bands(to_previous, -1)
    inner, edge = call(
        up_inner_kernel,
        [((2 * ROWS, OUT, 2 * W), BF16), ((2, OUT, 2 * W), F32)],
        attended,
        phases,
        small,
        name="up_inner",
        flops=2 * CELLS * 14 * C * OUT,
        scratch=[
            pltpu.VMEM((ROWS, W, 3 * C), BF16),
            pltpu.VMEM((2, 2 * ROWS, 2 * W, 128), F32),
        ],
    )
    result = call(
        up_edges_kernel,
        [((2 * ROWS, OUT, 2 * W), BF16)],
        edge_low,
        edge_high,
        phases,
        edge,
        inner,
        name="up_edges",
        flops=2 * CELLS * 2 * C * OUT,
        scratch=[
            pltpu.VMEM((2, W, 3 * C), BF16),
            pltpu.VMEM((2, 2, 2 * W, 128), F32),
            pltpu.VMEM((2, OUT, 2 * W), BF16),
            pltpu.SemaphoreType.DMA((2,)),
        ],
        specs=[VM, VM, VM, VM, ANY],
        out_spec=ANY,
        aliases={4: 0},
    )
    return result.transpose(0, 2, 1)[None]


def solution(mesh):
    return jax.shard_map(
        on_device,
        mesh=mesh,
        in_specs=(P("tm", "rows", None, None), P(), P(), P(), P(), P(), P(), P(), P(), P(), P()),
        out_specs=P("tm", "rows", None, None),
        check_vma=False,
    )
```

```python
import functools
import math

import jax
import jax.numpy as jnp
from jax import lax
from jax.experimental import pallas as pl
from jax.experimental.pallas import tpu as pltpu
from jax.sharding import PartitionSpec as P

F32 = jnp.float32
BF16 = jnp.bfloat16
ROWS = 3
W = 128
C = 384
OUT = 192
CELLS = ROWS * W
XN, ZN, TN = 4, 8, 8
QALL = XN * CELLS
HALF = C // 2
STAT = 16
LOG2E = math.log2(math.e)


def dot(a, b, dims):
    return lax.dot_general(a, b, (dims, ((), ())), preferred_element_type=F32)


def params(mib=32):
    return pltpu.CompilerParams(vmem_limit_bytes=mib * 2**20)


def cost(flops, bytes_accessed):
    return pl.CostEstimate(flops=int(flops), bytes_accessed=int(bytes_accessed), transcendentals=0)


VM = pl.BlockSpec(memory_space=pltpu.VMEM)
ANY = pl.BlockSpec(memory_space=pl.ANY)
HBM = pl.BlockSpec(memory_space=pltpu.HBM)


def call(body, outs, *args, name, flops=1e6, nbytes=1e6, aliases=None, scratch=(), mib=32, specs=None, out_spec=VM):
    shapes = [jax.ShapeDtypeStruct(shape, dtype) for shape, dtype in outs]
    result = pl.pallas_call(
        body,
        in_specs=specs or [VM] * len(args),
        out_specs=[out_spec] * len(shapes),
        out_shape=shapes,
        input_output_aliases=aliases or {},
        scratch_shapes=list(scratch),
        compiler_params=params(mib),
        cost_estimate=cost(flops, nbytes),
        name=name,
    )(*args)
    return result[0] if len(shapes) == 1 else result


def col_variants(y, store):
    column = lax.broadcasted_iota(jnp.int32, y.shape, 0)
    before = jnp.where(column == 0, 0.0, pltpu.roll(y, 1, 0))
    after = jnp.where(column == W - 1, 0.0, pltpu.roll(y, W - 1, 0))
    store(0, before.astype(BF16))
    store(1, y.astype(BF16))
    store(2, after.astype(BF16))


def activate(row, gain):
    x = row.astype(F32)
    y = x * lax.rsqrt(jnp.mean(x * x, -1, keepdims=True) + 1e-6) * gain
    y = y / (1.0 + jnp.exp(-y))
    return y.astype(BF16).astype(F32)


def inside():
    frame, band = lax.axis_index("tm"), lax.axis_index("rows")
    return frame >= 2, frame >= 1, band >= 1, band < XN * ZN - 1


def fill_rows(scratch, rows, gain, present=None):
    for index, row in enumerate(rows):
        y = activate(row, gain)
        if present is not None:
            y = jnp.where(present[index], y, 0.0)

        def store(variant, value, index=index):
            scratch[index, :, variant * C : (variant + 1) * C] = value

        col_variants(y, store)


def band_rows(scratch, t, frame, gain, present=None):
    zero = jnp.zeros((W, 3 * C), BF16)
    scratch[t, 0] = zero
    scratch[t, 1 + ROWS] = zero
    present = None if present is None else [present] * ROWS
    fill_rows(scratch.at[t, 1 : 1 + ROWS], [frame[i] for i in range(ROWS)], gain, present)


def band_tap(scratch, t, b, weight):
    left = scratch[t, pl.ds(b, ROWS)].reshape(CELLS, 3 * C)
    return dot(left, weight.reshape(3 * C, C), ((1,), (0,)))


def conv_own_kernel(own, small, weight, acc, beside, earlier, scratch, held, sem, rest_sem):
    def copy(b):
        return pltpu.make_async_copy(weight.at[2, b], held.at[b], sem.at[b])

    for b in range(3):
        copy(b).start()
    rest = [
        pltpu.make_async_copy(weight.at[2, 0], beside.at[0], rest_sem.at[0]),
        pltpu.make_async_copy(weight.at[2, 2], beside.at[1], rest_sem.at[1]),
        pltpu.make_async_copy(weight.at[:2], earlier, rest_sem.at[2]),
    ]
    for one in rest:
        one.start()
    band_rows(scratch, 0, own, small[0:1, :C])
    acc[...] = jnp.zeros((CELLS, C), F32)

    def step(b, carry):
        copy(b).wait()
        acc[...] += band_tap(scratch, 0, b, held[b])
        return carry

    lax.fori_loop(0, 3, step, 0)
    for one in rest:
        one.wait()


def conv_own(own, small, weight):
    return call(
        conv_own_kernel,
        [((CELLS, C), F32), ((2, 3, C, C), BF16), ((2, 3, 3, C, C), BF16)],
        own,
        small,
        weight,
        name="conv_own",
        flops=2 * CELLS * 9 * C * C,
        scratch=[
            pltpu.VMEM((1, ROWS + 2, W, 3 * C), BF16),
            pltpu.VMEM((3, 3, C, C), BF16),
            pltpu.SemaphoreType.DMA((3,)),
            pltpu.SemaphoreType.DMA((3,)),
        ],
        specs=[VM, VM, HBM],
        mib=46,
    )


def conv_earlier_kernel(two, one, small, weight, start, acc, scratch):
    has_two, has_one, _, _ = inside()
    band_rows(scratch, 0, two, small[0:1, :C], has_two)
    band_rows(scratch, 1, one, small[0:1, :C], has_one)
    acc[...] = start[...]

    def step(g, carry):
        t, b = g // 3, g % 3
        acc[...] += band_tap(scratch, t, b, weight[t, b])
        return carry

    lax.fori_loop(0, 6, step, 0)


def conv_earlier(two, one, small, weight, start):
    return call(
        conv_earlier_kernel,
        [((CELLS, C), F32)],
        two,
        one,
        small,
        weight,
        start,
        name="conv_earlier",
        flops=2 * CELLS * 18 * C * C,
        scratch=[pltpu.VMEM((2, ROWS + 2, W, 3 * C), BF16)],
        aliases={4: 0},
    )


def edge_taps(scratch, low, high, first, last):
    left = dot(scratch[low], first[...].reshape(3 * C, C), ((1,), (0,)))
    right = dot(scratch[high], last[...].reshape(3 * C, C), ((1,), (0,)))
    return left, right


def conv_edges_kernel(low, high, small, w_own, w_pair, start, acc, scratch):
    two, _, above, below = inside()
    present = [above, above & two, below, below & two]
    fill_rows(scratch, [low[0], low[1], high[0], high[1]], small[0:1, :C], present)
    own = edge_taps(scratch, 0, 2, w_own.at[0], w_own.at[1])
    two = edge_taps(scratch, 1, 3, w_pair.at[0, 0], w_pair.at[0, 2])
    acc[...] = start[...]
    acc[:W] += own[0] + two[0]
    acc[2 * W :] += own[1] + two[1]


def conv_last_kernel(edges, own, small, weight, start, block, normed, scratch):
    _, one, above, below = inside()
    fill_rows(scratch, [edges[0], edges[1]], small[0:1, :C], [above & one, below & one])
    sides = edge_taps(scratch, 0, 1, weight.at[1, 0], weight.at[1, 2])
    bias, gain2 = small[1:2, :C], small[2:3, :C]
    for i in range(ROWS):
        rows = slice(i * W, (i + 1) * W)
        total = start[rows] + bias
        if i != 1:
            total += sides[i // 2]
        x = (own[i].astype(F32) + total.astype(BF16).astype(F32)).astype(BF16)
        block[rows] = x
        x = x.astype(F32)
        x = x * lax.rsqrt(jnp.mean(x * x, -1, keepdims=True) + 1e-6) * gain2
        normed[rows] = x.astype(BF16)


def edge_payload_kernel(own, two, _acc, to_next, to_previous, pair):
    to_next[0] = own[ROWS - 1]
    to_next[1] = two[ROWS - 1]
    to_previous[0] = own[0]
    to_previous[1] = two[0]

    odd = lax.rem(lax.axis_index("tm"), 2)

    @pl.when(odd == 0)
    def _():
        pair[...] = own[...]

    @pl.when(odd == 1)
    def _():
        pair[...] = two[...]


def pair_edges_kernel(low, high, _acc, out):
    index = lax.rem(lax.axis_index("tm"), 2)
    out[0] = low[index]
    out[1] = high[index]


def query_kernel(normed, weight, small, out, shift):
    scale = C**-0.5 * LOG2E
    wq, wk = weight[:, :C], weight[:, C : 2 * C]
    q = (dot(normed[...], wq, ((1,), (0,))) + small[4:5, :C]).astype(BF16)
    out[...] = (dot(wk, q, ((1,), (1,))) * scale).astype(BF16)
    bk = jnp.broadcast_to(small[4:5, C : 2 * C], (8, C))
    shift[...] = dot(bk, q.astype(F32), ((1,), (1,)))[:1] * scale


def spans(refs, low, high):
    at = 0
    for ref in refs:
        n = ref.shape[1]
        first, last = max(low, at), min(high, at + n)
        if first < last:
            yield ref, first - at, last - at, first - low, last - low
        at += n


def read(refs, low, high):
    pieces = [ref[:, a:b] for ref, a, b, _, _ in spans(refs, low, high)]
    return pieces[0] if len(pieces) == 1 else jnp.concatenate(pieces, 1)


def write(refs, low, high, value):
    for ref, a, b, first, last in spans(refs, low, high):
        ref[:, a:b] = value[:, first:last]


def joined(refs):
    return refs[0][...] if len(refs) == 1 else jnp.concatenate([r[...] for r in refs], 0)


def softmax_tiles(keys, tiles, q_of, old_of, give):
    keys_t = keys.T

    def scores(tile):
        return dot(keys, q_of(*tile), ((1,), (0,)))

    following = scores(tiles[0])
    for i, tile in enumerate(tiles):
        s = following
        if i + 1 < len(tiles):
            following = scores(tiles[i + 1])
        old = old_of(*tile)
        m = jnp.max(s, 0, keepdims=True)
        if old is not None:
            m = jnp.maximum(m, old[0])
        p = jnp.exp2(s - m)
        total = jnp.sum(p, 0, keepdims=True)
        acc = dot(keys_t, p.astype(BF16), ((1,), (0,)))
        if old is not None:
            alpha = jnp.exp2(old[0] - m)
            total = total + alpha * old[1]
            acc = acc + alpha * old[2]
        give(*tile, (m, total, acc))


def tiles_of(low, high, size=512):
    return [(at, min(at + size, high)) for at in range(low, high, size)]


def attention_kernel(n_keys, n_q, n_state, n_out, low, high, *refs):
    keys = joined(refs[:n_keys])
    queries = refs[n_keys : n_keys + n_q]
    state = refs[n_keys + n_q : n_keys + n_q + 3 * n_state]
    outs = refs[n_keys + n_q + 3 * n_state :]

    def old_of(a, b):
        return [read(state[i::3], a, b) for i in range(3)] if n_state else None

    def give(a, b, values):
        for i, value in enumerate(values):
            write(outs[i::3], a - low, b - low, value)

    softmax_tiles(keys, tiles_of(low, high), lambda a, b: read(queries, a, b), old_of, give)


def attention_step(keys, queries, state=(), low=0, high=None):
    widths = [q.shape[1] for q in queries]
    high = sum(widths) if high is None else high
    rows = sum(k.shape[0] for k in keys)
    whole_state = bool(state) and high - low == sum(s[0].shape[1] for s in state)
    outs = [s[0].shape[1] for s in state] if whole_state else [high - low]
    flat = [v for s in state for v in s]
    before = len(keys) + len(queries)
    result = call(
        functools.partial(
            attention_kernel, len(keys), len(queries), len(state), len(outs), low, high
        ),
        [shape for n in outs for shape in (((1, n), F32), ((1, n), F32), ((C, n), F32))],
        *keys,
        *queries,
        *flat,
        name="attention_step",
        flops=4 * rows * (high - low) * C,
        nbytes=6e6,
        aliases={before + i: i for i in range(len(flat))} if whole_state else None,
    )
    return [tuple(result[i : i + 3]) for i in range(0, len(result), 3)]


def gate_kernel(*refs):
    pass


def after(values, *done):
    count = len(values)
    return call(
        gate_kernel,
        [(v.shape, v.dtype) for v in values],
        *values,
        *done,
        name="gate",
        flops=1,
        nbytes=1,
        specs=[ANY] * (count + len(done)),
        out_spec=ANY,
        aliases={i: i for i in range(count)},
    )


def split3(x):
    hi = x.astype(BF16)
    rest = x - hi.astype(F32)
    mid = rest.astype(BF16)
    low = (rest - mid.astype(F32)).astype(BF16)
    return hi, mid, low


def stat_rows(parts):
    n = parts[0].shape[1]
    row = lax.broadcasted_iota(jnp.int32, (STAT, n), 0)
    block = jnp.zeros((STAT, n), F32)
    for i, part in enumerate(parts):
        for j, piece in enumerate(split3(part)):
            block = jnp.where(row == 3 * i + j, piece.astype(F32), block)
    return block.astype(BF16)


def stat_of(block, i):
    b = block.astype(F32)
    return b[3 * i : 3 * i + 1] + b[3 * i + 1 : 3 * i + 2] + b[3 * i + 2 : 3 * i + 3]


def opposite_kernel(n_keys, *refs):
    q, m_old, l_old, acc_old, top, bottom = refs[n_keys:]

    def give(_a, _b, values):
        m, total, acc = values
        out = (acc / total).astype(BF16)
        stats = stat_rows([m + jnp.log2(total)])
        top[:HALF] = out[:HALF]
        top[HALF:] = stats
        bottom[:HALF] = out[HALF:]
        bottom[HALF:] = stats

    old = lambda a, b: (m_old[...], l_old[...], acc_old[...])
    softmax_tiles(joined(refs[:n_keys]), [(0, CELLS)], lambda a, b: q[...], old, give)


def opposite(keys, q_far, state):
    rows = sum(k.shape[0] for k in keys)
    return call(
        functools.partial(opposite_kernel, len(keys)),
        [((HALF + STAT, CELLS), BF16)] * 2,
        *keys,
        q_far,
        *state,
        name="opposite",
        flops=4 * rows * CELLS * C,
        nbytes=2e6,
    )


def merge(parts):
    top = functools.reduce(jnp.maximum, [s for s, _ in parts])
    w = [jnp.exp2(s - top) for s, _ in parts]
    total = functools.reduce(jnp.add, w)
    inverse = 1.0 / total
    out = functools.reduce(jnp.add, [(a * inverse) * o for a, (_, o) in zip(w, parts)])
    return top + jnp.log2(total), out


def relay_kernel(from_low, from_high, m, total, acc, to_low, to_high):
    for side, got, out in ((0, from_high, to_low), (1, from_low, to_high)):
        cols = slice(side * CELLS, (side + 1) * CELLS)
        stat = m[:, cols] + jnp.log2(total[:, cols])
        mine = acc[:, cols] / total[:, cols]
        theirs = (stat_of(got[HALF:], 0), got[:HALF].astype(F32))
        if side == 0:
            stat_t, half_t = stat, mine[:HALF]
            stat_b, half_b = merge([(stat, mine[HALF:]), theirs])
        else:
            stat_t, half_t = merge([(stat, mine[:HALF]), theirs])
            stat_b, half_b = stat, mine[HALF:]
        out[:HALF] = half_t.astype(BF16)
        out[HALF:C] = half_b.astype(BF16)
        out[C:] = stat_rows([stat_t, stat_b])


def finish_kernel(from_low, from_high, m, total, acc, shift, weight, wp, small, block, _phases, out):
    c = shift[...]
    stat = m[...] + jnp.log2(total[...]) + c
    mine = acc[...] / total[...]
    halves = []
    for i in range(2):
        rows = slice(i * HALF, (i + 1) * HALF)
        parts = [(stat, mine[rows])] + [
            (stat_of(got[C:], i) + c, got[rows].astype(F32)) for got in (from_low, from_high)
        ]
        halves.append(merge(parts)[1])
    mixed_in = jnp.concatenate(halves, 0).astype(BF16)
    mixed = (dot(mixed_in, weight[:, 2 * C :], ((0,), (0,))) + small[4:5, 2 * C :]).astype(BF16)
    attended = dot(mixed, wp[...], ((1,), (0,))) + small[3:4, :C] + block[...].astype(F32)
    out[...] = attended.astype(BF16)


def pack_kernel(flat, small):
    small[...] = jnp.zeros_like(small)
    at = 0
    for i, n in enumerate((C, C, C, C, 3 * C, OUT)):
        small[i, :n] = flat[at : at + n]
        at += n


def up_phases_kernel(weight, out):
    w = [[weight[b, c].astype(F32) for c in range(3)] for b in range(3)]

    def pairs(a, b, c):
        return ((a, b + c), (a + b, c))

    by_row = [pairs(*(w[b][c] for b in range(3))) for c in range(3)]
    for di in range(2):
        for rt in range(2):
            by_column = pairs(*(by_row[c][di][rt] for c in range(3)))
            for dj in range(2):
                for ct in range(2):
                    value = jnp.concatenate(
                        [by_column[dj][ct], jnp.zeros((256 - OUT, C), F32)], 0
                    )
                    out[di, dj, rt, ct * C : (ct + 1) * C] = value.T.astype(BF16)


def fill_plain(scratch, index, row):
    def store(variant, value):
        scratch[index, :, variant * C : (variant + 1) * C] = value

    col_variants(row.astype(F32), store)


def store_phase(wide, row, dj, value):
    for part in range(2):
        wide[part, row, pl.ds(dj, W, stride=2), :] = value[:, part * 128 : (part + 1) * 128]


def read_row(wide, row):
    return jnp.concatenate([wide[0, row].T, wide[1, row].T[: OUT - 128]], 0)


def up_inner_kernel(body, weight, small, out, edge, scratch, wide):
    for i in range(ROWS):
        fill_plain(scratch, i, body[i])
    b = small[5:6, :256]
    for di in range(2):
        for dj in range(2):
            full = scratch[:, :, dj * C : (dj + 2) * C].reshape(CELLS, 2 * C)
            if di == 0:
                here = dot(full, weight[0, dj, 1], ((1,), (0,))) + b
                beside = dot(full[: 2 * W], weight[0, dj, 0], ((1,), (0,)))
                parts = [here[:W], here[W : 2 * W] + beside[:W], here[2 * W :] + beside[W:]]
            else:
                here = dot(full, weight[1, dj, 0], ((1,), (0,))) + b
                beside = dot(full[W:], weight[1, dj, 1], ((1,), (0,)))
                parts = [here[:W] + beside[:W], here[W : 2 * W] + beside[W:], here[2 * W :]]
            for i, part in enumerate(parts):
                store_phase(wide, 2 * i + di, dj, part)
    for row in range(1, 2 * ROWS - 1):
        out[row] = read_row(wide, row).astype(BF16)
    edge[0] = read_row(wide, 0)
    edge[1] = read_row(wide, 2 * ROWS - 1)


def up_edges_kernel(low, high, weight, edge, _start, out, scratch, wide, rows, sem):
    _, _, above, below = inside()
    for i, (ref, present) in enumerate(((low, above), (high, below))):
        row = ref[0]
        fill_plain(scratch, i, jnp.where(present, row, jnp.zeros_like(row)))
    copies = []
    for side in range(2):
        for dj in range(2):
            left = scratch[side, :, dj * C : (dj + 2) * C]
            store_phase(wide, side, dj, dot(left, weight[side, dj, side], ((1,), (0,))))
        rows[side] = (edge[side] + read_row(wide, side)).astype(BF16)
        row = out.at[side * (2 * ROWS - 1)]
        copies.append(pltpu.make_async_copy(rows.at[side], row, sem.at[side]))
        copies[side].start()
    for copy in copies:
        copy.wait()


def permute_z(value, by):
    pairs = [(x * ZN + z, x * ZN + (z + by) % ZN) for x in range(XN) for z in range(ZN)]
    return lax.ppermute(value, "rows", pairs)


def permute_x(value, by):
    pairs = [(x * ZN + z, (x + by) % XN * ZN + z) for x in range(XN) for z in range(ZN)]
    return lax.ppermute(value, "rows", pairs)


def to_bands(value, by):
    n = XN * ZN
    return lax.ppermute(value, "rows", [(i, (i + by) % n) for i in range(n)])


def on_device(
    latent,
    norm1_gain,
    conv1_weight,
    conv1_bias,
    attention_gain,
    qkv_weight,
    qkv_bias,
    proj_weight,
    proj_bias,
    up_weight,
    up_bias,
):
    own = latent[0]
    two = lax.ppermute(own, "tm", [(t, (t + 2) % TN) for t in range(TN)])
    flat = (norm1_gain, conv1_bias, attention_gain, proj_bias, qkv_bias, up_bias)
    ends = [sum(v.shape[0] for v in flat[: i + 1]) for i in range(len(flat))]
    joined_flat = functools.reduce(
        jnp.add,
        [jnp.pad(v, (end - v.shape[0], ends[-1] - end)) for v, end in zip(flat, ends)],
    )
    small = call(pack_kernel, [((8, 3 * C), F32)], joined_flat, name="pack")
    acc, w_own, w_pair = conv_own(own, small, conv1_weight)
    pairs = [(t, t ^ 1) for t in range(TN)]
    to_next, to_previous, pair = call(
        edge_payload_kernel,
        [((2, W, C), BF16)] * 2 + [((ROWS, W, C), BF16)],
        own,
        two,
        acc,
        name="edge_payload",
        specs=[VM, VM, ANY],
    )
    low, high = to_bands(to_next, 1), to_bands(to_previous, -1)
    one = lax.ppermute(pair, "tm", pairs)
    acc = conv_earlier(two, one, small, w_pair, acc)
    pair_edges = call(
        pair_edges_kernel,
        [((2, W, C), BF16)],
        low,
        high,
        acc,
        name="pair_edges",
        specs=[VM, VM, ANY],
    )
    one_edges = lax.ppermute(pair_edges, "tm", pairs)
    acc = call(
        conv_edges_kernel,
        [((CELLS, C), F32)],
        low,
        high,
        small,
        w_own,
        w_pair,
        acc,
        name="conv_edges",
        flops=2 * CELLS * 2 * C * C,
        scratch=[pltpu.VMEM((4, W, 3 * C), BF16)],
        aliases={5: 0},
    )
    block, normed = call(
        conv_last_kernel,
        [((CELLS, C), BF16)] * 2,
        one_edges,
        own,
        small,
        w_pair,
        acc,
        name="conv_last",
        flops=2 * CELLS * C * C,
        scratch=[pltpu.VMEM((2, W, 3 * C), BF16)],
    )

    up, down = permute_z(normed, 1), permute_z(normed, -1)
    query, shift = call(
        query_kernel,
        [((C, CELLS), BF16), ((1, CELLS), F32)],
        normed,
        qkv_weight,
        small,
        name="queries",
        flops=4 * CELLS * C * C,
    )
    q_low, q_high = permute_x(query, 1), permute_x(query, -1)
    q_far = permute_x(query, 2)
    up2, down2 = permute_z(up, 1), permute_z(down, -1)
    early = [normed, up, down]
    near = [q_low, q_high, query]
    (state,) = attention_step(early, near)
    up2, down2 = after((up2, down2), state[0])
    up3, down3 = permute_z(up2, 1), permute_z(down2, -1)
    (far,) = attention_step(early, [q_far])
    queries = near + [q_far]
    state, far = attention_step([up2, down2], queries, (state, far))
    up4, down4 = permute_z(up3[: CELLS // 2], 1), permute_z(down3[CELLS // 2 :], -1)
    state, far = attention_step([up3, down3], queries, (state, far))
    last = [up4, down4]
    pay_t, pay_b = opposite(last, q_far, far)
    half_low, half_high = permute_x(pay_t, 1), permute_x(pay_b, -1)
    (sides,) = attention_step(last, near, (state,), 0, 2 * CELLS)
    phases = call(
        up_phases_kernel,
        [((2, 2, 2, 2 * C, 256), BF16)],
        up_weight.transpose(0, 1, 3, 2),
        name="up_phases",
        flops=1e7,
        nbytes=4e6,
    )
    to_low, to_high = call(
        relay_kernel,
        [((C + STAT, CELLS), BF16)] * 2,
        half_low,
        half_high,
        *sides,
        name="relay",
    )
    from_low, from_high = permute_x(to_high, 1), permute_x(to_low, -1)
    (mine,) = attention_step(last, near, (state,), 2 * CELLS, 3 * CELLS)
    attended = call(
        finish_kernel,
        [((CELLS, C), BF16)],
        from_low,
        from_high,
        *mine,
        shift,
        qkv_weight,
        proj_weight,
        small,
        block,
        phases,
        name="finish",
        specs=[VM] * 10 + [ANY],
        flops=4 * CELLS * C * C,
    ).reshape(ROWS, W, C)
    edge_low, edge_high = to_bands(attended[2:], 1), to_bands(attended[:1], -1)
    inner, edge = call(
        up_inner_kernel,
        [((2 * ROWS, OUT, 2 * W), BF16), ((2, OUT, 2 * W), F32)],
        attended,
        phases,
        small,
        name="up_inner",
        flops=2 * CELLS * 14 * C * OUT,
        scratch=[
            pltpu.VMEM((ROWS, W, 3 * C), BF16),
            pltpu.VMEM((2, 2 * ROWS, 2 * W, 128), F32),
        ],
    )
    result = call(
        up_edges_kernel,
        [((2 * ROWS, OUT, 2 * W), BF16)],
        edge_low,
        edge_high,
        phases,
        edge,
        inner,
        name="up_edges",
        flops=2 * CELLS * 2 * C * OUT,
        scratch=[
            pltpu.VMEM((2, W, 3 * C), BF16),
            pltpu.VMEM((2, 2, 2 * W, 128), F32),
            pltpu.VMEM((2, OUT, 2 * W), BF16),
            pltpu.SemaphoreType.DMA((2,)),
        ],
        specs=[VM, VM, VM, VM, ANY],
        out_spec=ANY,
        aliases={4: 0},
    )
    return result.transpose(0, 2, 1)[None]


def solution(mesh):
    return jax.shard_map(
        on_device,
        mesh=mesh,
        in_specs=(P("tm", "rows", None, None), P(), P(), P(), P(), P(), P(), P(), P(), P(), P()),
        out_specs=P("tm", "rows", None, None),
        check_vma=False,
    )
```

```python
import functools
import math

import jax
import jax.numpy as jnp
from jax import lax
from jax.experimental import pallas as pl
from jax.experimental.pallas import tpu as pltpu
from jax.sharding import PartitionSpec as P

F32 = jnp.float32
BF16 = jnp.bfloat16
ROWS = 3
W = 128
C = 384
OUT = 192
CELLS = ROWS * W
XN, ZN, TN = 4, 8, 8
QALL = XN * CELLS
HALF = C // 2
STAT = 16
LOG2E = math.log2(math.e)


def dot(a, b, dims):
    return lax.dot_general(a, b, (dims, ((), ())), preferred_element_type=F32)


def params(mib=32):
    return pltpu.CompilerParams(vmem_limit_bytes=mib * 2**20)


def cost(flops, bytes_accessed):
    return pl.CostEstimate(flops=int(flops), bytes_accessed=int(bytes_accessed), transcendentals=0)


VM = pl.BlockSpec(memory_space=pltpu.VMEM)
ANY = pl.BlockSpec(memory_space=pl.ANY)
HBM = pl.BlockSpec(memory_space=pltpu.HBM)


def call(body, outs, *args, name, flops=1e6, nbytes=1e6, aliases=None, scratch=(), mib=32, specs=None, out_spec=VM):
    shapes = [jax.ShapeDtypeStruct(shape, dtype) for shape, dtype in outs]
    result = pl.pallas_call(
        body,
        in_specs=specs or [VM] * len(args),
        out_specs=[out_spec] * len(shapes),
        out_shape=shapes,
        input_output_aliases=aliases or {},
        scratch_shapes=list(scratch),
        compiler_params=params(mib),
        cost_estimate=cost(flops, nbytes),
        name=name,
    )(*args)
    return result[0] if len(shapes) == 1 else result


def col_variants(y, store):
    column = lax.broadcasted_iota(jnp.int32, y.shape, 0)
    before = jnp.where(column == 0, 0.0, pltpu.roll(y, 1, 0))
    after = jnp.where(column == W - 1, 0.0, pltpu.roll(y, W - 1, 0))
    store(0, before.astype(BF16))
    store(1, y.astype(BF16))
    store(2, after.astype(BF16))


def activate(row, gain):
    x = row.astype(F32)
    y = x * lax.rsqrt(jnp.mean(x * x, -1, keepdims=True) + 1e-6) * gain
    y = y / (1.0 + jnp.exp(-y))
    return y.astype(BF16).astype(F32)


def inside():
    frame, band = lax.axis_index("tm"), lax.axis_index("rows")
    return frame >= 2, frame >= 1, band >= 1, band < XN * ZN - 1


def fill_rows(scratch, rows, gain, present=None):
    for index, row in enumerate(rows):
        y = activate(row, gain)
        if present is not None:
            y = jnp.where(present[index], y, 0.0)

        def store(variant, value, index=index):
            scratch[index, :, variant * C : (variant + 1) * C] = value

        col_variants(y, store)


def band_rows(scratch, t, frame, gain, present=None):
    zero = jnp.zeros((W, 3 * C), BF16)
    scratch[t, 0] = zero
    scratch[t, 1 + ROWS] = zero
    present = None if present is None else [present] * ROWS
    fill_rows(scratch.at[t, 1 : 1 + ROWS], [frame[i] for i in range(ROWS)], gain, present)


def band_tap(scratch, t, b, weight):
    left = scratch[t, pl.ds(b, ROWS)].reshape(CELLS, 3 * C)
    return dot(left, weight.reshape(3 * C, C), ((1,), (0,)))


def conv_own_kernel(own, small, weight, acc, beside, earlier, scratch, held, sem, rest_sem):
    def copy(b):
        return pltpu.make_async_copy(weight.at[2, b], held.at[b], sem.at[b])

    for b in range(3):
        copy(b).start()
    rest = [
        pltpu.make_async_copy(weight.at[2, 0], beside.at[0], rest_sem.at[0]),
        pltpu.make_async_copy(weight.at[2, 2], beside.at[1], rest_sem.at[1]),
        pltpu.make_async_copy(weight.at[:2], earlier, rest_sem.at[2]),
    ]
    for one in rest:
        one.start()
    band_rows(scratch, 0, own, small[0:1, :C])
    acc[...] = jnp.zeros((CELLS, C), F32)

    def step(b, carry):
        copy(b).wait()
        acc[...] += band_tap(scratch, 0, b, held[b])
        return carry

    lax.fori_loop(0, 3, step, 0)
    for one in rest:
        one.wait()


def conv_own(own, small, weight):
    return call(
        conv_own_kernel,
        [((CELLS, C), F32), ((2, 3, C, C), BF16), ((2, 3, 3, C, C), BF16)],
        own,
        small,
        weight,
        name="conv_own",
        flops=2 * CELLS * 9 * C * C,
        scratch=[
            pltpu.VMEM((1, ROWS + 2, W, 3 * C), BF16),
            pltpu.VMEM((3, 3, C, C), BF16),
            pltpu.SemaphoreType.DMA((3,)),
            pltpu.SemaphoreType.DMA((3,)),
        ],
        specs=[VM, VM, HBM],
        mib=46,
    )


def conv_earlier_kernel(time_tap, frame, small, weight, start, acc, scratch):
    band_rows(scratch, 0, frame, small[0:1, :C], inside()[time_tap])
    acc[...] = start[...]

    def step(b, carry):
        acc[...] += band_tap(scratch, 0, b, weight[time_tap, b])
        return carry

    lax.fori_loop(0, 3, step, 0)


def conv_earlier(frame, small, weight, time_tap, start):
    return call(
        functools.partial(conv_earlier_kernel, time_tap),
        [((CELLS, C), F32)],
        frame,
        small,
        weight,
        start,
        name="conv_earlier",
        flops=2 * CELLS * 9 * C * C,
        scratch=[pltpu.VMEM((1, ROWS + 2, W, 3 * C), BF16)],
        aliases={3: 0},
    )


def edge_taps(scratch, low, high, first, last):
    left = dot(scratch[low], first[...].reshape(3 * C, C), ((1,), (0,)))
    right = dot(scratch[high], last[...].reshape(3 * C, C), ((1,), (0,)))
    return left, right


def conv_edges_kernel(low, high, small, w_own, w_pair, start, acc, scratch):
    two, _, above, below = inside()
    present = [above, above & two, below, below & two]
    fill_rows(scratch, [low[0], low[1], high[0], high[1]], small[0:1, :C], present)
    own = edge_taps(scratch, 0, 2, w_own.at[0], w_own.at[1])
    two = edge_taps(scratch, 1, 3, w_pair.at[0, 0], w_pair.at[0, 2])
    acc[...] = start[...]
    acc[:W] += own[0] + two[0]
    acc[2 * W :] += own[1] + two[1]


def conv_last_kernel(edges, own, small, weight, start, block, normed, scratch):
    _, one, above, below = inside()
    fill_rows(scratch, [edges[0], edges[1]], small[0:1, :C], [above & one, below & one])
    sides = edge_taps(scratch, 0, 1, weight.at[1, 0], weight.at[1, 2])
    bias, gain2 = small[1:2, :C], small[2:3, :C]
    for i in range(ROWS):
        rows = slice(i * W, (i + 1) * W)
        total = start[rows] + bias
        if i != 1:
            total += sides[i // 2]
        x = (own[i].astype(F32) + total.astype(BF16).astype(F32)).astype(BF16)
        block[rows] = x
        x = x.astype(F32)
        x = x * lax.rsqrt(jnp.mean(x * x, -1, keepdims=True) + 1e-6) * gain2
        normed[rows] = x.astype(BF16)


def edge_payload_kernel(own, two, _acc, to_next, to_previous, pair):
    to_next[0] = own[ROWS - 1]
    to_next[1] = two[ROWS - 1]
    to_previous[0] = own[0]
    to_previous[1] = two[0]

    odd = lax.rem(lax.axis_index("tm"), 2)

    @pl.when(odd == 0)
    def _():
        pair[...] = own[...]

    @pl.when(odd == 1)
    def _():
        pair[...] = two[...]


def pair_edges_kernel(low, high, _acc, out):
    index = lax.rem(lax.axis_index("tm"), 2)
    out[0] = low[index]
    out[1] = high[index]


def query_kernel(normed, weight, small, out, shift):
    scale = C**-0.5 * LOG2E
    wq, wk = weight[:, :C], weight[:, C : 2 * C]
    q = (dot(normed[...], wq, ((1,), (0,))) + small[4:5, :C]).astype(BF16)
    out[...] = (dot(wk, q, ((1,), (1,))) * scale).astype(BF16)
    bk = jnp.broadcast_to(small[4:5, C : 2 * C], (8, C))
    shift[...] = dot(bk, q.astype(F32), ((1,), (1,)))[:1] * scale


def spans(refs, low, high):
    at = 0
    for ref in refs:
        n = ref.shape[1]
        first, last = max(low, at), min(high, at + n)
        if first < last:
            yield ref, first - at, last - at, first - low, last - low
        at += n


def read(refs, low, high):
    pieces = [ref[:, a:b] for ref, a, b, _, _ in spans(refs, low, high)]
    return pieces[0] if len(pieces) == 1 else jnp.concatenate(pieces, 1)


def write(refs, low, high, value):
    for ref, a, b, first, last in spans(refs, low, high):
        ref[:, a:b] = value[:, first:last]


def joined(refs):
    return refs[0][...] if len(refs) == 1 else jnp.concatenate([r[...] for r in refs], 0)


def softmax_tiles(keys, tiles, q_of, old_of, give):
    keys_t = keys.T

    def scores(tile):
        return dot(keys, q_of(*tile), ((1,), (0,)))

    following = scores(tiles[0])
    for i, tile in enumerate(tiles):
        s = following
        if i + 1 < len(tiles):
            following = scores(tiles[i + 1])
        old = old_of(*tile)
        m = jnp.max(s, 0, keepdims=True)
        if old is not None:
            m = jnp.maximum(m, old[0])
        p = jnp.exp2(s - m)
        total = jnp.sum(p, 0, keepdims=True)
        acc = dot(keys_t, p.astype(BF16), ((1,), (0,)))
        if old is not None:
            alpha = jnp.exp2(old[0] - m)
            total = total + alpha * old[1]
            acc = acc + alpha * old[2]
        give(*tile, (m, total, acc))


def tiles_of(low, high, size=512):
    return [(at, min(at + size, high)) for at in range(low, high, size)]


def attention_kernel(n_keys, n_q, n_state, n_out, low, high, *refs):
    keys = joined(refs[:n_keys])
    queries = refs[n_keys : n_keys + n_q]
    state = refs[n_keys + n_q : n_keys + n_q + 3 * n_state]
    outs = refs[n_keys + n_q + 3 * n_state :]

    def old_of(a, b):
        return [read(state[i::3], a, b) for i in range(3)] if n_state else None

    def give(a, b, values):
        for i, value in enumerate(values):
            write(outs[i::3], a - low, b - low, value)

    softmax_tiles(keys, tiles_of(low, high), lambda a, b: read(queries, a, b), old_of, give)


def attention_step(keys, queries, state=(), low=0, high=None):
    widths = [q.shape[1] for q in queries]
    high = sum(widths) if high is None else high
    rows = sum(k.shape[0] for k in keys)
    whole_state = bool(state) and high - low == sum(s[0].shape[1] for s in state)
    outs = [s[0].shape[1] for s in state] if whole_state else [high - low]
    flat = [v for s in state for v in s]
    before = len(keys) + len(queries)
    result = call(
        functools.partial(
            attention_kernel, len(keys), len(queries), len(state), len(outs), low, high
        ),
        [shape for n in outs for shape in (((1, n), F32), ((1, n), F32), ((C, n), F32))],
        *keys,
        *queries,
        *flat,
        name="attention_step",
        flops=4 * rows * (high - low) * C,
        nbytes=6e6,
        aliases={before + i: i for i in range(len(flat))} if whole_state else None,
    )
    return [tuple(result[i : i + 3]) for i in range(0, len(result), 3)]


def gate_kernel(*refs):
    pass


def after(values, *done):
    count = len(values)
    return call(
        gate_kernel,
        [(v.shape, v.dtype) for v in values],
        *values,
        *done,
        name="gate",
        flops=1,
        nbytes=1,
        specs=[ANY] * (count + len(done)),
        out_spec=ANY,
        aliases={i: i for i in range(count)},
    )


def split3(x):
    hi = x.astype(BF16)
    rest = x - hi.astype(F32)
    mid = rest.astype(BF16)
    low = (rest - mid.astype(F32)).astype(BF16)
    return hi, mid, low


def stat_rows(parts):
    n = parts[0].shape[1]
    row = lax.broadcasted_iota(jnp.int32, (STAT, n), 0)
    block = jnp.zeros((STAT, n), F32)
    for i, part in enumerate(parts):
        for j, piece in enumerate(split3(part)):
            block = jnp.where(row == 3 * i + j, piece.astype(F32), block)
    return block.astype(BF16)


def stat_of(block, i):
    b = block.astype(F32)
    return b[3 * i : 3 * i + 1] + b[3 * i + 1 : 3 * i + 2] + b[3 * i + 2 : 3 * i + 3]


def opposite_kernel(n_keys, *refs):
    q, m_old, l_old, acc_old, top, bottom = refs[n_keys:]

    def give(_a, _b, values):
        m, total, acc = values
        out = (acc / total).astype(BF16)
        stats = stat_rows([m + jnp.log2(total)])
        top[:HALF] = out[:HALF]
        top[HALF:] = stats
        bottom[:HALF] = out[HALF:]
        bottom[HALF:] = stats

    old = lambda a, b: (m_old[...], l_old[...], acc_old[...])
    softmax_tiles(joined(refs[:n_keys]), [(0, CELLS)], lambda a, b: q[...], old, give)


def opposite(keys, q_far, state):
    rows = sum(k.shape[0] for k in keys)
    return call(
        functools.partial(opposite_kernel, len(keys)),
        [((HALF + STAT, CELLS), BF16)] * 2,
        *keys,
        q_far,
        *state,
        name="opposite",
        flops=4 * rows * CELLS * C,
        nbytes=2e6,
    )


def merge(parts):
    top = functools.reduce(jnp.maximum, [s for s, _ in parts])
    w = [jnp.exp2(s - top) for s, _ in parts]
    total = functools.reduce(jnp.add, w)
    inverse = 1.0 / total
    out = functools.reduce(jnp.add, [(a * inverse) * o for a, (_, o) in zip(w, parts)])
    return top + jnp.log2(total), out


def relay_kernel(from_low, from_high, m, total, acc, _phases, to_low, to_high):
    for side, got, out in ((0, from_high, to_low), (1, from_low, to_high)):
        cols = slice(side * CELLS, (side + 1) * CELLS)
        stat = m[:, cols] + jnp.log2(total[:, cols])
        mine = acc[:, cols] / total[:, cols]
        theirs = (stat_of(got[HALF:], 0), got[:HALF].astype(F32))
        if side == 0:
            stat_t, half_t = stat, mine[:HALF]
            stat_b, half_b = merge([(stat, mine[HALF:]), theirs])
        else:
            stat_t, half_t = merge([(stat, mine[:HALF]), theirs])
            stat_b, half_b = stat, mine[HALF:]
        out[:HALF] = half_t.astype(BF16)
        out[HALF:C] = half_b.astype(BF16)
        out[C:] = stat_rows([stat_t, stat_b])


def finish_kernel(from_low, from_high, m, total, acc, shift, weight, wp, small, block, out):
    c = shift[...]
    stat = m[...] + jnp.log2(total[...]) + c
    mine = acc[...] / total[...]
    halves = []
    for i in range(2):
        rows = slice(i * HALF, (i + 1) * HALF)
        parts = [(stat, mine[rows])] + [
            (stat_of(got[C:], i) + c, got[rows].astype(F32)) for got in (from_low, from_high)
        ]
        halves.append(merge(parts)[1])
    mixed_in = jnp.concatenate(halves, 0).astype(BF16)
    mixed = (dot(mixed_in, weight[:, 2 * C :], ((0,), (0,))) + small[4:5, 2 * C :]).astype(BF16)
    attended = dot(mixed, wp[...], ((1,), (0,))) + small[3:4, :C] + block[...].astype(F32)
    out[...] = attended.astype(BF16)


def pack_kernel(flat, small):
    small[...] = jnp.zeros_like(small)
    at = 0
    for i, n in enumerate((C, C, C, C, 3 * C, OUT)):
        small[i, :n] = flat[at : at + n]
        at += n


def up_phases_kernel(weight, out):
    w = [[weight[b, c].astype(F32) for c in range(3)] for b in range(3)]

    def pairs(a, b, c):
        return ((a, b + c), (a + b, c))

    by_row = [pairs(*(w[b][c] for b in range(3))) for c in range(3)]
    for di in range(2):
        for rt in range(2):
            by_column = pairs(*(by_row[c][di][rt] for c in range(3)))
            for dj in range(2):
                for ct in range(2):
                    value = jnp.concatenate(
                        [by_column[dj][ct], jnp.zeros((256 - OUT, C), F32)], 0
                    )
                    out[di, dj, rt, ct * C : (ct + 1) * C] = value.T.astype(BF16)


def fill_plain(scratch, index, row):
    def store(variant, value):
        scratch[index, :, variant * C : (variant + 1) * C] = value

    col_variants(row.astype(F32), store)


def store_phase(wide, row, dj, value):
    for part in range(2):
        wide[part, row, pl.ds(dj, W, stride=2), :] = value[:, part * 128 : (part + 1) * 128]


def read_row(wide, row):
    return jnp.concatenate([wide[0, row].T, wide[1, row].T[: OUT - 128]], 0)


def up_inner_kernel(body, weight, small, out, edge, scratch, wide):
    for i in range(ROWS):
        fill_plain(scratch, i, body[i])
    b = small[5:6, :256]
    for di in range(2):
        for dj in range(2):
            full = scratch[:, :, dj * C : (dj + 2) * C].reshape(CELLS, 2 * C)
            if di == 0:
                here = dot(full, weight[0, dj, 1], ((1,), (0,))) + b
                beside = dot(full[: 2 * W], weight[0, dj, 0], ((1,), (0,)))
                parts = [here[:W], here[W : 2 * W] + beside[:W], here[2 * W :] + beside[W:]]
            else:
                here = dot(full, weight[1, dj, 0], ((1,), (0,))) + b
                beside = dot(full[W:], weight[1, dj, 1], ((1,), (0,)))
                parts = [here[:W] + beside[:W], here[W : 2 * W] + beside[W:], here[2 * W :]]
            for i, part in enumerate(parts):
                store_phase(wide, 2 * i + di, dj, part)
    for row in range(1, 2 * ROWS - 1):
        out[row] = read_row(wide, row).astype(BF16)
    edge[0] = read_row(wide, 0)
    edge[1] = read_row(wide, 2 * ROWS - 1)


def up_edges_kernel(low, high, weight, edge, _start, out, scratch, wide, rows, sem):
    _, _, above, below = inside()
    for i, (ref, present) in enumerate(((low, above), (high, below))):
        row = ref[0]
        fill_plain(scratch, i, jnp.where(present, row, jnp.zeros_like(row)))
    copies = []
    for side in range(2):
        for dj in range(2):
            left = scratch[side, :, dj * C : (dj + 2) * C]
            store_phase(wide, side, dj, dot(left, weight[side, dj, side], ((1,), (0,))))
        rows[side] = (edge[side] + read_row(wide, side)).astype(BF16)
        row = out.at[side * (2 * ROWS - 1)]
        copies.append(pltpu.make_async_copy(rows.at[side], row, sem.at[side]))
        copies[side].start()
    for copy in copies:
        copy.wait()


def permute_z(value, by):
    pairs = [(x * ZN + z, x * ZN + (z + by) % ZN) for x in range(XN) for z in range(ZN)]
    return lax.ppermute(value, "rows", pairs)


def permute_x(value, by):
    pairs = [(x * ZN + z, (x + by) % XN * ZN + z) for x in range(XN) for z in range(ZN)]
    return lax.ppermute(value, "rows", pairs)


def to_bands(value, by):
    n = XN * ZN
    return lax.ppermute(value, "rows", [(i, (i + by) % n) for i in range(n)])


def on_device(
    latent,
    norm1_gain,
    conv1_weight,
    conv1_bias,
    attention_gain,
    qkv_weight,
    qkv_bias,
    proj_weight,
    proj_bias,
    up_weight,
    up_bias,
):
    own = latent[0]
    two = lax.ppermute(own, "tm", [(t, (t + 2) % TN) for t in range(TN)])
    flat = (norm1_gain, conv1_bias, attention_gain, proj_bias, qkv_bias, up_bias)
    ends = [sum(v.shape[0] for v in flat[: i + 1]) for i in range(len(flat))]
    joined_flat = functools.reduce(
        jnp.add,
        [jnp.pad(v, (end - v.shape[0], ends[-1] - end)) for v, end in zip(flat, ends)],
    )
    small = call(pack_kernel, [((8, 3 * C), F32)], joined_flat, name="pack")
    acc, w_own, w_pair = conv_own(own, small, conv1_weight)
    pairs = [(t, t ^ 1) for t in range(TN)]
    to_next, to_previous, pair = call(
        edge_payload_kernel,
        [((2, W, C), BF16)] * 2 + [((ROWS, W, C), BF16)],
        own,
        two,
        acc,
        name="edge_payload",
        specs=[VM, VM, ANY],
    )
    low, high = to_bands(to_next, 1), to_bands(to_previous, -1)
    one = lax.ppermute(pair, "tm", pairs)
    acc = conv_earlier(two, small, w_pair, 0, acc)
    acc = conv_earlier(one, small, w_pair, 1, acc)
    pair_edges = call(
        pair_edges_kernel,
        [((2, W, C), BF16)],
        low,
        high,
        acc,
        name="pair_edges",
        specs=[VM, VM, ANY],
    )
    one_edges = lax.ppermute(pair_edges, "tm", pairs)
    acc = call(
        conv_edges_kernel,
        [((CELLS, C), F32)],
        low,
        high,
        small,
        w_own,
        w_pair,
        acc,
        name="conv_edges",
        flops=2 * CELLS * 2 * C * C,
        scratch=[pltpu.VMEM((4, W, 3 * C), BF16)],
        aliases={5: 0},
    )
    block, normed = call(
        conv_last_kernel,
        [((CELLS, C), BF16)] * 2,
        one_edges,
        own,
        small,
        w_pair,
        acc,
        name="conv_last",
        flops=2 * CELLS * C * C,
        scratch=[pltpu.VMEM((2, W, 3 * C), BF16)],
    )

    up, down = permute_z(normed, 1), permute_z(normed, -1)
    query, shift = call(
        query_kernel,
        [((C, CELLS), BF16), ((1, CELLS), F32)],
        normed,
        qkv_weight,
        small,
        name="queries",
        flops=4 * CELLS * C * C,
    )
    q_low, q_high = permute_x(query, 1), permute_x(query, -1)
    q_far = permute_x(query, 2)
    up2, down2 = permute_z(up, 1), permute_z(down, -1)
    early = [normed, up, down]
    near = [q_low, q_high, query]
    (state,) = attention_step(early, near)
    up2, down2 = after((up2, down2), state[0])
    up3, down3 = permute_z(up2, 1), permute_z(down2, -1)
    (far,) = attention_step(early, [q_far])
    queries = near + [q_far]
    state, far = attention_step([up2, down2], queries, (state, far))
    up4, down4 = permute_z(up3[: CELLS // 2], 1), permute_z(down3[CELLS // 2 :], -1)
    state, far = attention_step([up3, down3], queries, (state, far))
    last = [up4, down4]
    pay_t, pay_b = opposite(last, q_far, far)
    half_low, half_high = permute_x(pay_t, 1), permute_x(pay_b, -1)
    (sides,) = attention_step(last, near, (state,), 0, 2 * CELLS)
    phases = call(
        up_phases_kernel,
        [((2, 2, 2, 2 * C, 256), BF16)],
        up_weight.transpose(0, 1, 3, 2),
        name="up_phases",
        flops=1e7,
        nbytes=4e6,
    )
    to_low, to_high = call(
        relay_kernel,
        [((C + STAT, CELLS), BF16)] * 2,
        half_low,
        half_high,
        *sides,
        phases,
        name="relay",
        specs=[VM] * 5 + [ANY],
    )
    from_low, from_high = permute_x(to_high, 1), permute_x(to_low, -1)
    (mine,) = attention_step(last, near, (state,), 2 * CELLS, 3 * CELLS)
    attended = call(
        finish_kernel,
        [((CELLS, C), BF16)],
        from_low,
        from_high,
        *mine,
        shift,
        qkv_weight,
        proj_weight,
        small,
        block,
        name="finish",
        flops=4 * CELLS * C * C,
    ).reshape(ROWS, W, C)
    edge_low, edge_high = to_bands(attended[2:], 1), to_bands(attended[:1], -1)
    inner, edge = call(
        up_inner_kernel,
        [((2 * ROWS, OUT, 2 * W), BF16), ((2, OUT, 2 * W), F32)],
        attended,
        phases,
        small,
        name="up_inner",
        flops=2 * CELLS * 14 * C * OUT,
        scratch=[
            pltpu.VMEM((ROWS, W, 3 * C), BF16),
            pltpu.VMEM((2, 2 * ROWS, 2 * W, 128), F32),
        ],
    )
    result = call(
        up_edges_kernel,
        [((2 * ROWS, OUT, 2 * W), BF16)],
        edge_low,
        edge_high,
        phases,
        edge,
        inner,
        name="up_edges",
        flops=2 * CELLS * 2 * C * OUT,
        scratch=[
            pltpu.VMEM((2, W, 3 * C), BF16),
            pltpu.VMEM((2, 2, 2 * W, 128), F32),
            pltpu.VMEM((2, OUT, 2 * W), BF16),
            pltpu.SemaphoreType.DMA((2,)),
        ],
        specs=[VM, VM, VM, VM, ANY],
        out_spec=ANY,
        aliases={4: 0},
    )
    return result.transpose(0, 2, 1)[None]


def solution(mesh):
    return jax.shard_map(
        on_device,
        mesh=mesh,
        in_specs=(P("tm", "rows", None, None), P(), P(), P(), P(), P(), P(), P(), P(), P(), P()),
        out_specs=P("tm", "rows", None, None),
        check_vma=False,
    )
```
